128 devices in a mesh: dp: 2 (over core), context: 16 (over z, y), tensor: 4 (over x).
Axes of the slice: x: 4, y: 4, z: 4, core: 2. Of those that a mesh axis runs over, the one named last changes fastest.
Arguments:
- byte_grads: bfloat16 [2, 65536, 1024], P('dp', 'context'), may hold values from -6 to 6
- patch_starts: int32 [2, 8192], P('dp'), may hold values from 0 to 65535, as said below
- patch_owner: int32 [2, 8192], P('dp'), may hold values from 0 to 15, as said below
- attn_context: bfloat16 [2, 8192, 4096], P('dp', 'context', 'tensor'), may hold values from -0.0625 to 0.0625
- w_global: bfloat16 [4096, 4096], P(None, 'tensor'), may hold values from -0.09375 to 0.09375
- w_value: bfloat16 [4096, 1024], P('tensor'), may hold values from -0.09375 to 0.09375
- w_out: bfloat16 [1024, 1024], replicated, may hold values from -0.1875 to 0.1875
Outputs:
- context_grad: bfloat16 [2, 8192, 4096], P('dp', 'context', 'tensor')
- w_global_grad: float32 [4096, 4096], P(('dp', 'context'), 'tensor')
The draws below stay inside these ranges and needn't reach their ends.
Inputs may be any that keep to these rules, and one draw needn't show every extreme that they name: `patch_starts`: every row rises strictly from 0. The patches that intersect the 4096 bytes of one index of context number at most 1024, and in every sequence the second index has exactly that many, the first of them at the last place of an aligned group of 16 patches. `patch_owner`: in every aligned group of 16 consecutive patches each index of context holds exactly one patch.
All inputs are finite; a program needn't handle non-finite values.
Results may differ from the reference program's by a relative error of at most 0.02.
Values may be sent and summed in bfloat16 or wider, within the bound.
No kernel may reach another device: no remote copies, remote signals or barrier semaphores. Data moves between devices by JAX's collectives and lax.ppermute only.
A program may use at most 128 MiB of HBM per device.

```python
import jax
import jax.numpy as jnp
from jax import lax

D_GLOBAL = 4096
D_LOCAL = 1024
BYTES_DEV = 4096
PATCH_DEV = 512
MAX_TOUCH = 1024
SEQS = 2
SEQ_BYTES = 65536
NPATCH = 8192
N_CONTEXT = 16
N_TENSOR = 4


def one_sequence_starts(seq_key):
    key_weights, key_cross, key_scores = jax.random.split(seq_key, 3)
    groups_n = N_CONTEXT
    weights = jax.random.randint(key_weights, (groups_n,), 1000, 1601).astype(jnp.int32)
    weights = weights.at[1].set(0)
    remaining = NPATCH - (MAX_TOUCH - 1)
    counts = remaining * weights // jnp.sum(weights)
    leading = jnp.maximum(counts[0] // groups_n * groups_n, groups_n)
    counts = counts.at[0].set(leading).at[1].set(MAX_TOUCH - 1)
    counts = counts.at[groups_n - 1].add(NPATCH - jnp.sum(counts))
    crossing = jax.random.randint(key_cross, (groups_n,), 0, 2).astype(jnp.int32)
    crossing = crossing.at[0].set(0).at[1].set(1)
    opens = 1 - crossing
    chosen_count = counts - opens
    byte_index = jnp.arange(BYTES_DEV, dtype=jnp.int32)
    scores = jax.random.randint(key_scores, (groups_n, BYTES_DEV), 0, 2 ** 17).astype(jnp.int32) * BYTES_DEV + byte_index[None, :]
    scores = scores.at[:, 0].set(-1)
    ranks = jnp.argsort(jnp.argsort(-scores, axis=1), axis=1)
    picked = ranks < chosen_count[:, None]
    leading_byte = (byte_index == 0)[None, :] & (opens[:, None] == 1)
    marks = (picked | leading_byte).reshape(-1)
    places = jnp.cumsum(marks.astype(jnp.int32)) - 1
    targets = jnp.where(marks, places, NPATCH)
    all_bytes = jnp.arange(SEQ_BYTES, dtype=jnp.int32)
    return jnp.zeros((NPATCH,), jnp.int32).at[targets].set(all_bytes, mode='drop')


def draw_patch_starts(key, part):
    seq_keys = jax.random.split(jax.random.fold_in(key, 11), SEQS)
    return jax.vmap(one_sequence_starts)(seq_keys)


def draw_patch_owner(key, part):
    scores = jax.random.randint(jax.random.fold_in(key, 23), (SEQS, PATCH_DEV, N_CONTEXT), 0, 2 ** 20).astype(jnp.int32)
    scores = scores * N_CONTEXT + jnp.arange(N_CONTEXT, dtype=jnp.int32)[None, None, :]
    return jnp.argsort(scores, axis=2).astype(jnp.int32).reshape(SEQS, NPATCH)


def raised(result, rng, source, target, blocks, factor):
    def block_of(axis_at):
        return (jnp.arange(result.shape[axis_at]) // (result.shape[axis_at] // blocks)).reshape((-1,) + (1,) * (result.ndim - 1 - axis_at))

    first = jax.random.permutation(rng, blocks)[block_of(target)]
    far = (block_of(target) + blocks // 2) % blocks
    return jnp.where((block_of(source) == first) | (block_of(source) == far), factor * result, result)


def block_levels(rng, dims, cuts, smallest, high):
    def one(position, parts):
        draws = jax.random.uniform(jax.random.fold_in(jax.random.fold_in(rng, 6), position), (parts,), jnp.float32, smallest / len(cuts), high / len(cuts))
        return jnp.repeat(jnp.exp(draws), dims[position] // parts).reshape((-1,) + (1,) * (len(dims) - position - 1))

    gain = one(*cuts[0])
    for cut in cuts[1:]:
        gain = gain * one(*cut)
    return gain


def bell_draw(stream_key, extent, deviation, bound, shards=(), kind=jnp.bfloat16):
    result = jax.random.normal(stream_key, extent, jnp.float32) * deviation
    if len(shards) > 0:
        result = block_levels(stream_key, extent, shards, -0.22, 0.18) * result
    return jnp.clip(result, min=-bound, max=bound).astype(kind)


def heavy_noise(rng, dims, scale, reach, shards, heavy, held_as=jnp.bfloat16):
    result = scale * jax.random.normal(rng, dims, jnp.float32)
    if shards:
        result = result * block_levels(rng, dims, shards, -0.22, 0.18)
    return jnp.clip(raised(result, jax.random.fold_in(rng, 3), *heavy), -reach, reach).astype(held_as)


def setup_inputs(seed: int = 0) -> dict:
    key_list = jax.random.split(jax.random.key(seed), 8)
    return {
        "byte_grads": bell_draw(key_list[0], (SEQS, SEQ_BYTES, D_LOCAL), 1.0, 6.0, ((0, 2), (1, 16))),
        "patch_starts": draw_patch_starts(jax.random.fold_in(key_list[7], 71), 0),
        "patch_owner": draw_patch_owner(jax.random.fold_in(key_list[7], 71), 0),
        "attn_context": heavy_noise(key_list[3], (SEQS, NPATCH, D_GLOBAL), (SEQS * NPATCH) ** -0.5, 0.0625, ((0, 2), (1, 16), (2, 4)), (1, 2, 16, 2.0)),
        "w_global": bell_draw(key_list[4], (D_GLOBAL, D_GLOBAL), D_GLOBAL ** -0.5, 0.09375, ((1, 4),)),
        "w_value": bell_draw(key_list[5], (D_GLOBAL, D_LOCAL), D_GLOBAL ** -0.5, 0.09375, ((0, 4),)),
        "w_out": bell_draw(key_list[6], (D_LOCAL, D_LOCAL), D_LOCAL ** -0.5, 0.1875),
    }


def reference(byte_grads, patch_starts, patch_owner, attn_context, w_global, w_value, w_out):
    highest = lax.Precision.HIGHEST
    out_float = w_out.astype(jnp.float32)
    value_float = w_value.astype(jnp.float32)
    col_width = D_GLOBAL // N_TENSOR
    results = []
    weight_total = jnp.zeros((D_GLOBAL, D_GLOBAL), jnp.float32)
    for seq_index in range(SEQS):
        positions = jnp.arange(SEQ_BYTES, dtype=jnp.int32)
        patch_of = (jnp.searchsorted(patch_starts[seq_index], positions, side="right") - 1).astype(jnp.int32)
        patch_sums = jax.ops.segment_sum(byte_grads[seq_index].astype(jnp.float32), patch_of, num_segments=NPATCH)
        value_grad = jnp.dot(patch_sums, out_float.T, precision=highest)
        patch_grad = jnp.dot(value_grad, value_float.T, precision=highest)
        slot_of = (patch_owner[seq_index] * PATCH_DEV + jnp.arange(NPATCH, dtype=jnp.int32) // N_CONTEXT).astype(jnp.int32)
        rows_grad = jnp.zeros((NPATCH, D_GLOBAL), jnp.bfloat16).at[slot_of].set(patch_grad.astype(jnp.bfloat16))
        summed = jnp.zeros((NPATCH, D_GLOBAL), jnp.float32)
        for block_index in range(N_TENSOR):
            low_col = block_index * col_width
            high_col = low_col + col_width
            block_part = jnp.dot(rows_grad[:, low_col:high_col], w_global[:, low_col:high_col].T, preferred_element_type=jnp.float32).astype(jnp.bfloat16)
            block_part = lax.optimization_barrier(block_part)
            summed = summed + block_part.astype(jnp.float32)
        results.append(summed.astype(jnp.bfloat16))
        weight_total = weight_total + jnp.dot(attn_context[seq_index].T, rows_grad, preferred_element_type=jnp.float32)
    return jnp.stack(results), weight_total
```

```python
import functools

import jax
import jax.numpy as jnp
from jax import lax
from jax.experimental import pallas as pl
from jax.experimental.pallas import tpu as pltpu
from jax.sharding import PartitionSpec as P

LANES = 128
GROUP = 16
SUB = LANES // GROUP
WIN = 9
SLOT = WIN * SUB
VMEM = 48 * 1024 * 1024


def seg_kernel(idx_ref, starts_ref, owner_ref, bytes_ref, out_ref, next_ref, low_ref, high_ref, acc_ref):
    step = pl.program_id(0)
    block = bytes_ref.shape[0]
    shard = block * pl.num_programs(0)
    owners = out_ref.shape[0] // SLOT

    @pl.when(step == 0)
    def _():
        starts = starts_ref[...]
        rows = starts.shape[0]
        base = idx_ref[0] * shard
        count = jnp.sum((starts <= base).astype(jnp.float32)).astype(jnp.int32)
        first = jnp.minimum(lax.shift_right_logical(count - 1, 7), rows - WIN)
        lane = lax.broadcasted_iota(jnp.int32, starts.shape, 1)
        turned = pltpu.roll(starts, LANES - 1, 1)
        below = jnp.concatenate([turned[1:], jnp.full((1, LANES), 2**30, jnp.int32)], axis=0)
        next_ref[...] = jnp.where(lane == LANES - 1, below, turned)
        lane = lax.broadcasted_iota(jnp.int32, (SUB, LANES), 1)
        mine = lax.shift_right_logical(lane, 4) == lax.broadcasted_iota(jnp.int32, (SUB, LANES), 0)
        for t in range(WIN):
            low = jnp.clip(starts_ref[pl.ds(first + t, 1), :] - base, 0, shard).astype(jnp.float32)
            high = jnp.clip(next_ref[pl.ds(first + t, 1), :] - base, 0, shard).astype(jnp.float32)
            low = jnp.broadcast_to(low, (SUB, LANES))
            high = jnp.broadcast_to(high, (SUB, LANES))
            owner = jnp.broadcast_to(owner_ref[pl.ds(first + t, 1), :], (SUB, LANES))
            owner = jnp.where(mine, owner, -1)
            for j in range(owners):
                held = owner == j
                at = j * SLOT + t * SUB
                one = jnp.sum(jnp.where(held, low, 0.0), axis=1, keepdims=True)
                low_ref[at : at + SUB, :] = jnp.broadcast_to(one, (SUB, LANES))
                one = jnp.sum(jnp.where(held, high, 0.0), axis=1, keepdims=True)
                high_ref[at : at + SUB, :] = jnp.broadcast_to(one, (SUB, LANES))
        acc_ref[...] = jnp.zeros_like(acc_ref)

    low = low_ref[...]
    high = high_ref[...]
    parts = []
    for q in range(block // LANES):
        place = lax.broadcasted_iota(jnp.int32, (1, LANES), 1) + (step * block + q * LANES)
        place = place.astype(jnp.float32)
        parts.append(jnp.where((place >= low) & (place < high), 1.0, 0.0).astype(jnp.bfloat16))
    onehot = jnp.concatenate(parts, axis=1)
    acc_ref[...] += jnp.dot(onehot, bytes_ref[...], preferred_element_type=jnp.float32)

    @pl.when(step == pl.num_programs(0) - 1)
    def _():
        out_ref[...] = acc_ref[...].astype(jnp.bfloat16)


def segment_sums(idx, starts, owner, grads, owners, width, interpret=False):
    bytes_n = grads.shape[0]
    block = 512
    rows = owners * SLOT
    whole = pl.BlockSpec(starts.shape, lambda i, idx: (0, 0))
    return pl.pallas_call(
        seg_kernel,
        grid_spec=pltpu.PrefetchScalarGridSpec(
            num_scalar_prefetch=1,
            grid=(bytes_n // block,),
            in_specs=[whole, whole, pl.BlockSpec((block, width), lambda i, idx: (i, idx[1]))],
            out_specs=pl.BlockSpec((rows, width), lambda i, idx: (0, 0)),
            scratch_shapes=[
                pltpu.VMEM(starts.shape, jnp.int32),
                pltpu.VMEM((rows, LANES), jnp.float32),
                pltpu.VMEM((rows, LANES), jnp.float32),
                pltpu.VMEM((rows, width), jnp.float32),
            ],
        ),
        out_shape=jax.ShapeDtypeStruct((rows, width), jnp.bfloat16),
        compiler_params=pltpu.CompilerParams(vmem_limit_bytes=VMEM),
        interpret=interpret,
    )(idx, starts, owner, grads)


def collect_kernel(first_ref, in_ref, out_ref, wide_ref, acc_ref):
    wide_ref[...] = in_ref[...].astype(jnp.float32)
    acc_ref[...] = jnp.zeros_like(acc_ref)
    for s in range(in_ref.shape[0] // SLOT):
        at = pl.ds(pl.multiple_of(first_ref[s] * SUB, SUB), SLOT)
        acc_ref[at, :] += wide_ref[s * SLOT : (s + 1) * SLOT, :]
    total = acc_ref[...].astype(jnp.bfloat16)
    for x in range(out_ref.shape[0]):
        out_ref[x] = total


def collect(first, incoming, patch_rows, copies, interpret=False):
    rows, width = incoming.shape
    return pl.pallas_call(
        collect_kernel,
        in_specs=[pl.BlockSpec(memory_space=pltpu.SMEM), pl.BlockSpec(memory_space=pltpu.VMEM)],
        out_specs=pl.BlockSpec(memory_space=pltpu.VMEM),
        out_shape=jax.ShapeDtypeStruct((copies, patch_rows, width), jnp.bfloat16),
        scratch_shapes=[pltpu.VMEM((rows, width), jnp.float32), pltpu.VMEM((patch_rows, width), jnp.float32)],
        compiler_params=pltpu.CompilerParams(vmem_limit_bytes=VMEM),
        interpret=interpret,
    )(first, incoming)


def outer_kernel(half_ref, own_t_ref, far_t_ref, own_ref, far_ref, out_ref):
    total = jnp.dot(own_t_ref[...], own_ref[0], preferred_element_type=jnp.float32)
    total += jnp.dot(far_t_ref[...], far_ref[0], preferred_element_type=jnp.float32)
    out_ref[...] = total.astype(jnp.bfloat16)


def outer(half, own_t, far_t, own, far):
    cols, rows = own_t.shape
    parts, _, width = far.shape
    whole = pl.BlockSpec((cols, rows), lambda i, half: (0, 0))
    return pl.pallas_call(
        outer_kernel,
        grid_spec=pltpu.PrefetchScalarGridSpec(
            num_scalar_prefetch=1,
            grid=(parts,),
            in_specs=[
                whole,
                whole,
                pl.BlockSpec((1, rows, width), lambda i, half: (half[0] * parts + i, 0, 0)),
                pl.BlockSpec((1, rows, width), lambda i, half: (i, 0, 0)),
            ],
            out_specs=pl.BlockSpec((cols, width), lambda i, half: (0, i)),
        ),
        out_shape=jax.ShapeDtypeStruct((cols, parts * width), jnp.bfloat16),
        compiler_params=pltpu.CompilerParams(vmem_limit_bytes=VMEM),
    )(half, own_t, far_t, own, far)


def local(byte_grads, patch_starts, patch_owner, attn_context, w_global, w_value, w_out):
    dp_n, ctx_n, ten_n = (lax.axis_size(a) for a in ("dp", "context", "tensor"))
    dp = lax.axis_index("dp")
    ctx = lax.axis_index("context")
    ten = lax.axis_index("tensor")
    f32, bf16 = jnp.float32, jnp.bfloat16
    bytes_n, feats = byte_grads.shape[1:]
    width = feats // ten_n
    patch_rows, cols = attn_context.shape[1:]
    starts = patch_starts.reshape(-1, LANES)
    owner = patch_owner.reshape(-1, LANES)

    outgoing = segment_sums(jnp.stack([ctx, ten]), starts, owner, byte_grads[0], ctx_n, width)
    incoming = lax.all_to_all(outgoing, "context", split_axis=0, concat_axis=0, tiled=True)

    swap = [(i, dp_n - 1 - i) for i in range(dp_n)]
    far_context = lax.ppermute(attn_context[0], "dp", swap)
    own_t = attn_context[0].T
    far_t = far_context.T
    edges = jnp.arange(ctx_n, dtype=jnp.int32) * bytes_n
    counts = jnp.sum((patch_starts[0][None, :] <= edges[:, None]).astype(jnp.int32), axis=1)
    first = jnp.minimum((counts - 1) // LANES, starts.shape[0] - WIN)
    both = lax.dot_general(w_out, w_value, (((0,), (1,)), ((), ())), preferred_element_type=f32).astype(bf16)
    share = feats // (dp_n * ctx_n)
    some = lax.dynamic_slice_in_dim(both, (dp * ctx_n + ctx) * share, share, 0)
    term = lax.dot_general(some, w_global, (((1,), (1,)), ((), ())), preferred_element_type=f32).astype(bf16)
    term = lax.psum_scatter(term, "tensor", scatter_dimension=1, tiled=True)
    whole = lax.all_gather(term, ("dp", "context"), axis=0, tiled=True)

    sums = collect(first, incoming, patch_rows, ten_n)
    sums = lax.all_to_all(sums, "tensor", split_axis=0, concat_axis=0)
    half = ten_n // dp_n
    far_sums = lax.ppermute(lax.dynamic_slice_in_dim(sums, (dp_n - 1 - dp) * half, half, 0), "dp", swap)

    partial = outer(dp[None], own_t, far_t, sums, far_sums)
    pieces = lax.all_to_all(partial, "context", split_axis=0, concat_axis=0, tiled=True)
    rows_n = cols // ctx_n
    piece = jnp.sum(pieces.reshape(ctx_n, rows_n, -1).astype(f32), axis=0).astype(bf16)
    moves = []
    per = ctx_n * dp_n // ten_n
    cuts = ctx_n // per
    for d in range(dp_n):
        for c in range(ctx_n):
            for k in range(ten_n):
                to = (per * k + c // cuts) * ten_n + (c % cuts) * dp_n + d
                moves.append(((d * ctx_n + c) * ten_n + k, to))
    piece = lax.ppermute(piece, ("dp", "context", "tensor"), moves)
    block = lax.all_gather(piece, "tensor", axis=0)
    block = block.reshape(cuts, dp_n, rows_n, -1).transpose(0, 2, 1, 3).reshape(cuts * rows_n, feats)
    weight_grad = jnp.dot(block, both, preferred_element_type=f32)

    context_grad = lax.dot_general(
        sums, whole.reshape(ten_n, width, -1), (((0, 2), (0, 1)), ((), ())), preferred_element_type=f32
    ).astype(bf16)
    return (context_grad[None], weight_grad)


def solution(mesh):
    placed = (
        P("dp", "context", None),
        P("dp", None),
        P("dp", None),
        P("dp", "context", "tensor"),
        P(None, "tensor"),
        P("tensor", None),
        P(),
    )
    return jax.shard_map(
        local,
        mesh=mesh,
        in_specs=placed,
        out_specs=(P("dp", "context", "tensor"), P(("dp", "context"), "tensor")),
        check_vma=False,
    )
```

```python
import functools

import jax
import jax.numpy as jnp
from jax import lax
from jax.experimental import pallas as pl
from jax.experimental.pallas import tpu as pltpu
from jax.sharding import PartitionSpec as P

LANES = 128
GROUP = 16
SUB = LANES // GROUP
WIN = 9
SLOT = WIN * SUB
CUTS = (192, 320)
VMEM = 24 * 1024 * 1024


def seg_kernel(idx_ref, starts_ref, owner_ref, bytes_ref, out_ref, next_ref, low_ref, high_ref, acc_ref):
    step = pl.program_id(0)
    block = bytes_ref.shape[0]
    shard = block * pl.num_programs(0)
    owners = out_ref.shape[0] // SLOT

    @pl.when(step == 0)
    def _():
        starts = starts_ref[...]
        rows = starts.shape[0]
        base = idx_ref[0] * shard
        count = jnp.sum((starts <= base).astype(jnp.float32)).astype(jnp.int32)
        first = jnp.minimum(lax.shift_right_logical(count - 1, 7), rows - WIN)
        lane = lax.broadcasted_iota(jnp.int32, starts.shape, 1)
        turned = pltpu.roll(starts, LANES - 1, 1)
        below = jnp.concatenate([turned[1:], jnp.full((1, LANES), 2**30, jnp.int32)], axis=0)
        next_ref[...] = jnp.where(lane == LANES - 1, below, turned)
        lane = lax.broadcasted_iota(jnp.int32, (SUB, LANES), 1)
        mine = lax.shift_right_logical(lane, 4) == lax.broadcasted_iota(jnp.int32, (SUB, LANES), 0)
        for t in range(WIN):
            low = jnp.clip(starts_ref[pl.ds(first + t, 1), :] - base, 0, shard).astype(jnp.float32)
            high = jnp.clip(next_ref[pl.ds(first + t, 1), :] - base, 0, shard).astype(jnp.float32)
            low = jnp.broadcast_to(low, (SUB, LANES))
            high = jnp.broadcast_to(high, (SUB, LANES))
            owner = jnp.broadcast_to(owner_ref[pl.ds(first + t, 1), :], (SUB, LANES))
            owner = jnp.where(mine, owner, -1)
            for j in range(owners):
                held = owner == j
                at = j * SLOT + t * SUB
                one = jnp.sum(jnp.where(held, low, 0.0), axis=1, keepdims=True)
                low_ref[at : at + SUB, :] = jnp.broadcast_to(one, (SUB, LANES))
                one = jnp.sum(jnp.where(held, high, 0.0), axis=1, keepdims=True)
                high_ref[at : at + SUB, :] = jnp.broadcast_to(one, (SUB, LANES))
        acc_ref[...] = jnp.zeros_like(acc_ref)

    low = low_ref[...]
    high = high_ref[...]
    parts = []
    for q in range(block // LANES):
        place = lax.broadcasted_iota(jnp.int32, (1, LANES), 1) + (step * block + q * LANES)
        place = place.astype(jnp.float32)
        parts.append(jnp.where((place >= low) & (place < high), 1.0, 0.0).astype(jnp.bfloat16))
    onehot = jnp.concatenate(parts, axis=1)
    acc_ref[...] += jnp.dot(onehot, bytes_ref[...], preferred_element_type=jnp.float32)

    @pl.when(step == pl.num_programs(0) - 1)
    def _():
        out_ref[...] = acc_ref[...].astype(jnp.bfloat16)


def segment_sums(idx, starts, owner, grads, owners, width, interpret=False):
    bytes_n = grads.shape[0]
    block = 512
    rows = owners * SLOT
    whole = pl.BlockSpec(starts.shape, lambda i, idx: (0, 0))
    return pl.pallas_call(
        seg_kernel,
        grid_spec=pltpu.PrefetchScalarGridSpec(
            num_scalar_prefetch=1,
            grid=(bytes_n // block,),
            in_specs=[whole, whole, pl.BlockSpec((block, width), lambda i, idx: (i, idx[1]))],
            out_specs=pl.BlockSpec((rows, width), lambda i, idx: (0, 0)),
            scratch_shapes=[
                pltpu.VMEM(starts.shape, jnp.int32),
                pltpu.VMEM((rows, LANES), jnp.float32),
                pltpu.VMEM((rows, LANES), jnp.float32),
                pltpu.VMEM((rows, width), jnp.float32),
            ],
        ),
        out_shape=jax.ShapeDtypeStruct((rows, width), jnp.bfloat16),
        compiler_params=pltpu.CompilerParams(vmem_limit_bytes=VMEM),
        interpret=interpret,
    )(idx, starts, owner, grads)


def collect_kernel(first_ref, in_ref, out_ref, wide_ref, acc_ref):
    wide_ref[...] = in_ref[...].astype(jnp.float32)
    acc_ref[...] = jnp.zeros_like(acc_ref)
    for s in range(in_ref.shape[0] // SLOT):
        at = pl.ds(pl.multiple_of(first_ref[s] * SUB, SUB), SLOT)
        acc_ref[at, :] += wide_ref[s * SLOT : (s + 1) * SLOT, :]
    out_ref[...] = acc_ref[...].astype(jnp.bfloat16)


def collect(first, incoming, patch_rows, interpret=False):
    rows, width = incoming.shape
    return pl.pallas_call(
        collect_kernel,
        in_specs=[pl.BlockSpec(memory_space=pltpu.SMEM), pl.BlockSpec(memory_space=pltpu.VMEM)],
        out_specs=pl.BlockSpec(memory_space=pltpu.VMEM),
        out_shape=jax.ShapeDtypeStruct((patch_rows, width), jnp.bfloat16),
        scratch_shapes=[pltpu.VMEM((rows, width), jnp.float32), pltpu.VMEM((patch_rows, width), jnp.float32)],
        compiler_params=pltpu.CompilerParams(vmem_limit_bytes=VMEM),
        interpret=interpret,
    )(first, incoming)


def outer_kernel(idx_ref, mine_ref, third_ref, cross_ref, n0_ref, n1a_ref, n1b_ref, n1c_ref, f0_ref, f1a_ref, f1b_ref, f1c_ref, out_ref, near_t, far_t):
    step = pl.program_id(0)

    @pl.when(step == 0)
    def _():
        near = jnp.where(idx_ref[0] == 0, mine_ref[...], third_ref[...])
        near_t[...] = near.T
        far_t[...] = cross_ref[...].T

    low = lax.rem(idx_ref[1], 2)
    blocks = out_ref.shape[0] // 2
    per = n0_ref.shape[1] // LANES
    near1 = jnp.concatenate([n1a_ref[...], n1b_ref[...], n1c_ref[...]], axis=0)
    far1 = jnp.concatenate([f1a_ref[...], f1b_ref[...], f1c_ref[...]], axis=0)
    for near, far, which in ((n0_ref[...], f0_ref[...], low), (near1, far1, 1 - low)):
        total = jnp.dot(near_t[...], near, preferred_element_type=jnp.float32)
        total += jnp.dot(far_t[...], far, preferred_element_type=jnp.float32)
        total = total.astype(jnp.bfloat16)
        for i in range(per):
            out_ref[which * blocks + step * per + i] = total[:, i * LANES : (i + 1) * LANES]


def outer(idx, sums, columns):
    rows, width = sums[0].shape
    cols = columns[0].shape[1]
    block = 256
    whole = pl.BlockSpec((rows, width), lambda i, idx: (0, 0))
    shape = (2 * cols // LANES, width, LANES)
    return pl.pallas_call(
        outer_kernel,
        grid_spec=pltpu.PrefetchScalarGridSpec(
            num_scalar_prefetch=1,
            grid=(cols // block,),
            in_specs=[whole] * len(sums)
            + [pl.BlockSpec((c.shape[0], block), lambda i, idx: (0, i)) for c in columns],
            out_specs=pl.BlockSpec(shape, lambda i, idx: (0, 0, 0)),
            scratch_shapes=[pltpu.VMEM((width, rows), jnp.bfloat16)] * 2,
        ),
        out_shape=jax.ShapeDtypeStruct(shape, jnp.bfloat16),
        compiler_params=pltpu.CompilerParams(vmem_limit_bytes=VMEM),
    )(idx, *sums, *columns)


def chain_kernel(idx_ref, value_ref, global_ref, a_ref, b_ref, c_ref, d_ref, turned_ref):
    step = pl.program_id(0)
    share = a_ref.shape[0]

    @pl.when(step == 0)
    def _():
        turned_ref[...] = value_ref[...].T

    at = pl.ds(pl.multiple_of(lax.rem(idx_ref[0], LANES // share) * share, share), share)
    total = lax.dot_general(
        turned_ref[at, :], global_ref[...], (((1,), (1,)), ((), ())), preferred_element_type=jnp.float32
    ).astype(jnp.bfloat16)
    for s, ref in enumerate((a_ref, b_ref, c_ref, d_ref)):

        @pl.when(step == s)
        def _(ref=ref):
            ref[...] = total


def chain_terms(idx, w_value, w_global, share, parts):
    deep, feats = w_value.shape
    rows = w_global.shape[0] // parts
    per = LANES // share
    return pl.pallas_call(
        chain_kernel,
        grid_spec=pltpu.PrefetchScalarGridSpec(
            num_scalar_prefetch=1,
            grid=(parts,),
            in_specs=[
                pl.BlockSpec((deep, LANES), lambda i, idx: (0, lax.div(idx[0], per))),
                pl.BlockSpec((rows, deep), lambda i, idx: (lax.rem(idx[1] + i, parts), 0)),
            ],
            out_specs=[pl.BlockSpec((share, rows), lambda i, idx: (0, 0))] * parts,
            scratch_shapes=[pltpu.VMEM((LANES, deep), jnp.bfloat16)],
        ),
        out_shape=[jax.ShapeDtypeStruct((share, rows), jnp.bfloat16)] * parts,
        compiler_params=pltpu.CompilerParams(vmem_limit_bytes=VMEM),
    )(idx, w_value, w_global)


def value_kernel(feat_ref, a_ref, b_ref, c_ref, d_ref, w_ref, out_ref):
    width = a_ref.shape[1]
    total = jnp.zeros(out_ref.shape, jnp.float32)
    for s, ref in enumerate((a_ref, b_ref, c_ref, d_ref)):
        at = pl.ds(pl.multiple_of(feat_ref[s] * width, width), width)
        total += lax.dot_general(
            ref[...], w_ref[:, at], (((1,), (1,)), ((), ())), preferred_element_type=jnp.float32
        )
    out_ref[...] = total.astype(jnp.bfloat16)


def value(feats, pieces, weights):
    vmem = pl.BlockSpec(memory_space=pltpu.VMEM)
    return pl.pallas_call(
        value_kernel,
        in_specs=[pl.BlockSpec(memory_space=pltpu.SMEM)] + [vmem] * 5,
        out_specs=vmem,
        out_shape=jax.ShapeDtypeStruct((pieces[0].shape[0], weights.shape[0]), jnp.bfloat16),
        compiler_params=pltpu.CompilerParams(vmem_limit_bytes=VMEM),
    )(feats, *pieces, weights)


def last_kernel(feat_ref, a_ref, b_ref, c_ref, d_ref, w_ref, out_ref):
    total = jnp.zeros(out_ref.shape, jnp.float32)
    for s, ref in enumerate((a_ref, b_ref, c_ref, d_ref)):
        total += jnp.dot(ref[...].T, w_ref[feat_ref[s]], preferred_element_type=jnp.float32)
    out_ref[...] = total


def last(feats, pieces, weights):
    vmem = pl.BlockSpec(memory_space=pltpu.VMEM)
    return pl.pallas_call(
        last_kernel,
        in_specs=[pl.BlockSpec(memory_space=pltpu.SMEM)] + [vmem] * 5,
        out_specs=vmem,
        out_shape=jax.ShapeDtypeStruct((pieces[0].shape[1], weights.shape[2]), jnp.float32),
        compiler_params=pltpu.CompilerParams(vmem_limit_bytes=VMEM),
    )(feats, *pieces, weights)


def after(value, *others):
    return lax.optimization_barrier((value, *others))[0]


def local(byte_grads, patch_starts, patch_owner, attn_context, w_global, w_value, w_out):
    dp_n, ctx_n, ten_n = (lax.axis_size(a) for a in ("dp", "context", "tensor"))
    dp = lax.axis_index("dp")
    ctx = lax.axis_index("context")
    ten = lax.axis_index("tensor")
    f32, bf16 = jnp.float32, jnp.bfloat16
    bytes_n, feats = byte_grads.shape[1:]
    width = feats // ten_n
    patch_rows = attn_context.shape[1]
    starts = patch_starts.reshape(-1, LANES)
    owner = patch_owner.reshape(-1, LANES)
    line = ("dp", "tensor")

    def moves(target):
        pairs = []
        for d in range(dp_n):
            for x in range(ten_n):
                to = target(d, x)
                if to is not None:
                    pairs.append((d * ten_n + x, to[0] * ten_n + to[1]))
        return pairs

    swap = [(i, dp_n - 1 - i) for i in range(dp_n)]
    pair = [(x, x ^ 1) for x in range(ten_n)]
    near0 = attn_context[0]
    far0 = lax.ppermute(near0, "dp", swap)
    ends = (0,) + CUTS + (patch_rows,)
    near1 = [lax.ppermute(near0[: ends[1]], "tensor", pair)]

    outgoing = segment_sums(jnp.stack([ctx, ten]), starts, owner, byte_grads[0], ctx_n, width)
    outgoing = after(outgoing, near1[0])
    incoming = lax.all_to_all(outgoing, "context", split_axis=0, concat_axis=0, tiled=True)

    near1.append(lax.ppermute(after(near0, outgoing)[ends[1] : ends[2]], "tensor", pair))
    incoming = after(incoming, near1[1])
    near1.append(lax.ppermute(after(near0, incoming)[ends[2] :], "tensor", pair))

    share = feats // (dp_n * ctx_n)
    where = after(jnp.stack([dp * ctx_n + ctx, ten]), outgoing)
    terms = chain_terms(where, w_value, w_global, share, ten_n)
    chain = terms[0].astype(f32)
    for s in range(1, ten_n):
        chain += lax.ppermute(terms[s], "tensor", [(x, (x + s) % ten_n) for x in range(ten_n)]).astype(f32)
    chain = lax.all_gather(after(chain.astype(bf16), incoming), ("dp", "context"), axis=0, tiled=True)

    edges = jnp.arange(ctx_n, dtype=jnp.int32) * bytes_n
    counts = jnp.sum((patch_starts[0][None, :] <= edges[:, None]).astype(jnp.int32), axis=1)
    first = jnp.minimum((counts - 1) // LANES, starts.shape[0] - WIN)

    sums = collect(first, incoming, patch_rows)
    cross = lax.ppermute(sums, line, moves(lambda d, x: (0, x) if d == 1 else (1, ten_n - 1 - x)))
    third = lax.ppermute(sums, line, moves(lambda d, x: (1, ten_n - 1 - x) if d == 1 else None))
    far1 = [lax.ppermute(part, "dp", swap) for part in (near1[0], near1[1], after(near1[2], cross))]
    columns = (near0, *near1, far0, *far1)
    partial = outer(jnp.stack([dp, ten]), (sums, third, cross), columns)
    pieces = lax.all_to_all(partial, "context", split_axis=0, concat_axis=0, tiled=True)

    late = after(sums, partial)
    around = [late] + [
        lax.ppermute(late, "tensor", [(x, (x + s) % ten_n) for x in range(ten_n)]) for s in (1, ten_n - 1, 2)
    ]
    order = jnp.stack([ten, (ten + ten_n - 1) % ten_n, (ten + 1) % ten_n, (ten + 2) % ten_n])
    value_grad = value(order, around, w_out)
    both = lax.dot_general(
        after(w_out, partial), w_value, (((0,), (1,)), ((), ())), preferred_element_type=f32
    ).astype(bf16)

    pieces = after(pieces, both)
    piece = jnp.sum(pieces.astype(f32), axis=0).astype(bf16)
    parts, blocks = [], []
    for s in range(ten_n):
        parts.append(lax.ppermute(piece, line, moves(lambda d, x, s=s: (x // 2, (2 * d + x % 2) ^ s))))
        source = ten ^ s
        near = 2 * dp + source % 2
        blocks.append(jnp.where(source < 2, near, ten_n - 1 - near))
    weight_grad = last(jnp.stack(blocks), parts, both.reshape(ten_n, width, -1))
    context_grad = jnp.dot(value_grad, chain, preferred_element_type=f32).astype(bf16)
    return (context_grad[None], weight_grad)


def solution(mesh):
    placed = (
        P("dp", "context", None),
        P("dp", None),
        P("dp", None),
        P("dp", "context", "tensor"),
        P(None, "tensor"),
        P("tensor", None),
        P(),
    )
    return jax.shard_map(
        local,
        mesh=mesh,
        in_specs=placed,
        out_specs=(P("dp", "context", "tensor"), P(("dp", "context"), "tensor")),
        check_vma=False,
    )
```

```python
import functools

import jax
import jax.numpy as jnp
from jax import lax
from jax.experimental import pallas as pl
from jax.experimental.pallas import tpu as pltpu
from jax.sharding import PartitionSpec as P

LANES = 128
GROUP = 16
SUB = LANES // GROUP
WIN = 9
SLOT = WIN * SUB
SIDE = 4
CUT = 256
VMEM = 24 * 1024 * 1024
WIDE = 56 * 1024 * 1024


def seg_kernel(idx_ref, starts_ref, owner_ref, bytes_ref, out_ref, next_ref, low_ref, high_ref, acc_ref):
    step = pl.program_id(0)
    block = bytes_ref.shape[0]
    shard = block * pl.num_programs(0)
    owners = out_ref.shape[0] // SLOT

    @pl.when(step == 0)
    def _():
        starts = starts_ref[...]
        rows = starts.shape[0]
        base = idx_ref[0] * shard
        count = jnp.sum((starts <= base).astype(jnp.float32)).astype(jnp.int32)
        first = jnp.minimum(lax.shift_right_logical(count - 1, 7), rows - WIN)
        lane = lax.broadcasted_iota(jnp.int32, starts.shape, 1)
        turned = pltpu.roll(starts, LANES - 1, 1)
        below = jnp.concatenate([turned[1:], jnp.full((1, LANES), 2**30, jnp.int32)], axis=0)
        next_ref[...] = jnp.where(lane == LANES - 1, below, turned)
        lane = lax.broadcasted_iota(jnp.int32, (SUB, LANES), 1)
        mine = lax.shift_right_logical(lane, 4) == lax.broadcasted_iota(jnp.int32, (SUB, LANES), 0)
        for t in range(WIN):
            low = jnp.clip(starts_ref[pl.ds(first + t, 1), :] - base, 0, shard).astype(jnp.float32)
            high = jnp.clip(next_ref[pl.ds(first + t, 1), :] - base, 0, shard).astype(jnp.float32)
            low = jnp.broadcast_to(low, (SUB, LANES))
            high = jnp.broadcast_to(high, (SUB, LANES))
            owner = jnp.broadcast_to(owner_ref[pl.ds(first + t, 1), :], (SUB, LANES))
            owner = jnp.where(mine, owner, -1)
            for j in range(owners):
                held = owner == j
                at = j * SLOT + t * SUB
                one = jnp.sum(jnp.where(held, low, 0.0), axis=1, keepdims=True)
                low_ref[at : at + SUB, :] = jnp.broadcast_to(one, (SUB, LANES))
                one = jnp.sum(jnp.where(held, high, 0.0), axis=1, keepdims=True)
                high_ref[at : at + SUB, :] = jnp.broadcast_to(one, (SUB, LANES))
        acc_ref[...] = jnp.zeros_like(acc_ref)

    low = low_ref[...]
    high = high_ref[...]
    parts = []
    for q in range(block // LANES):
        place = lax.broadcasted_iota(jnp.int32, (1, LANES), 1) + (step * block + q * LANES)
        place = place.astype(jnp.float32)
        parts.append(jnp.where((place >= low) & (place < high), 1.0, 0.0).astype(jnp.bfloat16))
    onehot = jnp.concatenate(parts, axis=1)
    acc_ref[...] += jnp.dot(onehot, bytes_ref[...], preferred_element_type=jnp.float32)

    @pl.when(step == pl.num_programs(0) - 1)
    def _():
        out_ref[...] = acc_ref[...].astype(jnp.bfloat16)


def segment_sums(idx, starts, owner, grads, owners, width, interpret=False):
    bytes_n = grads.shape[0]
    block = 512
    rows = owners * SLOT
    whole = pl.BlockSpec(starts.shape, lambda i, idx: (0, 0))
    return pl.pallas_call(
        seg_kernel,
        grid_spec=pltpu.PrefetchScalarGridSpec(
            num_scalar_prefetch=1,
            grid=(bytes_n // block,),
            in_specs=[whole, whole, pl.BlockSpec((block, width), lambda i, idx: (i, idx[1]))],
            out_specs=pl.BlockSpec((rows, width), lambda i, idx: (0, 0)),
            scratch_shapes=[
                pltpu.VMEM(starts.shape, jnp.int32),
                pltpu.VMEM((rows, LANES), jnp.float32),
                pltpu.VMEM((rows, LANES), jnp.float32),
                pltpu.VMEM((rows, width), jnp.float32),
            ],
        ),
        out_shape=jax.ShapeDtypeStruct((rows, width), jnp.bfloat16),
        compiler_params=pltpu.CompilerParams(vmem_limit_bytes=WIDE),
        interpret=interpret,
    )(idx, starts, owner, grads)


def collect_kernel(first_ref, in_ref, out_ref, wide_ref, acc_ref):
    wide_ref[...] = in_ref[...].astype(jnp.float32)
    acc_ref[...] = jnp.zeros_like(acc_ref)
    for s in range(in_ref.shape[0] // SLOT):
        at = pl.ds(pl.multiple_of(first_ref[s] * SUB, SUB), SLOT)
        acc_ref[at, :] += wide_ref[s * SLOT : (s + 1) * SLOT, :]
    out_ref[...] = acc_ref[...].astype(jnp.bfloat16)


def collect(first, incoming, patch_rows, interpret=False):
    rows, width = incoming.shape
    return pl.pallas_call(
        collect_kernel,
        in_specs=[pl.BlockSpec(memory_space=pltpu.SMEM), pl.BlockSpec(memory_space=pltpu.VMEM)],
        out_specs=pl.BlockSpec(memory_space=pltpu.VMEM),
        out_shape=jax.ShapeDtypeStruct((patch_rows, width), jnp.bfloat16),
        scratch_shapes=[pltpu.VMEM((rows, width), jnp.float32), pltpu.VMEM((patch_rows, width), jnp.float32)],
        compiler_params=pltpu.CompilerParams(vmem_limit_bytes=VMEM),
        interpret=interpret,
    )(first, incoming)


def outer_kernel(idx_ref, mine_ref, third_ref, cross_ref, n0_ref, n1a_ref, n1b_ref, f0_ref, f1a_ref, f1b_ref, out_ref, both_ref, near_t, far_t):
    step = pl.program_id(0)

    @pl.when(step == 0)
    def _():
        near = jnp.where(idx_ref[0] == 0, mine_ref[...], third_ref[...])
        near_t[...] = near.T
        far_t[...] = cross_ref[...].T
        both_ref[0] = near
        both_ref[1] = cross_ref[...]

    low = lax.rem(idx_ref[1], 2)
    blocks = out_ref.shape[0] // 2
    per = n0_ref.shape[1] // LANES
    near1 = jnp.concatenate([n1a_ref[...], n1b_ref[...]], axis=0)
    far1 = jnp.concatenate([f1a_ref[...], f1b_ref[...]], axis=0)
    for near, far, which in ((n0_ref[...], f0_ref[...], low), (near1, far1, 1 - low)):
        total = jnp.dot(near_t[...], near, preferred_element_type=jnp.float32)
        total += jnp.dot(far_t[...], far, preferred_element_type=jnp.float32)
        total = total.astype(jnp.bfloat16)
        for i in range(per):
            out_ref[which * blocks + step * per + i] = total[:, i * LANES : (i + 1) * LANES]


def outer(idx, sums, columns):
    rows, width = sums[0].shape
    cols = columns[0].shape[1]
    block = 256
    whole = pl.BlockSpec((rows, width), lambda i, idx: (0, 0))
    shape = (2 * cols // LANES, width, LANES)
    return pl.pallas_call(
        outer_kernel,
        grid_spec=pltpu.PrefetchScalarGridSpec(
            num_scalar_prefetch=1,
            grid=(cols // block,),
            in_specs=[whole] * len(sums)
            + [pl.BlockSpec((c.shape[0], block), lambda i, idx: (0, i)) for c in columns],
            out_specs=[
                pl.BlockSpec(shape, lambda i, idx: (0, 0, 0)),
                pl.BlockSpec((2, rows, width), lambda i, idx: (0, 0, 0)),
            ],
            scratch_shapes=[pltpu.VMEM((width, rows), jnp.bfloat16)] * 2,
        ),
        out_shape=[
            jax.ShapeDtypeStruct(shape, jnp.bfloat16),
            jax.ShapeDtypeStruct((2, rows, width), jnp.bfloat16),
        ],
        compiler_params=pltpu.CompilerParams(vmem_limit_bytes=WIDE),
    )(idx, *sums, *columns)


def chain_kernel(idx_ref, both_ref, global_ref, a_ref, b_ref, c_ref, d_ref, turned_ref):
    step = pl.program_id(0)
    share = a_ref.shape[0]
    turned_ref[...] = both_ref[...].T
    at = pl.ds(pl.multiple_of(lax.rem(idx_ref[1], LANES // share) * share, share), share)
    total = lax.dot_general(
        turned_ref[at, :], global_ref[...], (((1,), (1,)), ((), ())), preferred_element_type=jnp.float32
    ).astype(jnp.bfloat16)
    for s, ref in enumerate((a_ref, b_ref, c_ref, d_ref)):

        @pl.when(step == s)
        def _(ref=ref):
            ref[...] = total


def chain_terms(idx, both_t, w_global, share, parts):
    deep, feats = both_t.shape
    rows = w_global.shape[0] // parts

    def rows_of(i, idx):
        half = lax.div(lax.rem(idx[2] + i, parts), 2)
        block = (idx[0] + half - 2 * idx[0] * half) * 2 * SIDE + idx[1]
        return (0, lax.div(block, LANES // share))

    return pl.pallas_call(
        chain_kernel,
        grid_spec=pltpu.PrefetchScalarGridSpec(
            num_scalar_prefetch=1,
            grid=(parts,),
            in_specs=[
                pl.BlockSpec((deep, LANES), rows_of),
                pl.BlockSpec((rows, deep), lambda i, idx: (lax.rem(idx[2] + i, parts), 0)),
            ],
            out_specs=[pl.BlockSpec((share, rows), lambda i, idx: (0, 0))] * parts,
            scratch_shapes=[pltpu.VMEM((LANES, deep), jnp.bfloat16)],
        ),
        out_shape=[jax.ShapeDtypeStruct((share, rows), jnp.bfloat16)] * parts,
        compiler_params=pltpu.CompilerParams(vmem_limit_bytes=WIDE),
    )(idx, both_t, w_global)


def theirs_kernel(idx_ref, near_ref, far_ref, low_ref, high_ref, out_ref, table_ref):
    share = low_ref.shape[2]
    deep = table_ref.shape[0] // 2
    z, odd = lax.div(idx_ref[1], SIDE), lax.rem(idx_ref[1], 2)
    for ref, base in ((low_ref, z), (high_ref, SIDE - 1 - z)):
        for i in range(2):
            for j in range(2):
                other = base + i - 2 * i * lax.rem(base, 2)
                to = 2 * other + odd + j - 2 * odd * j
                table_ref[pl.ds(pl.multiple_of(to * share, share), share), :] = ref[i, j]
    odd = lax.rem(idx_ref[2] + idx_ref[0], 2)
    first = table_ref[pl.ds(pl.multiple_of(odd * deep, deep), deep), :]
    second = table_ref[pl.ds(pl.multiple_of((1 - odd) * deep, deep), deep), :]
    total = jnp.dot(near_ref[1], first, preferred_element_type=jnp.float32)
    total += jnp.dot(far_ref[1], second, preferred_element_type=jnp.float32)
    out_ref[...] = total.astype(jnp.bfloat16)


def theirs(idx, near, far, low, high):
    vmem = pl.BlockSpec(memory_space=pltpu.VMEM)
    rows, cols = near.shape[1], low.shape[3]
    deep = 8 * low.shape[2]
    return pl.pallas_call(
        theirs_kernel,
        in_specs=[pl.BlockSpec(memory_space=pltpu.SMEM)] + [vmem] * 4,
        out_specs=[vmem, vmem],
        out_shape=[
            jax.ShapeDtypeStruct((rows, cols), jnp.bfloat16),
            jax.ShapeDtypeStruct((deep, cols), jnp.bfloat16),
        ],
        compiler_params=pltpu.CompilerParams(vmem_limit_bytes=VMEM),
    )(idx, near, far, low, high)


def ours_kernel(idx_ref, near_ref, far_ref, table_ref, back_ref, out_ref):
    deep = table_ref.shape[0] // 2
    odd = lax.rem(idx_ref[2] + idx_ref[0], 2)
    first = table_ref[pl.ds(pl.multiple_of(odd * deep, deep), deep), :]
    second = table_ref[pl.ds(pl.multiple_of((1 - odd) * deep, deep), deep), :]
    total = jnp.dot(near_ref[0], first, preferred_element_type=jnp.float32)
    total += jnp.dot(far_ref[0], second, preferred_element_type=jnp.float32)
    out_ref[...] = (total + back_ref[...].astype(jnp.float32)).astype(jnp.bfloat16)


def ours(idx, near, far, table, back):
    vmem = pl.BlockSpec(memory_space=pltpu.VMEM)
    return pl.pallas_call(
        ours_kernel,
        in_specs=[pl.BlockSpec(memory_space=pltpu.SMEM)] + [vmem] * 4,
        out_specs=vmem,
        out_shape=jax.ShapeDtypeStruct(back.shape, jnp.bfloat16),
        compiler_params=pltpu.CompilerParams(vmem_limit_bytes=VMEM),
    )(idx, near, far, table, back)


def last_kernel(feat_ref, a_ref, b_ref, c_ref, d_ref, w_ref, out_ref):
    width = a_ref.shape[0]
    total = jnp.zeros(out_ref.shape, jnp.float32)
    for s, ref in enumerate((a_ref, b_ref, c_ref, d_ref)):
        at = pl.ds(pl.multiple_of(feat_ref[s] * width, width), width)
        total += lax.dot_general(
            ref[...].T, w_ref[:, at], (((1,), (1,)), ((), ())), preferred_element_type=jnp.float32
        )
    out_ref[...] = total


def last(feats, pieces, weights):
    vmem = pl.BlockSpec(memory_space=pltpu.VMEM)
    return pl.pallas_call(
        last_kernel,
        in_specs=[pl.BlockSpec(memory_space=pltpu.SMEM)] + [vmem] * 5,
        out_specs=vmem,
        out_shape=jax.ShapeDtypeStruct((pieces[0].shape[1], weights.shape[0]), jnp.float32),
        compiler_params=pltpu.CompilerParams(vmem_limit_bytes=VMEM),
    )(feats, *pieces, weights)


def after(value, *others):
    return lax.optimization_barrier((value, *others))[0]


def local(byte_grads, patch_starts, patch_owner, attn_context, w_global, w_value, w_out):
    dp_n, ctx_n, ten_n = (lax.axis_size(a) for a in ("dp", "context", "tensor"))
    dp = lax.axis_index("dp")
    ctx = lax.axis_index("context")
    ten = lax.axis_index("tensor")
    f32, bf16 = jnp.float32, jnp.bfloat16
    bytes_n, feats = byte_grads.shape[1:]
    width = feats // ten_n
    patch_rows = attn_context.shape[1]
    starts = patch_starts.reshape(-1, LANES)
    owner = patch_owner.reshape(-1, LANES)
    line = ("dp", "tensor")

    def moves(target):
        pairs = []
        for d in range(dp_n):
            for x in range(ten_n):
                to = target(d, x)
                if to is not None:
                    pairs.append((d * ten_n + x, to[0] * ten_n + to[1]))
        return pairs

    swap = [(i, dp_n - 1 - i) for i in range(dp_n)]
    pair = [(x, x ^ 1) for x in range(ten_n)]
    near0 = attn_context[0]
    far0 = lax.ppermute(near0, "dp", swap)
    near1 = [lax.ppermute(near0[:CUT], "tensor", pair)]

    here = jnp.stack([dp, ctx, ten])
    outgoing = segment_sums(here[1:], starts, owner, byte_grads[0], ctx_n, width)
    both_t = jnp.dot(after(w_value, outgoing), w_out, preferred_element_type=f32).astype(bf16)
    outgoing = after(outgoing, near1[0], both_t)
    incoming = lax.all_to_all(outgoing, "context", split_axis=0, concat_axis=0, tiled=True)

    z, y = ctx // SIDE, ctx % SIDE
    share = feats // (4 * SIDE)
    where = after(jnp.stack([dp, 2 * z + y % 2, ten]), outgoing)
    terms = chain_terms(where, both_t, w_global, share, ten_n)
    chain = terms[0].astype(f32)
    for s in range(1, ten_n):
        chain += lax.ppermute(terms[s], "tensor", [(x, (x + s) % ten_n) for x in range(ten_n)]).astype(f32)
    chain = chain.astype(bf16)
    edges = jnp.arange(ctx_n, dtype=jnp.int32) * bytes_n
    counts = jnp.sum((patch_starts[0][None, :] <= edges[:, None]).astype(jnp.int32), axis=1)
    first = jnp.minimum((counts - 1) // LANES, starts.shape[0] - WIN)
    incoming = after(incoming, first, chain)

    near1.append(lax.ppermute(after(near0, incoming)[CUT:], "tensor", pair))
    sums = collect(first, incoming, patch_rows)
    cross = lax.ppermute(sums, line, moves(lambda d, x: (0, x) if d == 1 else (1, ten_n - 1 - x)))
    third = lax.ppermute(sums, line, moves(lambda d, x: (1, ten_n - 1 - x) if d == 1 else None))
    far1 = [lax.ppermute(part, "dp", swap) for part in (near1[0], after(near1[1], cross, third))]

    def along(target):
        return [
            (i * SIDE + j, target(i, j)[0] * SIDE + target(i, j)[1]) for i in range(SIDE) for j in range(SIDE)
        ]

    chain = after(chain, sums)
    chain = jnp.stack([chain, lax.ppermute(chain, "context", along(lambda i, j: (i, j ^ 1)))])
    chain = jnp.stack([chain, lax.ppermute(chain, "context", along(lambda i, j: (i ^ 1, j)))])
    columns = (near0, *near1, far0, *far1)
    partial, near = outer(after(jnp.stack([dp, ten]), chain), (sums, third, cross), columns)
    pieces = lax.all_to_all(partial, "context", split_axis=0, concat_axis=0, tiled=True)
    rest = lax.ppermute(after(chain, partial), "context", along(lambda i, j: (SIDE - 1 - i, j)))

    far = lax.ppermute(near, "tensor", pair)
    give, table = theirs(here, near, far, chain, rest)
    pieces = after(pieces, give)
    piece = jnp.sum(pieces.astype(f32), axis=0).astype(bf16)
    parts, blocks = [], []
    for s in range(ten_n):
        parts.append(lax.ppermute(piece, line, moves(lambda d, x, s=s: (x // 2, (2 * d + x % 2) ^ s))))
        source = ten ^ s
        pick = 2 * dp + source % 2
        blocks.append(jnp.where(source < 2, pick, ten_n - 1 - pick))
    back = lax.ppermute(give, "dp", swap)
    context_grad = ours(here, near, far, table, back)
    weight_grad = last(jnp.stack(blocks), parts, both_t)
    return (context_grad[None], weight_grad)


def solution(mesh):
    placed = (
        P("dp", "context", None),
        P("dp", None),
        P("dp", None),
        P("dp", "context", "tensor"),
        P(None, "tensor"),
        P("tensor", None),
        P(),
    )
    return jax.shard_map(
        local,
        mesh=mesh,
        in_specs=placed,
        out_specs=(P("dp", "context", "tensor"), P(("dp", "context"), "tensor")),
        check_vma=False,
    )
```

```python
import functools

import jax
import jax.numpy as jnp
from jax import lax
from jax.experimental import pallas as pl
from jax.experimental.pallas import tpu as pltpu
from jax.sharding import PartitionSpec as P

LANES = 128
GROUP = 16
SUB = LANES // GROUP
WIN = 9
SLOT = WIN * SUB
SIDE = 4
CUT = 256
VMEM = 24 * 1024 * 1024
WIDE = 56 * 1024 * 1024


def seg_kernel(idx_ref, starts_ref, owner_ref, bytes_ref, out_ref, next_ref, low_ref, high_ref, acc_ref, turn_ref, row_ref):
    step = pl.program_id(0)
    steps = pl.num_programs(0)
    block = bytes_ref.shape[0]
    shard = block * steps
    owners = LANES // SUB

    @pl.when(step == 0)
    def _():
        starts = starts_ref[...]
        rows = starts.shape[0]
        base = idx_ref[0] * shard
        for k in range(row_ref.shape[0]):
            count = jnp.sum((starts <= base + k * block).astype(jnp.float32)).astype(jnp.int32)
            row_ref[k] = lax.shift_right_logical(count - 1, 7)
        first = jnp.minimum(row_ref[0], rows - WIN)
        for k in range(row_ref.shape[0]):
            row_ref[k] = row_ref[k] - first
        lane = lax.broadcasted_iota(jnp.int32, starts.shape, 1)
        turned = pltpu.roll(starts, LANES - 1, 1)
        below = jnp.concatenate([turned[1:], jnp.full((1, LANES), 2**30, jnp.int32)], axis=0)
        next_ref[...] = jnp.where(lane == LANES - 1, below, turned)
        lane = lax.broadcasted_iota(jnp.int32, (SUB, LANES), 1)
        mine = lax.shift_right_logical(lane, 4) == lax.broadcasted_iota(jnp.int32, (SUB, LANES), 0)
        for t in range(WIN):
            low = jnp.clip(starts_ref[pl.ds(first + t, 1), :] - base, 0, shard).astype(jnp.float32)
            high = jnp.clip(next_ref[pl.ds(first + t, 1), :] - base, 0, shard).astype(jnp.float32)
            low = jnp.broadcast_to(low, (SUB, LANES))
            high = jnp.broadcast_to(high, (SUB, LANES))
            owner = jnp.broadcast_to(owner_ref[pl.ds(first + t, 1), :], (SUB, LANES))
            owner = jnp.where(mine, owner, -1)
            for j in range(owners):
                held = owner == j
                at = t * LANES + j * SUB
                one = jnp.sum(jnp.where(held, low, 0.0), axis=1, keepdims=True)
                low_ref[at : at + SUB, :] = jnp.broadcast_to(one, (SUB, LANES))
                one = jnp.sum(jnp.where(held, high, 0.0), axis=1, keepdims=True)
                high_ref[at : at + SUB, :] = jnp.broadcast_to(one, (SUB, LANES))
        acc_ref[...] = jnp.zeros_like(acc_ref)

    values = bytes_ref[...]

    def one_row(t, carry):
        at = pl.ds(pl.multiple_of(t * LANES, LANES), LANES)
        low = low_ref[at, :]
        high = high_ref[at, :]
        parts = []
        for q in range(block // LANES):
            place = lax.broadcasted_iota(jnp.int32, (1, LANES), 1) + (step * block + q * LANES)
            place = place.astype(jnp.float32)
            parts.append(jnp.where((place >= low) & (place < high), 1.0, 0.0).astype(jnp.bfloat16))
        onehot = jnp.concatenate(parts, axis=1)
        acc_ref[at, :] += jnp.dot(onehot, values, preferred_element_type=jnp.float32)
        return carry

    lax.fori_loop(row_ref[step], jnp.minimum(row_ref[step + 1], WIN - 1) + 1, one_row, 0)

    @pl.when(step == steps - 1)
    def _():
        for t in range(WIN):
            for j in range(owners):
                turn_ref[j * SLOT + t * SUB : j * SLOT + (t + 1) * SUB, :] = acc_ref[
                    t * LANES + j * SUB : t * LANES + (j + 1) * SUB, :
                ]
        out_ref[...] = turn_ref[...].astype(jnp.bfloat16)


def segment_sums(idx, starts, owner, grads, owners, width, interpret=False):
    bytes_n = grads.shape[0]
    block = 512
    rows = owners * SLOT
    whole = pl.BlockSpec(starts.shape, lambda i, idx: (0, 0))
    return pl.pallas_call(
        seg_kernel,
        grid_spec=pltpu.PrefetchScalarGridSpec(
            num_scalar_prefetch=1,
            grid=(bytes_n // block,),
            in_specs=[whole, whole, pl.BlockSpec((block, width), lambda i, idx: (i, idx[1]))],
            out_specs=pl.BlockSpec((rows, width), lambda i, idx: (0, 0)),
            scratch_shapes=[
                pltpu.VMEM(starts.shape, jnp.int32),
                pltpu.VMEM((rows, LANES), jnp.float32),
                pltpu.VMEM((rows, LANES), jnp.float32),
                pltpu.VMEM((rows, width), jnp.float32),
                pltpu.VMEM((rows, width), jnp.float32),
                pltpu.SMEM((bytes_n // block + 1,), jnp.int32),
            ],
        ),
        out_shape=jax.ShapeDtypeStruct((rows, width), jnp.bfloat16),
        compiler_params=pltpu.CompilerParams(vmem_limit_bytes=WIDE),
        interpret=interpret,
    )(idx, starts, owner, grads)


def collect_kernel(first_ref, in_ref, out_ref, wide_ref, acc_ref):
    wide_ref[...] = in_ref[...].astype(jnp.float32)
    acc_ref[...] = jnp.zeros_like(acc_ref)
    for s in range(in_ref.shape[0] // SLOT):
        at = pl.ds(pl.multiple_of(first_ref[s] * SUB, SUB), SLOT)
        acc_ref[at, :] += wide_ref[s * SLOT : (s + 1) * SLOT, :]
    out_ref[...] = acc_ref[...].T.astype(jnp.bfloat16)


def collect(first, incoming, patch_rows, interpret=False):
    rows, width = incoming.shape
    return pl.pallas_call(
        collect_kernel,
        in_specs=[pl.BlockSpec(memory_space=pltpu.SMEM), pl.BlockSpec(memory_space=pltpu.VMEM)],
        out_specs=pl.BlockSpec(memory_space=pltpu.VMEM),
        out_shape=jax.ShapeDtypeStruct((width, patch_rows), jnp.bfloat16),
        scratch_shapes=[pltpu.VMEM((rows, width), jnp.float32), pltpu.VMEM((patch_rows, width), jnp.float32)],
        compiler_params=pltpu.CompilerParams(vmem_limit_bytes=VMEM),
        interpret=interpret,
    )(first, incoming)


def outer_kernel(idx_ref, mine_ref, third_ref, cross_ref, n0_ref, n1a_ref, n1b_ref, f0_ref, f1a_ref, f1b_ref, out_ref, both_ref):
    step = pl.program_id(0)

    @pl.when(step == 0)
    def _():
        both_ref[0] = jnp.where(idx_ref[0] == 0, mine_ref[...], third_ref[...])
        both_ref[1] = cross_ref[...]

    low = lax.rem(idx_ref[1], 2)
    blocks = out_ref.shape[0] // 2
    per = n0_ref.shape[1] // LANES
    near1 = jnp.concatenate([n1a_ref[...], n1b_ref[...]], axis=0)
    far1 = jnp.concatenate([f1a_ref[...], f1b_ref[...]], axis=0)
    for near, far, which in ((n0_ref[...], f0_ref[...], low), (near1, far1, 1 - low)):
        total = jnp.dot(both_ref[0], near, preferred_element_type=jnp.float32)
        total += jnp.dot(both_ref[1], far, preferred_element_type=jnp.float32)
        total = total.astype(jnp.bfloat16)
        for i in range(per):
            out_ref[which * blocks + step * per + i] = total[:, i * LANES : (i + 1) * LANES]


def outer(idx, sums, columns):
    width, rows = sums[0].shape
    cols = columns[0].shape[1]
    block = 256
    whole = pl.BlockSpec((width, rows), lambda i, idx: (0, 0))
    shape = (2 * cols // LANES, width, LANES)
    return pl.pallas_call(
        outer_kernel,
        grid_spec=pltpu.PrefetchScalarGridSpec(
            num_scalar_prefetch=1,
            grid=(cols // block,),
            in_specs=[whole] * len(sums)
            + [pl.BlockSpec((c.shape[0], block), lambda i, idx: (0, i)) for c in columns],
            out_specs=[
                pl.BlockSpec(shape, lambda i, idx: (0, 0, 0)),
                pl.BlockSpec((2, width, rows), lambda i, idx: (0, 0, 0)),
            ],
        ),
        out_shape=[
            jax.ShapeDtypeStruct(shape, jnp.bfloat16),
            jax.ShapeDtypeStruct((2, width, rows), jnp.bfloat16),
        ],
        compiler_params=pltpu.CompilerParams(vmem_limit_bytes=VMEM),
    )(idx, *sums, *columns)


def chain_kernel(idx_ref, value_ref, out_w_ref, g0_ref, g1_ref, g2_ref, g3_ref, both_ref, p0_ref, p1_ref, p2_ref, p3_ref):
    step = pl.program_id(0)
    rows = value_ref.shape[0]
    at = pl.ds(pl.multiple_of(step * rows, rows), rows)
    both_ref[at, :] = jnp.dot(
        value_ref[...], out_w_ref[...], preferred_element_type=jnp.float32
    ).astype(jnp.bfloat16)

    @pl.when(step == pl.num_programs(0) - 1)
    def _():
        wide = p0_ref.shape[1]
        for s, (g, p) in enumerate(((g0_ref, p0_ref), (g1_ref, p1_ref), (g2_ref, p2_ref), (g3_ref, p3_ref))):
            half = lax.div(lax.rem(idx_ref[2] + s, 4), 2)
            half = idx_ref[0] + half - 2 * idx_ref[0] * half
            cols = pl.ds(pl.multiple_of(half * wide, wide), wide)
            p[...] = jnp.dot(g[...], both_ref[:, cols], preferred_element_type=jnp.float32).astype(jnp.bfloat16)


def chain_terms(idx, w_value, w_out, w_global, parts):
    deep, feats = w_value.shape
    rows = w_global.shape[0] // parts // 4
    block = deep // 4

    def rows_of(s):
        return lambda i, idx: (lax.rem(idx[2] + s, parts) * 4 + idx[1], 0)

    return pl.pallas_call(
        chain_kernel,
        grid_spec=pltpu.PrefetchScalarGridSpec(
            num_scalar_prefetch=1,
            grid=(deep // block,),
            in_specs=[
                pl.BlockSpec((block, w_value.shape[1]), lambda i, idx: (i, 0)),
                pl.BlockSpec(w_out.shape, lambda i, idx: (0, 0)),
            ]
            + [pl.BlockSpec((rows, deep), rows_of(s)) for s in range(parts)],
            out_specs=[pl.BlockSpec((deep, feats), lambda i, idx: (0, 0))]
            + [pl.BlockSpec((rows, feats // 2), lambda i, idx: (0, 0))] * parts,
        ),
        out_shape=[jax.ShapeDtypeStruct((deep, feats), jnp.bfloat16)]
        + [jax.ShapeDtypeStruct((rows, feats // 2), jnp.bfloat16)] * parts,
        compiler_params=pltpu.CompilerParams(vmem_limit_bytes=WIDE),
    )(idx, w_value, w_out, w_global, w_global, w_global, w_global)


def rows_kernel(which, idx_ref, near_ref, far_ref, low_ref, high_ref, *rest):
    out_ref = rest[-1]
    deep = near_ref.shape[1]
    odd = lax.rem(idx_ref[2] + idx_ref[0], 2)
    near = near_ref[which].T
    far = far_ref[which].T
    rows = low_ref.shape[1]
    for i, ref in enumerate((low_ref, high_ref)):
        for j in range(2):
            z, y = lax.div(idx_ref[1], 2), lax.rem(idx_ref[1], 2)
            at = 2 * (z + i - 2 * i * z) + y + j - 2 * j * y
            at = pl.ds(pl.multiple_of(at * rows, rows), rows)
            first = ref[j, :, pl.ds(pl.multiple_of(odd * deep, deep), deep)]
            second = ref[j, :, pl.ds(pl.multiple_of((1 - odd) * deep, deep), deep)]
            dims = (((1,), (1,)), ((), ()))
            total = lax.dot_general(near, first, dims, preferred_element_type=jnp.float32)
            total += lax.dot_general(far, second, dims, preferred_element_type=jnp.float32)
            if len(rest) > 1:
                total += rest[0][:, at].astype(jnp.float32)
            out_ref[:, at] = total.astype(jnp.bfloat16)


def context_rows(which, idx, near, far, low, high, *back):
    vmem = pl.BlockSpec(memory_space=pltpu.VMEM)
    return pl.pallas_call(
        functools.partial(rows_kernel, which),
        in_specs=[pl.BlockSpec(memory_space=pltpu.SMEM)] + [vmem] * (4 + len(back)),
        out_specs=vmem,
        out_shape=jax.ShapeDtypeStruct((near.shape[2], 4 * low.shape[1]), jnp.bfloat16),
        compiler_params=pltpu.CompilerParams(vmem_limit_bytes=VMEM),
    )(idx, near, far, low, high, *back)


def last_kernel(feat_ref, a_ref, b_ref, c_ref, d_ref, w_ref, out_ref):
    width = a_ref.shape[0]
    total = jnp.zeros(out_ref.shape, jnp.float32)
    for s, ref in enumerate((a_ref, b_ref, c_ref, d_ref)):
        at = pl.ds(pl.multiple_of(feat_ref[s] * width, width), width)
        total += lax.dot_general(
            ref[...].T, w_ref[:, at], (((1,), (1,)), ((), ())), preferred_element_type=jnp.float32
        )
    out_ref[...] = total


def last(feats, pieces, weights):
    cols, deep = weights.shape
    block = 256
    whole = pl.BlockSpec(pieces[0].shape, lambda i, feats: (0, 0))
    return pl.pallas_call(
        last_kernel,
        grid_spec=pltpu.PrefetchScalarGridSpec(
            num_scalar_prefetch=1,
            grid=(cols // block,),
            in_specs=[whole] * len(pieces) + [pl.BlockSpec((block, deep), lambda i, feats: (i, 0))],
            out_specs=pl.BlockSpec((pieces[0].shape[1], block), lambda i, feats: (0, i)),
        ),
        out_shape=jax.ShapeDtypeStruct((pieces[0].shape[1], cols), jnp.float32),
        compiler_params=pltpu.CompilerParams(vmem_limit_bytes=VMEM),
    )(feats, *pieces, weights)


def after(value, *others):
    return lax.optimization_barrier((value, *others))[0]


def local(byte_grads, patch_starts, patch_owner, attn_context, w_global, w_value, w_out):
    dp_n, ctx_n, ten_n = (lax.axis_size(a) for a in ("dp", "context", "tensor"))
    dp = lax.axis_index("dp")
    ctx = lax.axis_index("context")
    ten = lax.axis_index("tensor")
    f32, bf16 = jnp.float32, jnp.bfloat16
    bytes_n, feats = byte_grads.shape[1:]
    width = feats // ten_n
    patch_rows = attn_context.shape[1]
    starts = patch_starts.reshape(-1, LANES)
    owner = patch_owner.reshape(-1, LANES)
    line = ("dp", "tensor")

    def moves(target):
        pairs = []
        for d in range(dp_n):
            for x in range(ten_n):
                to = target(d, x)
                if to is not None:
                    pairs.append((d * ten_n + x, to[0] * ten_n + to[1]))
        return pairs

    swap = [(i, dp_n - 1 - i) for i in range(dp_n)]
    pair = [(x, x ^ 1) for x in range(ten_n)]
    near0 = attn_context[0]
    far0 = lax.ppermute(near0, "dp", swap)
    near1 = [lax.ppermute(near0[:CUT], "tensor", pair)]

    outgoing = segment_sums(jnp.stack([ctx, ten]), starts, owner, byte_grads[0], ctx_n, width)

    here = jnp.stack([dp, 2 * (ctx // SIDE % 2) + ctx % 2, ten])
    both_t, *terms = chain_terms(after(here, outgoing), w_value, w_out, w_global, ten_n)
    outgoing = after(outgoing, near1[0], both_t)
    incoming = lax.all_to_all(outgoing, "context", split_axis=0, concat_axis=0, tiled=True)

    chain = terms[0].astype(f32)
    for s in range(1, ten_n):
        term = after(terms[s], outgoing)
        chain += lax.ppermute(term, "tensor", [(x, (x + s) % ten_n) for x in range(ten_n)]).astype(f32)
    chain = chain.astype(bf16)
    edges = jnp.arange(ctx_n, dtype=jnp.int32) * bytes_n
    counts = jnp.sum((patch_starts[0][None, :] <= edges[:, None]).astype(jnp.int32), axis=1)
    first = jnp.minimum((counts - 1) // LANES, starts.shape[0] - WIN)
    incoming = after(incoming, first, chain)

    near1.append(lax.ppermute(after(near0, incoming)[CUT:], "tensor", pair))
    sums = collect(first, incoming, patch_rows)
    cross = lax.ppermute(sums, line, moves(lambda d, x: (0, x) if d == 1 else (1, ten_n - 1 - x)))
    third = lax.ppermute(sums, line, moves(lambda d, x: (1, ten_n - 1 - x) if d == 1 else None))

    def along(target):
        return [
            (i * SIDE + j, target(i, j)[0] * SIDE + target(i, j)[1]) for i in range(SIDE) for j in range(SIDE)
        ]

    chain = after(chain, sums)
    chain = jnp.stack([chain, lax.ppermute(chain, "context", along(lambda i, j: (i, j ^ 1)))])
    far1 = [lax.ppermute(part, "dp", swap) for part in (near1[0], after(near1[1], cross, third, chain))]
    columns = (near0, *near1, far0, *far1)
    partial, near = outer(jnp.stack([dp, ten]), (sums, third, cross), columns)
    pieces = lax.all_to_all(partial, "context", split_axis=0, concat_axis=0, tiled=True)
    rest = lax.ppermute(after(chain, partial), "context", along(lambda i, j: (i ^ 1, j)))

    far = lax.ppermute(near, "tensor", pair)
    give = context_rows(1, here, near, far, chain, rest)
    pieces = after(pieces, give)
    piece = jnp.sum(pieces.astype(f32), axis=0).astype(bf16)
    parts, blocks = [], []
    for s in range(ten_n):
        parts.append(lax.ppermute(piece, line, moves(lambda d, x, s=s: (x // 2, (2 * d + x % 2) ^ s))))
        source = ten ^ s
        pick = 2 * dp + source % 2
        blocks.append(jnp.where(source < 2, pick, ten_n - 1 - pick))
    back = lax.ppermute(give, "dp", swap)
    context_grad = context_rows(0, here, near, far, chain, rest, back)
    weight_grad = last(jnp.stack(blocks), parts, both_t)
    return (context_grad[None], weight_grad)


def solution(mesh):
    placed = (
        P("dp", "context", None),
        P("dp", None),
        P("dp", None),
        P("dp", "context", "tensor"),
        P(None, "tensor"),
        P("tensor", None),
        P(),
    )
    return jax.shard_map(
        local,
        mesh=mesh,
        in_specs=placed,
        out_specs=(P("dp", "context", "tensor"), P(("dp", "context"), "tensor")),
        check_vma=False,
    )
```

```python
import functools

import jax
import jax.numpy as jnp
from jax import lax
from jax.experimental import pallas as pl
from jax.experimental.pallas import tpu as pltpu
from jax.sharding import PartitionSpec as P

LANES = 128
GROUP = 16
SUB = LANES // GROUP
WIN = 9
SLOT = WIN * SUB
SIDE = 4
CUT = 256
VMEM = 24 * 1024 * 1024
WIDE = 56 * 1024 * 1024


def seg_kernel(starts_ref, owner_ref, bytes_ref, out_ref, next_ref, low_ref, high_ref, acc_ref, turn_ref, held_ref, row_ref, sems):
    steps = sems.shape[0]
    shard, width = held_ref.shape
    block = shard // steps
    owners = LANES // SUB
    from_col = pl.ds(pl.multiple_of(lax.axis_index("tensor") * width, width), width)
    copies = []
    for k in range(steps):
        at = pl.ds(k * block, block)
        copies.append(pltpu.make_async_copy(bytes_ref.at[at, from_col], held_ref.at[at, :], sems.at[k]))
        copies[k].start()

    starts = starts_ref[...]
    rows = starts.shape[0]
    base = lax.axis_index("context") * shard
    for k in range(steps + 1):
        count = jnp.sum((starts <= base + k * block).astype(jnp.float32)).astype(jnp.int32)
        row_ref[k] = lax.shift_right_logical(count - 1, 7)
    first = jnp.minimum(row_ref[0], rows - WIN)
    lane = lax.broadcasted_iota(jnp.int32, starts.shape, 1)
    turned = pltpu.roll(starts, LANES - 1, 1)
    below = jnp.concatenate([turned[1:], jnp.full((1, LANES), 2**30, jnp.int32)], axis=0)
    next_ref[...] = jnp.where(lane == LANES - 1, below, turned)
    lane = lax.broadcasted_iota(jnp.int32, (SUB, LANES), 1)
    mine = lax.shift_right_logical(lane, 4) == lax.broadcasted_iota(jnp.int32, (SUB, LANES), 0)
    for t in range(WIN):
        low = jnp.clip(starts_ref[pl.ds(first + t, 1), :] - base, 0, shard).astype(jnp.float32)
        high = jnp.clip(next_ref[pl.ds(first + t, 1), :] - base, 0, shard).astype(jnp.float32)
        low = jnp.broadcast_to(low, (SUB, LANES))
        high = jnp.broadcast_to(high, (SUB, LANES))
        owner = jnp.broadcast_to(owner_ref[pl.ds(first + t, 1), :], (SUB, LANES))
        owner = jnp.where(mine, owner, -1)
        for j in range(owners):
            held = owner == j
            at = t * LANES + j * SUB
            one = jnp.sum(jnp.where(held, low, 0.0), axis=1, keepdims=True)
            low_ref[at : at + SUB, :] = jnp.broadcast_to(one, (SUB, LANES))
            one = jnp.sum(jnp.where(held, high, 0.0), axis=1, keepdims=True)
            high_ref[at : at + SUB, :] = jnp.broadcast_to(one, (SUB, LANES))
    acc_ref[...] = jnp.zeros_like(acc_ref)

    for k in range(steps):
        copies[k].wait()

        def one_row(t, carry, k=k):
            at = pl.ds(pl.multiple_of(t * LANES, LANES), LANES)
            low = low_ref[at, :]
            high = high_ref[at, :]
            parts = []
            for q in range(block // LANES):
                place = lax.broadcasted_iota(jnp.int32, (1, LANES), 1) + (k * block + q * LANES)
                place = place.astype(jnp.float32)
                parts.append(jnp.where((place >= low) & (place < high), 1.0, 0.0).astype(jnp.bfloat16))
            onehot = jnp.concatenate(parts, axis=1)
            acc_ref[at, :] += jnp.dot(
                onehot, held_ref[k * block : (k + 1) * block, :], preferred_element_type=jnp.float32
            )
            return carry

        lax.fori_loop(row_ref[k] - first, jnp.minimum(row_ref[k + 1] - first, WIN - 1) + 1, one_row, 0)

    for t in range(WIN):
        for j in range(owners):
            turn_ref[j * SLOT + t * SUB : j * SLOT + (t + 1) * SUB, :] = acc_ref[
                t * LANES + j * SUB : t * LANES + (j + 1) * SUB, :
            ]
    out_ref[...] = turn_ref[...].astype(jnp.bfloat16)


def segment_sums(starts, owner, grads, owners, width):
    steps = 8
    rows = owners * SLOT
    vmem = pl.BlockSpec(memory_space=pltpu.VMEM)
    return pl.pallas_call(
        seg_kernel,
        in_specs=[vmem, vmem, pl.BlockSpec(memory_space=pl.ANY)],
        out_shape=jax.ShapeDtypeStruct((rows, width), jnp.bfloat16),
        scratch_shapes=[
            pltpu.VMEM(starts.shape, jnp.int32),
            pltpu.VMEM((rows, LANES), jnp.float32),
            pltpu.VMEM((rows, LANES), jnp.float32),
            pltpu.VMEM((rows, width), jnp.float32),
            pltpu.VMEM((rows, width), jnp.float32),
            pltpu.VMEM((grads.shape[0], width), jnp.bfloat16),
            pltpu.SMEM((steps + 1,), jnp.int32),
            pltpu.SemaphoreType.DMA((steps,)),
        ],
        compiler_params=pltpu.CompilerParams(vmem_limit_bytes=WIDE),
    )(starts, owner, grads)


def collect_kernel(first_ref, in_ref, out_ref, wide_ref, acc_ref):
    wide_ref[...] = in_ref[...].astype(jnp.float32)
    acc_ref[...] = jnp.zeros_like(acc_ref)
    for s in range(in_ref.shape[0] // SLOT):
        at = pl.ds(pl.multiple_of(first_ref[s] * SUB, SUB), SLOT)
        acc_ref[at, :] += wide_ref[s * SLOT : (s + 1) * SLOT, :]
    out_ref[...] = acc_ref[...].T.astype(jnp.bfloat16)


def collect(first, incoming, patch_rows, interpret=False):
    rows, width = incoming.shape
    return pl.pallas_call(
        collect_kernel,
        in_specs=[pl.BlockSpec(memory_space=pltpu.SMEM), pl.BlockSpec(memory_space=pltpu.VMEM)],
        out_specs=pl.BlockSpec(memory_space=pltpu.VMEM),
        out_shape=jax.ShapeDtypeStruct((width, patch_rows), jnp.bfloat16),
        scratch_shapes=[pltpu.VMEM((rows, width), jnp.float32), pltpu.VMEM((patch_rows, width), jnp.float32)],
        compiler_params=pltpu.CompilerParams(vmem_limit_bytes=VMEM),
        interpret=interpret,
    )(first, incoming)


def outer_kernel(mine_ref, third_ref, cross_ref, n0_ref, n1a_ref, n1b_ref, f0_ref, f1a_ref, f1b_ref, out_ref, both_ref, held_ref, sems):
    near_t = jnp.where(lax.axis_index("dp") == 0, mine_ref[...], third_ref[...])
    far_t = cross_ref[...]
    both_ref[0] = near_t
    both_ref[1] = far_t
    low = lax.rem(lax.axis_index("tensor"), 2)
    blocks = out_ref.shape[0] // 2
    cols = n0_ref.shape[1]
    wide = 256
    per = wide // LANES
    copies = []
    for i in range(cols // wide):
        at = slice(i * wide, (i + 1) * wide)
        near1 = jnp.concatenate([n1a_ref[:, at], n1b_ref[:, at]], axis=0)
        far1 = jnp.concatenate([f1a_ref[:, at], f1b_ref[:, at]], axis=0)
        for k, (near, far, which) in enumerate(((n0_ref[:, at], f0_ref[:, at], low), (near1, far1, 1 - low))):
            total = jnp.dot(near_t, near, preferred_element_type=jnp.float32)
            total += jnp.dot(far_t, far, preferred_element_type=jnp.float32)
            total = total.astype(jnp.bfloat16)
            here = k * blocks + i * per
            for j in range(per):
                held_ref[here + j] = total[:, j * LANES : (j + 1) * LANES]
            copy = pltpu.make_async_copy(
                held_ref.at[pl.ds(here, per)],
                out_ref.at[pl.ds(which * blocks + i * per, per)],
                sems.at[2 * i + k],
            )
            copy.start()
            copies.append(copy)
    for copy in copies:
        copy.wait()


def outer(sums, columns):
    width, rows = sums[0].shape
    cols = columns[0].shape[1]
    vmem = pl.BlockSpec(memory_space=pltpu.VMEM)
    shape = (2 * cols // LANES, width, LANES)
    return pl.pallas_call(
        outer_kernel,
        in_specs=[vmem] * (len(sums) + len(columns)),
        out_specs=[pl.BlockSpec(memory_space=pltpu.HBM), vmem],
        out_shape=[
            jax.ShapeDtypeStruct(shape, jnp.bfloat16),
            jax.ShapeDtypeStruct((2, width, rows), jnp.bfloat16),
        ],
        scratch_shapes=[pltpu.VMEM(shape, jnp.bfloat16), pltpu.SemaphoreType.DMA((2 * cols // 256,))],
        compiler_params=pltpu.CompilerParams(vmem_limit_bytes=VMEM),
    )(*sums, *columns)


def quarter():
    ctx = lax.axis_index("context")
    return 2 * lax.rem(lax.div(ctx, SIDE), 2) + lax.rem(ctx, 2)


def chain_kernel(value_ref, out_w_ref, global_ref, both_ref, p0_ref, p1_ref, p2_ref, p3_ref, held_ref, sems):
    rows, wide = p0_ref.shape
    parts = held_ref.shape[0]
    dp, ten = lax.axis_index("dp"), lax.axis_index("tensor")
    copies = []
    for s in range(parts):
        at = (lax.rem(ten + s, parts) * 4 + quarter()) * rows
        copy = pltpu.make_async_copy(global_ref.at[pl.ds(pl.multiple_of(at, rows), rows)], held_ref.at[s], sems.at[s])
        copy.start()
        copies.append(copy)
    both_ref[...] = jnp.dot(
        value_ref[...], out_w_ref[...], preferred_element_type=jnp.float32
    ).astype(jnp.bfloat16)
    for s, p in enumerate((p0_ref, p1_ref, p2_ref, p3_ref)):
        copies[s].wait()
        half = lax.div(lax.rem(ten + s, parts), 2)
        half = dp + half - 2 * dp * half
        cols = pl.ds(pl.multiple_of(half * wide, wide), wide)
        p[...] = jnp.dot(held_ref[s], both_ref[:, cols], preferred_element_type=jnp.float32).astype(jnp.bfloat16)


def chain_terms(w_value, w_out, w_global, parts):
    deep, feats = w_value.shape
    rows = w_global.shape[0] // parts // 4
    vmem = pl.BlockSpec(memory_space=pltpu.VMEM)
    return pl.pallas_call(
        chain_kernel,
        in_specs=[vmem, vmem, pl.BlockSpec(memory_space=pl.ANY)],
        out_specs=[vmem] * (1 + parts),
        out_shape=[jax.ShapeDtypeStruct((deep, feats), jnp.bfloat16)]
        + [jax.ShapeDtypeStruct((rows, feats // 2), jnp.bfloat16)] * parts,
        scratch_shapes=[pltpu.VMEM((parts, rows, deep), jnp.bfloat16), pltpu.SemaphoreType.DMA((parts,))],
        compiler_params=pltpu.CompilerParams(vmem_limit_bytes=WIDE),
    )(w_value, w_out, w_global)


def rows_kernel(which, near_ref, far_ref, low_ref, high_ref, *rest):
    out_ref = rest[-1]
    deep = near_ref.shape[1]
    odd = lax.rem(lax.axis_index("tensor") + lax.axis_index("dp"), 2)
    near = near_ref[which].T
    far = far_ref[which].T
    rows = low_ref.shape[1]
    for i, ref in enumerate((low_ref, high_ref)):
        for j in range(2):
            z, y = lax.div(quarter(), 2), lax.rem(quarter(), 2)
            at = 2 * (z + i - 2 * i * z) + y + j - 2 * j * y
            at = pl.ds(pl.multiple_of(at * rows, rows), rows)
            first = ref[j, :, pl.ds(pl.multiple_of(odd * deep, deep), deep)]
            second = ref[j, :, pl.ds(pl.multiple_of((1 - odd) * deep, deep), deep)]
            dims = (((1,), (1,)), ((), ()))
            total = lax.dot_general(near, first, dims, preferred_element_type=jnp.float32)
            total += lax.dot_general(far, second, dims, preferred_element_type=jnp.float32)
            if len(rest) > 1:
                total += rest[0][:, at].astype(jnp.float32)
            out_ref[:, at] = total.astype(jnp.bfloat16)


def context_rows(which, near, far, low, high, *back):
    vmem = pl.BlockSpec(memory_space=pltpu.VMEM)
    return pl.pallas_call(
        functools.partial(rows_kernel, which),
        in_specs=[vmem] * (4 + len(back)),
        out_specs=vmem,
        out_shape=jax.ShapeDtypeStruct((near.shape[2], 4 * low.shape[1]), jnp.bfloat16),
        compiler_params=pltpu.CompilerParams(vmem_limit_bytes=VMEM),
    )(near, far, low, high, *back)


def last_kernel(a_ref, b_ref, c_ref, d_ref, w_ref, out_ref):
    width = a_ref.shape[0]
    dp, ten = lax.axis_index("dp"), lax.axis_index("tensor")
    total = jnp.zeros(out_ref.shape, jnp.float32)
    for s, ref in enumerate((a_ref, b_ref, c_ref, d_ref)):
        source = lax.bitwise_xor(ten, s)
        near = 2 * dp + lax.rem(source, 2)
        at = jnp.where(source < 2, near, 3 - near)
        total += lax.dot_general(
            ref[...].T,
            w_ref[:, pl.ds(pl.multiple_of(at * width, width), width)],
            (((1,), (1,)), ((), ())),
            preferred_element_type=jnp.float32,
        )
    out_ref[...] = total


def last(pieces, weights):
    vmem = pl.BlockSpec(memory_space=pltpu.VMEM)
    return pl.pallas_call(
        last_kernel,
        in_specs=[vmem] * (len(pieces) + 1),
        out_shape=jax.ShapeDtypeStruct((pieces[0].shape[1], weights.shape[0]), jnp.float32),
        compiler_params=pltpu.CompilerParams(vmem_limit_bytes=VMEM),
    )(*pieces, weights)


def after(value, *others):
    return lax.optimization_barrier((value, *others))[0]


def local(byte_grads, patch_starts, patch_owner, attn_context, w_global, w_value, w_out):
    dp_n, ctx_n, ten_n = (lax.axis_size(a) for a in ("dp", "context", "tensor"))
    f32, bf16 = jnp.float32, jnp.bfloat16
    bytes_n, feats = byte_grads.shape[1:]
    width = feats // ten_n
    patch_rows = attn_context.shape[1]
    starts = patch_starts.reshape(-1, LANES)
    owner = patch_owner.reshape(-1, LANES)
    line = ("dp", "tensor")

    def moves(target):
        pairs = []
        for d in range(dp_n):
            for x in range(ten_n):
                to = target(d, x)
                if to is not None:
                    pairs.append((d * ten_n + x, to[0] * ten_n + to[1]))
        return pairs

    swap = [(i, dp_n - 1 - i) for i in range(dp_n)]
    pair = [(x, x ^ 1) for x in range(ten_n)]
    near0 = attn_context[0]
    far0 = lax.ppermute(near0, "dp", swap)
    near1 = [lax.ppermute(near0[:CUT], "tensor", pair)]

    outgoing = segment_sums(starts, owner, byte_grads[0], ctx_n, width)

    both_t, *terms = chain_terms(after(w_value, outgoing), w_out, w_global, ten_n)
    outgoing = after(outgoing, near1[0], both_t, far0)
    incoming = lax.all_to_all(outgoing, "context", split_axis=0, concat_axis=0, tiled=True)

    chain = terms[0].astype(f32)
    for s in range(1, ten_n):
        term = after(terms[s], outgoing)
        chain += lax.ppermute(term, "tensor", [(x, (x + s) % ten_n) for x in range(ten_n)]).astype(f32)
    chain = chain.astype(bf16)
    edges = jnp.arange(ctx_n, dtype=jnp.int32) * bytes_n
    counts = jnp.sum((patch_starts[0][None, :] <= edges[:, None]).astype(jnp.int32), axis=1)
    first = jnp.minimum((counts - 1) // LANES, starts.shape[0] - WIN)
    far1 = [lax.ppermute(near1[0], "dp", swap)]
    incoming = after(incoming, first, far1[0])

    near1.append(lax.ppermute(after(near0, incoming)[CUT:], "tensor", pair))
    sums = collect(first, incoming, patch_rows)
    cross = lax.ppermute(sums, line, moves(lambda d, x: (0, x) if d == 1 else (1, ten_n - 1 - x)))
    third = lax.ppermute(sums, line, moves(lambda d, x: (1, ten_n - 1 - x) if d == 1 else None))

    def along(target):
        return [
            (i * SIDE + j, target(i, j)[0] * SIDE + target(i, j)[1]) for i in range(SIDE) for j in range(SIDE)
        ]

    chain = after(chain, sums)
    far1.append(lax.ppermute(after(near1[1], cross, third, chain), "dp", swap))
    other = lax.ppermute(chain, "context", along(lambda i, j: (i, j ^ 1)))
    columns = (near0, *near1, far0, *far1)
    partial, near = outer((sums, third, cross), columns)
    pieces = lax.all_to_all(partial, "context", split_axis=0, concat_axis=0, tiled=True)
    chain = jnp.stack([after(chain, partial), after(other, partial)])
    rest = lax.ppermute(chain, "context", along(lambda i, j: (i ^ 1, j)))

    far = lax.ppermute(near, "tensor", pair)
    give = context_rows(1, near, far, chain, rest)
    pieces = after(pieces, give)
    piece = jnp.sum(pieces.astype(f32), axis=0).astype(bf16)
    parts = []
    for s in range(ten_n):
        parts.append(lax.ppermute(piece, line, moves(lambda d, x, s=s: (x // 2, (2 * d + x % 2) ^ s))))
    back = lax.ppermute(give, "dp", swap)
    context_grad = context_rows(0, near, far, chain, rest, back)
    weight_grad = last(parts, both_t)
    return (context_grad[None], weight_grad)


def solution(mesh):
    placed = (
        P("dp", "context", None),
        P("dp", None),
        P("dp", None),
        P("dp", "context", "tensor"),
        P(None, "tensor"),
        P("tensor", None),
        P(),
    )
    return jax.shard_map(
        local,
        mesh=mesh,
        in_specs=placed,
        out_specs=(P("dp", "context", "tensor"), P(("dp", "context"), "tensor")),
        check_vma=False,
    )
```

```python
import functools

import jax
import jax.numpy as jnp
from jax import lax
from jax.experimental import pallas as pl
from jax.experimental.pallas import tpu as pltpu
from jax.sharding import PartitionSpec as P

LANES = 128
GROUP = 16
SUB = LANES // GROUP
WIN = 9
SLOT = WIN * SUB
SIDE = 4
CUT = 320
VMEM = 24 * 1024 * 1024
WIDE = 56 * 1024 * 1024


def seg_kernel(starts_ref, owner_ref, bytes_ref, out_ref, next_ref, low_ref, high_ref, acc_ref, turn_ref, held_ref, row_ref, sems):
    steps = sems.shape[0]
    shard, width = held_ref.shape
    block = shard // steps
    owners = LANES // SUB
    from_col = pl.ds(pl.multiple_of(lax.axis_index("tensor") * width, width), width)
    copies = []
    for k in range(steps):
        at = pl.ds(k * block, block)
        copies.append(pltpu.make_async_copy(bytes_ref.at[at, from_col], held_ref.at[at, :], sems.at[k]))
        copies[k].start()

    starts = starts_ref[...]
    rows = starts.shape[0]
    base = lax.axis_index("context") * shard
    for k in range(steps + 1):
        count = jnp.sum((starts <= base + k * block).astype(jnp.float32)).astype(jnp.int32)
        row_ref[k] = lax.shift_right_logical(count - 1, 7)
    first = jnp.minimum(row_ref[0], rows - WIN)
    lane = lax.broadcasted_iota(jnp.int32, starts.shape, 1)
    turned = pltpu.roll(starts, LANES - 1, 1)
    below = jnp.concatenate([turned[1:], jnp.full((1, LANES), 2**30, jnp.int32)], axis=0)
    next_ref[...] = jnp.where(lane == LANES - 1, below, turned)
    lane = lax.broadcasted_iota(jnp.int32, (SUB, LANES), 1)
    mine = lax.shift_right_logical(lane, 4) == lax.broadcasted_iota(jnp.int32, (SUB, LANES), 0)
    for t in range(WIN):
        low = jnp.clip(starts_ref[pl.ds(first + t, 1), :] - base, 0, shard).astype(jnp.float32)
        high = jnp.clip(next_ref[pl.ds(first + t, 1), :] - base, 0, shard).astype(jnp.float32)
        low = jnp.broadcast_to(low, (SUB, LANES))
        high = jnp.broadcast_to(high, (SUB, LANES))
        owner = jnp.broadcast_to(owner_ref[pl.ds(first + t, 1), :], (SUB, LANES))
        owner = jnp.where(mine, owner, -1)
        for j in range(owners):
            held = owner == j
            at = t * LANES + j * SUB
            one = jnp.sum(jnp.where(held, low, 0.0), axis=1, keepdims=True)
            low_ref[at : at + SUB, :] = jnp.broadcast_to(one, (SUB, LANES))
            one = jnp.sum(jnp.where(held, high, 0.0), axis=1, keepdims=True)
            high_ref[at : at + SUB, :] = jnp.broadcast_to(one, (SUB, LANES))
    acc_ref[...] = jnp.zeros_like(acc_ref)

    for k in range(steps):
        copies[k].wait()

        def one_row(t, carry, k=k):
            at = pl.ds(pl.multiple_of(t * LANES, LANES), LANES)
            low = low_ref[at, :]
            high = high_ref[at, :]
            parts = []
            for q in range(block // LANES):
                place = lax.broadcasted_iota(jnp.int32, (1, LANES), 1) + (k * block + q * LANES)
                place = place.astype(jnp.float32)
                parts.append(jnp.where((place >= low) & (place < high), 1.0, 0.0).astype(jnp.bfloat16))
            onehot = jnp.concatenate(parts, axis=1)
            acc_ref[at, :] += jnp.dot(
                onehot, held_ref[k * block : (k + 1) * block, :], preferred_element_type=jnp.float32
            )
            return carry

        lax.fori_loop(row_ref[k] - first, jnp.minimum(row_ref[k + 1] - first, WIN - 1) + 1, one_row, 0)

    for t in range(WIN):
        for j in range(owners):
            turn_ref[j * SLOT + t * SUB : j * SLOT + (t + 1) * SUB, :] = acc_ref[
                t * LANES + j * SUB : t * LANES + (j + 1) * SUB, :
            ]
    out_ref[...] = turn_ref[...].astype(jnp.bfloat16)


def segment_sums(starts, owner, grads, owners, width):
    steps = 8
    rows = owners * SLOT
    vmem = pl.BlockSpec(memory_space=pltpu.VMEM)
    return pl.pallas_call(
        seg_kernel,
        in_specs=[vmem, vmem, pl.BlockSpec(memory_space=pl.ANY)],
        out_shape=jax.ShapeDtypeStruct((rows, width), jnp.bfloat16),
        scratch_shapes=[
            pltpu.VMEM(starts.shape, jnp.int32),
            pltpu.VMEM((rows, LANES), jnp.float32),
            pltpu.VMEM((rows, LANES), jnp.float32),
            pltpu.VMEM((rows, width), jnp.float32),
            pltpu.VMEM((rows, width), jnp.float32),
            pltpu.VMEM((grads.shape[0], width), jnp.bfloat16),
            pltpu.SMEM((steps + 1,), jnp.int32),
            pltpu.SemaphoreType.DMA((steps,)),
        ],
        compiler_params=pltpu.CompilerParams(vmem_limit_bytes=WIDE),
    )(starts, owner, grads)


def collect_kernel(first_ref, in_ref, out_ref, wide_ref, acc_ref):
    wide_ref[...] = in_ref[...].astype(jnp.float32)
    acc_ref[...] = jnp.zeros_like(acc_ref)
    for s in range(in_ref.shape[0] // SLOT):
        at = pl.ds(pl.multiple_of(first_ref[s] * SUB, SUB), SLOT)
        acc_ref[at, :] += wide_ref[s * SLOT : (s + 1) * SLOT, :]
    out_ref[...] = acc_ref[...].T.astype(jnp.bfloat16)


def collect(first, incoming, patch_rows, interpret=False):
    rows, width = incoming.shape
    return pl.pallas_call(
        collect_kernel,
        in_specs=[pl.BlockSpec(memory_space=pltpu.SMEM), pl.BlockSpec(memory_space=pltpu.VMEM)],
        out_specs=pl.BlockSpec(memory_space=pltpu.VMEM),
        out_shape=jax.ShapeDtypeStruct((width, patch_rows), jnp.bfloat16),
        scratch_shapes=[pltpu.VMEM((rows, width), jnp.float32), pltpu.VMEM((patch_rows, width), jnp.float32)],
        compiler_params=pltpu.CompilerParams(vmem_limit_bytes=VMEM),
        interpret=interpret,
    )(first, incoming)


def outer_kernel(mine_ref, third_ref, cross_ref, n0_ref, n1a_ref, n1b_ref, f0_ref, f1a_ref, f1b_ref, out_ref, both_ref, held_ref, sems):
    near_t = jnp.where(lax.axis_index("dp") == 0, mine_ref[...], third_ref[...])
    far_t = cross_ref[...]
    both_ref[0] = near_t
    both_ref[1] = far_t
    low = lax.rem(lax.axis_index("tensor"), 2)
    blocks = out_ref.shape[0] // 2
    cols = n0_ref.shape[1]
    wide = 256
    per = wide // LANES
    copies = []
    for i in range(cols // wide):
        at = slice(i * wide, (i + 1) * wide)
        near1 = jnp.concatenate([n1a_ref[:, at], n1b_ref[:, at]], axis=0)
        far1 = jnp.concatenate([f1a_ref[:, at], f1b_ref[:, at]], axis=0)
        for k, (near, far, which) in enumerate(((n0_ref[:, at], f0_ref[:, at], low), (near1, far1, 1 - low))):
            total = jnp.dot(near_t, near, preferred_element_type=jnp.float32)
            total += jnp.dot(far_t, far, preferred_element_type=jnp.float32)
            total = total.astype(jnp.bfloat16)
            here = k * blocks + i * per
            for j in range(per):
                held_ref[here + j] = total[:, j * LANES : (j + 1) * LANES]
            copy = pltpu.make_async_copy(
                held_ref.at[pl.ds(here, per)],
                out_ref.at[pl.ds(which * blocks + i * per, per)],
                sems.at[2 * i + k],
            )
            copy.start()
            copies.append(copy)
    for copy in copies:
        copy.wait()


def outer(sums, columns):
    width, rows = sums[0].shape
    cols = columns[0].shape[1]
    vmem = pl.BlockSpec(memory_space=pltpu.VMEM)
    shape = (2 * cols // LANES, width, LANES)
    return pl.pallas_call(
        outer_kernel,
        in_specs=[vmem] * (len(sums) + len(columns)),
        out_specs=[pl.BlockSpec(memory_space=pltpu.HBM), vmem],
        out_shape=[
            jax.ShapeDtypeStruct(shape, jnp.bfloat16),
            jax.ShapeDtypeStruct((2, width, rows), jnp.bfloat16),
        ],
        scratch_shapes=[pltpu.VMEM(shape, jnp.bfloat16), pltpu.SemaphoreType.DMA((2 * cols // 256,))],
        compiler_params=pltpu.CompilerParams(vmem_limit_bytes=VMEM),
    )(*sums, *columns)


def eighth():
    ctx = lax.axis_index("context")
    return 2 * lax.div(ctx, SIDE) + lax.rem(ctx, 2)


def flip(a, b):
    return a + b - 2 * b * lax.rem(a, 2)


def chain_kernel(value_ref, out_w_ref, global_ref, both_ref, own_ref, pair_ref, away_ref, held_ref, sems):
    rows, wide = own_ref.shape
    dp, ten = lax.axis_index("dp"), lax.axis_index("tensor")
    targets = (ten, flip(ten, 1), 3 - ten, flip(3 - ten, 1))
    copies = []
    for s, target in enumerate(targets):
        at = (target * 8 + eighth()) * rows
        copy = pltpu.make_async_copy(global_ref.at[pl.ds(pl.multiple_of(at, rows), rows)], held_ref.at[s], sems.at[s])
        copy.start()
        copies.append(copy)
    both_ref[...] = jnp.dot(
        value_ref[...], out_w_ref[...], preferred_element_type=jnp.float32
    ).astype(jnp.bfloat16)
    for s in range(0, 4, 2):
        copies[s].wait()
        copies[s + 1].wait()
        half = flip(dp, lax.div(targets[s], 2))
        cols = pl.ds(pl.multiple_of(half * wide, wide), wide)
        left = jnp.concatenate([held_ref[s], held_ref[s + 1]], axis=0)
        total = jnp.dot(left, both_ref[:, cols], preferred_element_type=jnp.float32).astype(jnp.bfloat16)
        if s == 0:
            own_ref[...] = total[:rows]
            pair_ref[...] = total[rows:]
        else:
            away_ref[0] = total[:rows]
            away_ref[1] = total[rows:]


def chain_terms(w_value, w_out, w_global):
    deep, feats = w_value.shape
    rows = w_global.shape[0] // 32
    vmem = pl.BlockSpec(memory_space=pltpu.VMEM)
    part = jax.ShapeDtypeStruct((rows, feats // 2), jnp.bfloat16)
    return pl.pallas_call(
        chain_kernel,
        in_specs=[vmem, vmem, pl.BlockSpec(memory_space=pl.ANY)],
        out_specs=[vmem] * 4,
        out_shape=[
            jax.ShapeDtypeStruct((deep, feats), jnp.bfloat16),
            part,
            part,
            jax.ShapeDtypeStruct((2, rows, feats // 2), jnp.bfloat16),
        ],
        scratch_shapes=[pltpu.VMEM((4, rows, deep), jnp.bfloat16), pltpu.SemaphoreType.DMA((4,))],
        compiler_params=pltpu.CompilerParams(vmem_limit_bytes=WIDE),
    )(w_value, w_out, w_global)


def rows_kernel(which, near_ref, far_ref, low_ref, high_ref, *rest):
    out_ref, table_ref = rest[-2:]
    deep = near_ref.shape[1]
    rows = low_ref.shape[2]
    z, y = lax.div(eighth(), 2), lax.rem(eighth(), 2)
    for ref, base in ((low_ref, z), (high_ref, SIDE - 1 - z)):
        for i in range(2):
            for j in range(2):
                to = 2 * flip(base, i) + flip(y, j)
                table_ref[pl.ds(pl.multiple_of(to * rows, rows), rows), :] = ref[i, j]
    odd = lax.rem(lax.axis_index("tensor") + lax.axis_index("dp"), 2)
    dims = (((1,), (1,)), ((), ()))
    first = table_ref[:, pl.ds(pl.multiple_of(odd * deep, deep), deep)]
    second = table_ref[:, pl.ds(pl.multiple_of((1 - odd) * deep, deep), deep)]
    total = lax.dot_general(near_ref[which].T, first, dims, preferred_element_type=jnp.float32)
    total += lax.dot_general(far_ref[which].T, second, dims, preferred_element_type=jnp.float32)
    if len(rest) > 2:
        total += rest[0][...].astype(jnp.float32)
    out_ref[...] = total.astype(jnp.bfloat16)


def context_rows(which, near, far, low, high, *back):
    vmem = pl.BlockSpec(memory_space=pltpu.VMEM)
    cols, half = 8 * low.shape[2], low.shape[3]
    return pl.pallas_call(
        functools.partial(rows_kernel, which),
        in_specs=[vmem] * (4 + len(back)),
        out_specs=vmem,
        out_shape=jax.ShapeDtypeStruct((near.shape[2], cols), jnp.bfloat16),
        scratch_shapes=[pltpu.VMEM((cols, half), jnp.bfloat16)],
        compiler_params=pltpu.CompilerParams(vmem_limit_bytes=VMEM),
    )(near, far, low, high, *back)


def last_kernel(a_ref, b_ref, c_ref, d_ref, w_ref, out_ref):
    width = a_ref.shape[0]
    dp, ten = lax.axis_index("dp"), lax.axis_index("tensor")
    total = jnp.zeros(out_ref.shape, jnp.float32)
    for s, ref in enumerate((a_ref, b_ref, c_ref, d_ref)):
        source = lax.bitwise_xor(ten, s)
        near = 2 * dp + lax.rem(source, 2)
        at = jnp.where(source < 2, near, 3 - near)
        total += lax.dot_general(
            ref[...].T,
            w_ref[:, pl.ds(pl.multiple_of(at * width, width), width)],
            (((1,), (1,)), ((), ())),
            preferred_element_type=jnp.float32,
        )
    out_ref[...] = total


def last(pieces, weights):
    vmem = pl.BlockSpec(memory_space=pltpu.VMEM)
    return pl.pallas_call(
        last_kernel,
        in_specs=[vmem] * (len(pieces) + 1),
        out_shape=jax.ShapeDtypeStruct((pieces[0].shape[1], weights.shape[0]), jnp.float32),
        compiler_params=pltpu.CompilerParams(vmem_limit_bytes=VMEM),
    )(*pieces, weights)


def after(value, *others):
    return lax.optimization_barrier((value, *others))[0]


def local(byte_grads, patch_starts, patch_owner, attn_context, w_global, w_value, w_out):
    dp_n, ctx_n, ten_n = (lax.axis_size(a) for a in ("dp", "context", "tensor"))
    f32, bf16 = jnp.float32, jnp.bfloat16
    bytes_n, feats = byte_grads.shape[1:]
    width = feats // ten_n
    patch_rows = attn_context.shape[1]
    starts = patch_starts.reshape(-1, LANES)
    owner = patch_owner.reshape(-1, LANES)
    line = ("dp", "tensor")

    def moves(target):
        pairs = []
        for d in range(dp_n):
            for x in range(ten_n):
                to = target(d, x)
                if to is not None:
                    pairs.append((d * ten_n + x, to[0] * ten_n + to[1]))
        return pairs

    swap = [(i, dp_n - 1 - i) for i in range(dp_n)]
    pair = [(x, x ^ 1) for x in range(ten_n)]
    near0 = attn_context[0]
    far0 = lax.ppermute(near0, "dp", swap)
    near1 = [lax.ppermute(near0[:CUT], "tensor", pair)]

    def along(target):
        return [
            (i * SIDE + j, target(i, j)[0] * SIDE + target(i, j)[1]) for i in range(SIDE) for j in range(SIDE)
        ]

    both_t, own, paired, away = chain_terms(w_value, w_out, w_global)
    away = lax.ppermute(away, "tensor", [(x, ten_n - 1 - x) for x in range(ten_n)])

    outgoing = segment_sums(after(starts, both_t), owner, byte_grads[0], ctx_n, width)
    outgoing = after(outgoing, near1[0], far0, away)
    incoming = lax.all_to_all(outgoing, "context", split_axis=0, concat_axis=0, tiled=True)

    away = after(away, outgoing)
    paired = (paired.astype(f32) + away[1].astype(f32)).astype(bf16)
    paired = lax.ppermute(paired, "tensor", pair)
    chain = (own.astype(f32) + away[0].astype(f32) + paired.astype(f32)).astype(bf16)
    chain = jnp.stack([chain, lax.ppermute(chain, "context", along(lambda i, j: (i, j ^ 1)))])
    edges = jnp.arange(ctx_n, dtype=jnp.int32) * bytes_n
    counts = jnp.sum((patch_starts[0][None, :] <= edges[:, None]).astype(jnp.int32), axis=1)
    first = jnp.minimum((counts - 1) // LANES, starts.shape[0] - WIN)
    far1 = [lax.ppermute(near1[0], "dp", swap)]
    incoming = after(incoming, first, far1[0], chain)

    near1.append(lax.ppermute(after(near0, incoming)[CUT:], "tensor", pair))
    sums = collect(first, incoming, patch_rows)
    cross = lax.ppermute(sums, line, moves(lambda d, x: (0, x) if d == 1 else (1, ten_n - 1 - x)))
    third = lax.ppermute(sums, line, moves(lambda d, x: (1, ten_n - 1 - x) if d == 1 else None))
    chain = after(chain, sums)
    other = lax.ppermute(chain, "context", along(lambda i, j: (i ^ 1, j)))
    far1.append(lax.ppermute(after(near1[1], cross, third), "dp", swap))
    columns = (near0, *near1, far0, *far1)
    partial, near = outer((sums, third, cross), columns)
    pieces = lax.all_to_all(partial, "context", split_axis=0, concat_axis=0, tiled=True)
    chain = jnp.stack([after(chain, partial), after(other, partial)])
    rest = lax.ppermute(chain, "context", along(lambda i, j: (SIDE - 1 - i, j)))

    far = lax.ppermute(near, "tensor", pair)
    give = context_rows(1, near, far, chain, rest)
    pieces = after(pieces, give)
    piece = jnp.sum(pieces.astype(f32), axis=0).astype(bf16)
    parts = []
    for s in range(ten_n):
        parts.append(lax.ppermute(piece, line, moves(lambda d, x, s=s: (x // 2, (2 * d + x % 2) ^ s))))
    back = lax.ppermute(give, "dp", swap)
    context_grad = context_rows(0, near, far, chain, rest, back)
    weight_grad = last(parts, both_t)
    return (context_grad[None], weight_grad)


def solution(mesh):
    placed = (
        P("dp", "context", None),
        P("dp", None),
        P("dp", None),
        P("dp", "context", "tensor"),
        P(None, "tensor"),
        P("tensor", None),
        P(),
    )
    return jax.shard_map(
        local,
        mesh=mesh,
        in_specs=placed,
        out_specs=(P("dp", "context", "tensor"), P(("dp", "context"), "tensor")),
        check_vma=False,
    )
```

```python
import functools

import jax
import jax.numpy as jnp
from jax import lax
from jax.experimental import pallas as pl
from jax.experimental.pallas import tpu as pltpu
from jax.sharding import PartitionSpec as P

LANES = 128
GROUP = 16
SUB = LANES // GROUP
WIN = 9
SLOT = WIN * SUB
SIDE = 4
CUT = 320
VMEM = 24 * 1024 * 1024
WIDE = 56 * 1024 * 1024


def seg_kernel(starts_ref, owner_ref, bytes_ref, out_ref, next_ref, low_ref, high_ref, acc_ref, turn_ref, held_ref, row_ref, sems):
    steps = sems.shape[0]
    shard, width = held_ref.shape
    block = shard // steps
    owners = LANES // SUB
    from_col = pl.ds(pl.multiple_of(lax.axis_index("tensor") * width, width), width)
    copies = []
    for k in range(steps):
        at = pl.ds(k * block, block)
        copies.append(pltpu.make_async_copy(bytes_ref.at[at, from_col], held_ref.at[at, :], sems.at[k]))
        copies[k].start()

    starts = starts_ref[...]
    rows = starts.shape[0]
    base = lax.axis_index("context") * shard
    for k in range(steps + 1):
        count = jnp.sum((starts <= base + k * block).astype(jnp.float32)).astype(jnp.int32)
        row_ref[k] = lax.shift_right_logical(count - 1, 7)
    first = jnp.minimum(row_ref[0], rows - WIN)
    lane = lax.broadcasted_iota(jnp.int32, starts.shape, 1)
    turned = pltpu.roll(starts, LANES - 1, 1)
    below = jnp.concatenate([turned[1:], jnp.full((1, LANES), 2**30, jnp.int32)], axis=0)
    next_ref[...] = jnp.where(lane == LANES - 1, below, turned)
    lane = lax.broadcasted_iota(jnp.int32, (SUB, LANES), 1)
    mine = lax.shift_right_logical(lane, 4) == lax.broadcasted_iota(jnp.int32, (SUB, LANES), 0)
    for t in range(WIN):
        low = jnp.clip(starts_ref[pl.ds(first + t, 1), :] - base, 0, shard).astype(jnp.float32)
        high = jnp.clip(next_ref[pl.ds(first + t, 1), :] - base, 0, shard).astype(jnp.float32)
        low = jnp.broadcast_to(low, (SUB, LANES))
        high = jnp.broadcast_to(high, (SUB, LANES))
        owner = jnp.broadcast_to(owner_ref[pl.ds(first + t, 1), :], (SUB, LANES))
        owner = jnp.where(mine, owner, -1)
        for j in range(owners):
            held = owner == j
            at = t * LANES + j * SUB
            one = jnp.sum(jnp.where(held, low, 0.0), axis=1, keepdims=True)
            low_ref[at : at + SUB, :] = jnp.broadcast_to(one, (SUB, LANES))
            one = jnp.sum(jnp.where(held, high, 0.0), axis=1, keepdims=True)
            high_ref[at : at + SUB, :] = jnp.broadcast_to(one, (SUB, LANES))
    acc_ref[...] = jnp.zeros_like(acc_ref)

    for k in range(steps):
        copies[k].wait()

        def one_row(t, carry, k=k):
            at = pl.ds(pl.multiple_of(t * LANES, LANES), LANES)
            low = low_ref[at, :]
            high = high_ref[at, :]
            parts = []
            for q in range(block // LANES):
                place = lax.broadcasted_iota(jnp.int32, (1, LANES), 1) + (k * block + q * LANES)
                place = place.astype(jnp.float32)
                parts.append(jnp.where((place >= low) & (place < high), 1.0, 0.0).astype(jnp.bfloat16))
            onehot = jnp.concatenate(parts, axis=1)
            acc_ref[at, :] += jnp.dot(
                onehot, held_ref[k * block : (k + 1) * block, :], preferred_element_type=jnp.float32
            )
            return carry

        lax.fori_loop(row_ref[k] - first, jnp.minimum(row_ref[k + 1] - first, WIN - 1) + 1, one_row, 0)

    for t in range(WIN):
        for j in range(owners):
            turn_ref[j * SLOT + t * SUB : j * SLOT + (t + 1) * SUB, :] = acc_ref[
                t * LANES + j * SUB : t * LANES + (j + 1) * SUB, :
            ]
    out_ref[...] = turn_ref[...].astype(jnp.bfloat16)


def segment_sums(starts, owner, grads, owners, width):
    steps = 8
    rows = owners * SLOT
    vmem = pl.BlockSpec(memory_space=pltpu.VMEM)
    return pl.pallas_call(
        seg_kernel,
        in_specs=[vmem, vmem, pl.BlockSpec(memory_space=pl.ANY)],
        out_shape=jax.ShapeDtypeStruct((rows, width), jnp.bfloat16),
        scratch_shapes=[
            pltpu.VMEM(starts.shape, jnp.int32),
            pltpu.VMEM((rows, LANES), jnp.float32),
            pltpu.VMEM((rows, LANES), jnp.float32),
            pltpu.VMEM((rows, width), jnp.float32),
            pltpu.VMEM((rows, width), jnp.float32),
            pltpu.VMEM((grads.shape[0], width), jnp.bfloat16),
            pltpu.SMEM((steps + 1,), jnp.int32),
            pltpu.SemaphoreType.DMA((steps,)),
        ],
        compiler_params=pltpu.CompilerParams(vmem_limit_bytes=WIDE),
    )(starts, owner, grads)


def collect_kernel(first_ref, in_ref, out_ref, wide_ref, acc_ref):
    wide_ref[...] = in_ref[...].astype(jnp.float32)
    acc_ref[...] = jnp.zeros_like(acc_ref)
    for s in range(in_ref.shape[0] // SLOT):
        at = pl.ds(pl.multiple_of(first_ref[s] * SUB, SUB), SLOT)
        acc_ref[at, :] += wide_ref[s * SLOT : (s + 1) * SLOT, :]
    out_ref[...] = acc_ref[...].T.astype(jnp.bfloat16)


def collect(first, incoming, patch_rows, interpret=False):
    rows, width = incoming.shape
    return pl.pallas_call(
        collect_kernel,
        in_specs=[pl.BlockSpec(memory_space=pltpu.SMEM), pl.BlockSpec(memory_space=pltpu.VMEM)],
        out_specs=pl.BlockSpec(memory_space=pltpu.VMEM),
        out_shape=jax.ShapeDtypeStruct((width, patch_rows), jnp.bfloat16),
        scratch_shapes=[pltpu.VMEM((rows, width), jnp.float32), pltpu.VMEM((patch_rows, width), jnp.float32)],
        compiler_params=pltpu.CompilerParams(vmem_limit_bytes=VMEM),
        interpret=interpret,
    )(first, incoming)


def outer_kernel(mine_ref, third_ref, cross_ref, n0_ref, n1a_ref, n1b_ref, f0_ref, f1a_ref, f1b_ref, out_ref, both_ref, held_ref, sems):
    near_t = jnp.where(lax.axis_index("dp") == 0, mine_ref[...], third_ref[...])
    far_t = cross_ref[...]
    both_ref[0] = near_t
    both_ref[1] = far_t
    low = lax.rem(lax.axis_index("tensor"), 2)
    blocks = out_ref.shape[0] // 2
    cols = n0_ref.shape[1]
    wide = 256
    per = wide // LANES
    copies = []
    for i in range(cols // wide):
        at = slice(i * wide, (i + 1) * wide)
        near1 = jnp.concatenate([n1a_ref[:, at], n1b_ref[:, at]], axis=0)
        far1 = jnp.concatenate([f1a_ref[:, at], f1b_ref[:, at]], axis=0)
        for k, (near, far, which) in enumerate(((n0_ref[:, at], f0_ref[:, at], low), (near1, far1, 1 - low))):
            total = jnp.dot(near_t, near, preferred_element_type=jnp.float32)
            total += jnp.dot(far_t, far, preferred_element_type=jnp.float32)
            total = total.astype(jnp.bfloat16)
            here = k * blocks + i * per
            for j in range(per):
                held_ref[here + j] = total[:, j * LANES : (j + 1) * LANES]
            copy = pltpu.make_async_copy(
                held_ref.at[pl.ds(here, per)],
                out_ref.at[pl.ds(which * blocks + i * per, per)],
                sems.at[2 * i + k],
            )
            copy.start()
            copies.append(copy)
    for copy in copies:
        copy.wait()


def outer(sums, columns):
    width, rows = sums[0].shape
    cols = columns[0].shape[1]
    vmem = pl.BlockSpec(memory_space=pltpu.VMEM)
    shape = (2 * cols // LANES, width, LANES)
    return pl.pallas_call(
        outer_kernel,
        in_specs=[vmem] * (len(sums) + len(columns)),
        out_specs=[pl.BlockSpec(memory_space=pltpu.HBM), vmem],
        out_shape=[
            jax.ShapeDtypeStruct(shape, jnp.bfloat16),
            jax.ShapeDtypeStruct((2, width, rows), jnp.bfloat16),
        ],
        scratch_shapes=[pltpu.VMEM(shape, jnp.bfloat16), pltpu.SemaphoreType.DMA((2 * cols // 256,))],
        compiler_params=pltpu.CompilerParams(vmem_limit_bytes=VMEM),
    )(*sums, *columns)


def eighth():
    ctx = lax.axis_index("context")
    return 2 * lax.div(ctx, SIDE) + lax.rem(ctx, 2)


def flip(a, b):
    return a + b - 2 * b * lax.rem(a, 2)


def chain_kernel(value_ref, out_w_ref, global_ref, both_ref, own_ref, pair_ref, away_ref, held_ref, sems):
    rows, wide = own_ref.shape
    dp, ten = lax.axis_index("dp"), lax.axis_index("tensor")
    targets = (ten, flip(ten, 1), 3 - ten, flip(3 - ten, 1))
    copies = []
    for s, target in enumerate(targets):
        at = (target * 8 + eighth()) * rows
        copy = pltpu.make_async_copy(global_ref.at[pl.ds(pl.multiple_of(at, rows), rows)], held_ref.at[s], sems.at[s])
        copy.start()
        copies.append(copy)
    both_ref[...] = jnp.dot(
        value_ref[...], out_w_ref[...], preferred_element_type=jnp.float32
    ).astype(jnp.bfloat16)
    for s in range(0, 4, 2):
        copies[s].wait()
        copies[s + 1].wait()
        half = flip(dp, lax.div(targets[s], 2))
        cols = pl.ds(pl.multiple_of(half * wide, wide), wide)
        left = jnp.concatenate([held_ref[s], held_ref[s + 1]], axis=0)
        total = jnp.dot(left, both_ref[:, cols], preferred_element_type=jnp.float32).astype(jnp.bfloat16)
        if s == 0:
            own_ref[...] = total[:rows]
            pair_ref[...] = total[rows:]
        else:
            away_ref[0] = total[:rows]
            away_ref[1] = total[rows:]


def chain_terms(w_value, w_out, w_global):
    deep, feats = w_value.shape
    rows = w_global.shape[0] // 32
    vmem = pl.BlockSpec(memory_space=pltpu.VMEM)
    part = jax.ShapeDtypeStruct((rows, feats // 2), jnp.bfloat16)
    return pl.pallas_call(
        chain_kernel,
        in_specs=[vmem, vmem, pl.BlockSpec(memory_space=pl.ANY)],
        out_specs=[vmem] * 4,
        out_shape=[
            jax.ShapeDtypeStruct((deep, feats), jnp.bfloat16),
            part,
            part,
            jax.ShapeDtypeStruct((2, rows, feats // 2), jnp.bfloat16),
        ],
        scratch_shapes=[pltpu.VMEM((4, rows, deep), jnp.bfloat16), pltpu.SemaphoreType.DMA((4,))],
        compiler_params=pltpu.CompilerParams(vmem_limit_bytes=WIDE),
    )(w_value, w_out, w_global)


def rows_kernel(which, near_ref, far_ref, low_ref, high_ref, *rest):
    out_ref, table_ref = rest[-2:]
    deep = near_ref.shape[1]
    rows = low_ref.shape[2]
    z, y = lax.div(eighth(), 2), lax.rem(eighth(), 2)
    for ref, base in ((low_ref, z), (high_ref, SIDE - 1 - z)):
        for i in range(2):
            for j in range(2):
                to = 2 * flip(base, i) + flip(y, j)
                table_ref[pl.ds(pl.multiple_of(to * rows, rows), rows), :] = ref[i, j]
    odd = lax.rem(lax.axis_index("tensor") + lax.axis_index("dp"), 2)
    dims = (((1,), (1,)), ((), ()))
    first = table_ref[:, pl.ds(pl.multiple_of(odd * deep, deep), deep)]
    second = table_ref[:, pl.ds(pl.multiple_of((1 - odd) * deep, deep), deep)]
    total = lax.dot_general(near_ref[which].T, first, dims, preferred_element_type=jnp.float32)
    total += lax.dot_general(far_ref[which].T, second, dims, preferred_element_type=jnp.float32)
    if len(rest) > 2:
        total += rest[0][...].astype(jnp.float32)
    out_ref[...] = total.astype(jnp.bfloat16)


def context_rows(which, near, far, low, high, *back):
    vmem = pl.BlockSpec(memory_space=pltpu.VMEM)
    cols, half = 8 * low.shape[2], low.shape[3]
    return pl.pallas_call(
        functools.partial(rows_kernel, which),
        in_specs=[vmem] * (4 + len(back)),
        out_specs=vmem,
        out_shape=jax.ShapeDtypeStruct((near.shape[2], cols), jnp.bfloat16),
        scratch_shapes=[pltpu.VMEM((cols, half), jnp.bfloat16)],
        compiler_params=pltpu.CompilerParams(vmem_limit_bytes=VMEM),
    )(near, far, low, high, *back)


def last_kernel(a_ref, b_ref, c_ref, d_ref, w_ref, out_ref):
    width = a_ref.shape[0]
    dp, ten = lax.axis_index("dp"), lax.axis_index("tensor")
    total = jnp.zeros(out_ref.shape, jnp.float32)
    for s, ref in enumerate((a_ref, b_ref, c_ref, d_ref)):
        source = lax.bitwise_xor(ten, s)
        near = 2 * dp + lax.rem(source, 2)
        at = jnp.where(source < 2, near, 3 - near)
        total += lax.dot_general(
            ref[...].T,
            w_ref[:, pl.ds(pl.multiple_of(at * width, width), width)],
            (((1,), (1,)), ((), ())),
            preferred_element_type=jnp.float32,
        )
    out_ref[...] = total


def last(pieces, weights):
    vmem = pl.BlockSpec(memory_space=pltpu.VMEM)
    return pl.pallas_call(
        last_kernel,
        in_specs=[vmem] * (len(pieces) + 1),
        out_shape=jax.ShapeDtypeStruct((pieces[0].shape[1], weights.shape[0]), jnp.float32),
        compiler_params=pltpu.CompilerParams(vmem_limit_bytes=VMEM),
    )(*pieces, weights)


def after(value, *others):
    return lax.optimization_barrier((value, *others))[0]


def local(byte_grads, patch_starts, patch_owner, attn_context, w_global, w_value, w_out):
    dp_n, ctx_n, ten_n = (lax.axis_size(a) for a in ("dp", "context", "tensor"))
    f32, bf16 = jnp.float32, jnp.bfloat16
    bytes_n, feats = byte_grads.shape[1:]
    width = feats // ten_n
    patch_rows = attn_context.shape[1]
    starts = patch_starts.reshape(-1, LANES)
    owner = patch_owner.reshape(-1, LANES)
    line = ("dp", "tensor")

    def moves(target):
        pairs = []
        for d in range(dp_n):
            for x in range(ten_n):
                to = target(d, x)
                if to is not None:
                    pairs.append((d * ten_n + x, to[0] * ten_n + to[1]))
        return pairs

    swap = [(i, dp_n - 1 - i) for i in range(dp_n)]
    pair = [(x, x ^ 1) for x in range(ten_n)]
    near0 = attn_context[0]
    far0 = lax.ppermute(near0, "dp", swap)
    near1 = [lax.ppermute(near0[:CUT], "tensor", pair)]

    def along(target):
        return [
            (i * SIDE + j, target(i, j)[0] * SIDE + target(i, j)[1]) for i in range(SIDE) for j in range(SIDE)
        ]

    both_t, own, paired, away = chain_terms(w_value, w_out, w_global)
    away = lax.ppermute(away, "tensor", [(x, ten_n - 1 - x) for x in range(ten_n)])

    outgoing = segment_sums(after(starts, both_t), owner, byte_grads[0], ctx_n, width)
    outgoing = after(outgoing, near1[0], away)
    incoming = lax.all_to_all(outgoing, "context", split_axis=0, concat_axis=0, tiled=True)

    away = after(away, outgoing)
    paired = (paired.astype(f32) + away[1].astype(f32)).astype(bf16)
    paired = lax.ppermute(paired, "tensor", pair)
    chain = (own.astype(f32) + away[0].astype(f32) + paired.astype(f32)).astype(bf16)
    edges = jnp.arange(ctx_n, dtype=jnp.int32) * bytes_n
    counts = jnp.sum((patch_starts[0][None, :] <= edges[:, None]).astype(jnp.int32), axis=1)
    first = jnp.minimum((counts - 1) // LANES, starts.shape[0] - WIN)
    far1 = [lax.ppermute(near1[0], "dp", swap)]
    incoming = after(incoming, first, far0, far1[0], chain)

    near1.append(lax.ppermute(after(near0, incoming)[CUT:], "tensor", pair))
    sums = collect(first, incoming, patch_rows)
    cross = lax.ppermute(sums, line, moves(lambda d, x: (0, x) if d == 1 else (1, ten_n - 1 - x)))
    third = lax.ppermute(sums, line, moves(lambda d, x: (1, ten_n - 1 - x) if d == 1 else None))
    other = lax.ppermute(after(chain, sums), "context", along(lambda i, j: (i, j ^ 1)))
    far1.append(lax.ppermute(after(near1[1], cross, third, other), "dp", swap))
    chain = jnp.stack([chain, other])
    other = lax.ppermute(chain, "context", along(lambda i, j: (i ^ 1, j)))
    columns = (near0, *near1, far0, *far1)
    partial, near = outer((sums, third, cross), columns)
    pieces = lax.all_to_all(partial, "context", split_axis=0, concat_axis=0, tiled=True)
    chain = jnp.stack([after(chain, partial), after(other, partial)])
    rest = lax.ppermute(chain, "context", along(lambda i, j: (SIDE - 1 - i, j)))

    far = lax.ppermute(near, "tensor", pair)
    piece = jnp.sum(pieces.astype(f32), axis=0).astype(bf16)
    parts = []
    for s in range(ten_n):
        parts.append(lax.ppermute(piece, line, moves(lambda d, x, s=s: (x // 2, (2 * d + x % 2) ^ s))))
    give = context_rows(1, after(near, parts[0]), far, chain, rest)
    back = lax.ppermute(give, "dp", swap)
    context_grad = context_rows(0, near, far, chain, rest, back)
    weight_grad = last(parts, both_t)
    return (context_grad[None], weight_grad)


def solution(mesh):
    placed = (
        P("dp", "context", None),
        P("dp", None),
        P("dp", None),
        P("dp", "context", "tensor"),
        P(None, "tensor"),
        P("tensor", None),
        P(),
    )
    return jax.shard_map(
        local,
        mesh=mesh,
        in_specs=placed,
        out_specs=(P("dp", "context", "tensor"), P(("dp", "context"), "tensor")),
        check_vma=False,
    )
```

```python
import functools

import jax
import jax.numpy as jnp
from jax import lax
from jax.experimental import pallas as pl
from jax.experimental.pallas import tpu as pltpu
from jax.sharding import PartitionSpec as P

LANES = 128
GROUP = 16
SUB = LANES // GROUP
WIN = 9
SLOT = WIN * SUB
SIDE = 4
CUT = 320
VMEM = 24 * 1024 * 1024
WIDE = 56 * 1024 * 1024


def seg_kernel(starts_ref, owner_ref, bytes_ref, out_ref, next_ref, low_ref, high_ref, acc_ref, turn_ref, held_ref, row_ref, sems):
    steps = sems.shape[0]
    shard, width = held_ref.shape
    block = shard // steps
    owners = LANES // SUB
    from_col = pl.ds(pl.multiple_of(lax.axis_index("tensor") * width, width), width)
    copies = []
    for k in range(steps):
        at = pl.ds(k * block, block)
        copies.append(pltpu.make_async_copy(bytes_ref.at[at, from_col], held_ref.at[at, :], sems.at[k]))
        copies[k].start()

    starts = starts_ref[...]
    rows = starts.shape[0]
    base = lax.axis_index("context") * shard
    for k in range(steps + 1):
        count = jnp.sum((starts <= base + k * block).astype(jnp.float32)).astype(jnp.int32)
        row_ref[k] = lax.shift_right_logical(count - 1, 7)
    first = jnp.minimum(row_ref[0], rows - WIN)
    lane = lax.broadcasted_iota(jnp.int32, starts.shape, 1)
    turned = pltpu.roll(starts, LANES - 1, 1)
    below = jnp.concatenate([turned[1:], jnp.full((1, LANES), 2**30, jnp.int32)], axis=0)
    next_ref[...] = jnp.where(lane == LANES - 1, below, turned)
    lane = lax.broadcasted_iota(jnp.int32, (SUB, LANES), 1)
    mine = lax.shift_right_logical(lane, 4) == lax.broadcasted_iota(jnp.int32, (SUB, LANES), 0)
    for t in range(WIN):
        low = jnp.clip(starts_ref[pl.ds(first + t, 1), :] - base, 0, shard).astype(jnp.float32)
        high = jnp.clip(next_ref[pl.ds(first + t, 1), :] - base, 0, shard).astype(jnp.float32)
        low = jnp.broadcast_to(low, (SUB, LANES))
        high = jnp.broadcast_to(high, (SUB, LANES))
        owner = jnp.broadcast_to(owner_ref[pl.ds(first + t, 1), :], (SUB, LANES))
        owner = jnp.where(mine, owner, -1)
        for j in range(owners):
            held = owner == j
            at = t * LANES + j * SUB
            one = jnp.sum(jnp.where(held, low, 0.0), axis=1, keepdims=True)
            low_ref[at : at + SUB, :] = jnp.broadcast_to(one, (SUB, LANES))
            one = jnp.sum(jnp.where(held, high, 0.0), axis=1, keepdims=True)
            high_ref[at : at + SUB, :] = jnp.broadcast_to(one, (SUB, LANES))
    acc_ref[...] = jnp.zeros_like(acc_ref)

    for k in range(steps):
        copies[k].wait()

        def one_row(t, carry, k=k):
            at = pl.ds(pl.multiple_of(t * LANES, LANES), LANES)
            low = low_ref[at, :]
            high = high_ref[at, :]
            parts = []
            for q in range(block // LANES):
                place = lax.broadcasted_iota(jnp.int32, (1, LANES), 1) + (k * block + q * LANES)
                place = place.astype(jnp.float32)
                parts.append(jnp.where((place >= low) & (place < high), 1.0, 0.0).astype(jnp.bfloat16))
            onehot = jnp.concatenate(parts, axis=1)
            acc_ref[at, :] += jnp.dot(
                onehot, held_ref[k * block : (k + 1) * block, :], preferred_element_type=jnp.float32
            )
            return carry

        lax.fori_loop(row_ref[k] - first, jnp.minimum(row_ref[k + 1] - first, WIN - 1) + 1, one_row, 0)

    for t in range(WIN):
        for j in range(owners):
            turn_ref[j * SLOT + t * SUB : j * SLOT + (t + 1) * SUB, :] = acc_ref[
                t * LANES + j * SUB : t * LANES + (j + 1) * SUB, :
            ]
    out_ref[...] = turn_ref[...].astype(jnp.bfloat16)


def segment_sums(starts, owner, grads, owners, width):
    steps = 8
    rows = owners * SLOT
    vmem = pl.BlockSpec(memory_space=pltpu.VMEM)
    return pl.pallas_call(
        seg_kernel,
        in_specs=[vmem, vmem, pl.BlockSpec(memory_space=pl.ANY)],
        out_shape=jax.ShapeDtypeStruct((rows, width), jnp.bfloat16),
        scratch_shapes=[
            pltpu.VMEM(starts.shape, jnp.int32),
            pltpu.VMEM((rows, LANES), jnp.float32),
            pltpu.VMEM((rows, LANES), jnp.float32),
            pltpu.VMEM((rows, width), jnp.float32),
            pltpu.VMEM((rows, width), jnp.float32),
            pltpu.VMEM((grads.shape[0], width), jnp.bfloat16),
            pltpu.SMEM((steps + 1,), jnp.int32),
            pltpu.SemaphoreType.DMA((steps,)),
        ],
        compiler_params=pltpu.CompilerParams(vmem_limit_bytes=WIDE),
    )(starts, owner, grads)


def collect_kernel(first_ref, in_ref, out_ref, wide_ref, acc_ref):
    wide_ref[...] = in_ref[...].astype(jnp.float32)
    acc_ref[...] = jnp.zeros_like(acc_ref)
    for s in range(in_ref.shape[0] // SLOT):
        at = pl.ds(pl.multiple_of(first_ref[s] * SUB, SUB), SLOT)
        acc_ref[at, :] += wide_ref[s * SLOT : (s + 1) * SLOT, :]
    out_ref[...] = acc_ref[...].T.astype(jnp.bfloat16)


def collect(first, incoming, patch_rows, interpret=False):
    rows, width = incoming.shape
    return pl.pallas_call(
        collect_kernel,
        in_specs=[pl.BlockSpec(memory_space=pltpu.SMEM), pl.BlockSpec(memory_space=pltpu.VMEM)],
        out_specs=pl.BlockSpec(memory_space=pltpu.VMEM),
        out_shape=jax.ShapeDtypeStruct((width, patch_rows), jnp.bfloat16),
        scratch_shapes=[pltpu.VMEM((rows, width), jnp.float32), pltpu.VMEM((patch_rows, width), jnp.float32)],
        compiler_params=pltpu.CompilerParams(vmem_limit_bytes=VMEM),
        interpret=interpret,
    )(first, incoming)


def outer_kernel(mine_ref, third_ref, cross_ref, n0_ref, n1a_ref, n1b_ref, f0_ref, f1a_ref, f1b_ref, out_ref, both_ref, cols_ref, held_ref, in_sems, sems):
    cut, cols = n1a_ref.shape
    rows = n0_ref.shape[0]
    arrivals = []
    for k, (ref, to, low, high) in enumerate((
        (n0_ref, 0, 0, rows),
        (f0_ref, 1, 0, rows),
        (n1a_ref, 2, 0, cut),
        (n1b_ref, 2, cut, rows),
        (f1a_ref, 3, 0, cut),
        (f1b_ref, 3, cut, rows),
    )):
        arrivals.append(pltpu.make_async_copy(ref, cols_ref.at[to, pl.ds(low, high - low)], in_sems.at[k]))
        arrivals[k].start()
    near_t = jnp.where(lax.axis_index("dp") == 0, mine_ref[...], third_ref[...])
    far_t = cross_ref[...]
    both_ref[0] = near_t
    both_ref[1] = far_t
    low = lax.rem(lax.axis_index("tensor"), 2)
    blocks = out_ref.shape[0] // 2
    wide = 256
    per = wide // LANES
    copies = []
    for k, which in ((0, low), (1, 1 - low)):
        for arrival in arrivals[:2] if k == 0 else arrivals[2:]:
            arrival.wait()
        for i in range(cols // wide):
            at = slice(i * wide, (i + 1) * wide)
            total = jnp.dot(near_t, cols_ref[2 * k, :, at], preferred_element_type=jnp.float32)
            total += jnp.dot(far_t, cols_ref[2 * k + 1, :, at], preferred_element_type=jnp.float32)
            total = total.astype(jnp.bfloat16)
            here = k * blocks + i * per
            for j in range(per):
                held_ref[here + j] = total[:, j * LANES : (j + 1) * LANES]
            copy = pltpu.make_async_copy(
                held_ref.at[pl.ds(here, per)],
                out_ref.at[pl.ds(which * blocks + i * per, per)],
                sems.at[2 * i + k],
            )
            copy.start()
            copies.append(copy)
    for copy in copies:
        copy.wait()


def outer(sums, columns):
    width, rows = sums[0].shape
    cols = columns[0].shape[1]
    vmem = pl.BlockSpec(memory_space=pltpu.VMEM)
    shape = (2 * cols // LANES, width, LANES)
    return pl.pallas_call(
        outer_kernel,
        in_specs=[vmem] * len(sums) + [pl.BlockSpec(memory_space=pl.ANY)] * len(columns),
        out_specs=[pl.BlockSpec(memory_space=pltpu.HBM), vmem],
        out_shape=[
            jax.ShapeDtypeStruct(shape, jnp.bfloat16),
            jax.ShapeDtypeStruct((2, width, rows), jnp.bfloat16),
        ],
        scratch_shapes=[
            pltpu.VMEM((4, rows, cols), jnp.bfloat16),
            pltpu.VMEM(shape, jnp.bfloat16),
            pltpu.SemaphoreType.DMA((len(columns),)),
            pltpu.SemaphoreType.DMA((2 * cols // 256,)),
        ],
        compiler_params=pltpu.CompilerParams(vmem_limit_bytes=62 * 1024 * 1024),
    )(*sums, *columns)


def eighth():
    ctx = lax.axis_index("context")
    return 2 * lax.div(ctx, SIDE) + lax.rem(ctx, 2)


def flip(a, b):
    return a + b - 2 * b * lax.rem(a, 2)


def chain_kernel(value_ref, out_w_ref, global_ref, both_ref, own_ref, pair_ref, away_ref, held_ref, sems):
    rows, wide = own_ref.shape
    dp, ten = lax.axis_index("dp"), lax.axis_index("tensor")
    targets = (ten, flip(ten, 1), 3 - ten, flip(3 - ten, 1))
    copies = []
    for s, target in enumerate(targets):
        at = (target * 8 + eighth()) * rows
        copy = pltpu.make_async_copy(global_ref.at[pl.ds(pl.multiple_of(at, rows), rows)], held_ref.at[s], sems.at[s])
        copy.start()
        copies.append(copy)
    both_ref[...] = jnp.dot(
        value_ref[...], out_w_ref[...], preferred_element_type=jnp.float32
    ).astype(jnp.bfloat16)
    for s in range(0, 4, 2):
        copies[s].wait()
        copies[s + 1].wait()
        half = flip(dp, lax.div(targets[s], 2))
        cols = pl.ds(pl.multiple_of(half * wide, wide), wide)
        left = jnp.concatenate([held_ref[s], held_ref[s + 1]], axis=0)
        total = jnp.dot(left, both_ref[:, cols], preferred_element_type=jnp.float32).astype(jnp.bfloat16)
        if s == 0:
            own_ref[...] = total[:rows]
            pair_ref[...] = total[rows:]
        else:
            away_ref[0] = total[:rows]
            away_ref[1] = total[rows:]


def chain_terms(w_value, w_out, w_global):
    deep, feats = w_value.shape
    rows = w_global.shape[0] // 32
    vmem = pl.BlockSpec(memory_space=pltpu.VMEM)
    part = jax.ShapeDtypeStruct((rows, feats // 2), jnp.bfloat16)
    return pl.pallas_call(
        chain_kernel,
        in_specs=[vmem, vmem, pl.BlockSpec(memory_space=pl.ANY)],
        out_specs=[vmem] * 4,
        out_shape=[
            jax.ShapeDtypeStruct((deep, feats), jnp.bfloat16),
            part,
            part,
            jax.ShapeDtypeStruct((2, rows, feats // 2), jnp.bfloat16),
        ],
        scratch_shapes=[pltpu.VMEM((4, rows, deep), jnp.bfloat16), pltpu.SemaphoreType.DMA((4,))],
        compiler_params=pltpu.CompilerParams(vmem_limit_bytes=WIDE),
    )(w_value, w_out, w_global)


def rows_kernel(which, near_ref, far_ref, low_ref, high_ref, *rest):
    out_ref, table_ref = rest[-2:]
    deep = near_ref.shape[1]
    rows = low_ref.shape[2]
    z, y = lax.div(eighth(), 2), lax.rem(eighth(), 2)
    for ref, base in ((low_ref, z), (high_ref, SIDE - 1 - z)):
        for i in range(2):
            for j in range(2):
                to = 2 * flip(base, i) + flip(y, j)
                table_ref[pl.ds(pl.multiple_of(to * rows, rows), rows), :] = ref[i, j]
    odd = lax.rem(lax.axis_index("tensor") + lax.axis_index("dp"), 2)
    dims = (((1,), (1,)), ((), ()))
    first = table_ref[:, pl.ds(pl.multiple_of(odd * deep, deep), deep)]
    second = table_ref[:, pl.ds(pl.multiple_of((1 - odd) * deep, deep), deep)]
    total = lax.dot_general(near_ref[which].T, first, dims, preferred_element_type=jnp.float32)
    total += lax.dot_general(far_ref[which].T, second, dims, preferred_element_type=jnp.float32)
    if len(rest) > 2:
        total += rest[0][...].astype(jnp.float32)
    out_ref[...] = total.astype(jnp.bfloat16)


def context_rows(which, near, far, low, high, *back):
    vmem = pl.BlockSpec(memory_space=pltpu.VMEM)
    cols, half = 8 * low.shape[2], low.shape[3]
    return pl.pallas_call(
        functools.partial(rows_kernel, which),
        in_specs=[vmem] * (4 + len(back)),
        out_specs=vmem,
        out_shape=jax.ShapeDtypeStruct((near.shape[2], cols), jnp.bfloat16),
        scratch_shapes=[pltpu.VMEM((cols, half), jnp.bfloat16)],
        compiler_params=pltpu.CompilerParams(vmem_limit_bytes=VMEM),
    )(near, far, low, high, *back)


def last_kernel(a_ref, b_ref, c_ref, d_ref, w_ref, out_ref):
    width = a_ref.shape[0]
    dp, ten = lax.axis_index("dp"), lax.axis_index("tensor")
    total = jnp.zeros(out_ref.shape, jnp.float32)
    for s, ref in enumerate((a_ref, b_ref, c_ref, d_ref)):
        source = lax.bitwise_xor(ten, s)
        near = 2 * dp + lax.rem(source, 2)
        at = jnp.where(source < 2, near, 3 - near)
        total += lax.dot_general(
            ref[...].T,
            w_ref[:, pl.ds(pl.multiple_of(at * width, width), width)],
            (((1,), (1,)), ((), ())),
            preferred_element_type=jnp.float32,
        )
    out_ref[...] = total


def last(pieces, weights):
    vmem = pl.BlockSpec(memory_space=pltpu.VMEM)
    return pl.pallas_call(
        last_kernel,
        in_specs=[vmem] * (len(pieces) + 1),
        out_shape=jax.ShapeDtypeStruct((pieces[0].shape[1], weights.shape[0]), jnp.float32),
        compiler_params=pltpu.CompilerParams(vmem_limit_bytes=VMEM),
    )(*pieces, weights)


def after(value, *others):
    return lax.optimization_barrier((value, *others))[0]


def local(byte_grads, patch_starts, patch_owner, attn_context, w_global, w_value, w_out):
    dp_n, ctx_n, ten_n = (lax.axis_size(a) for a in ("dp", "context", "tensor"))
    f32, bf16 = jnp.float32, jnp.bfloat16
    bytes_n, feats = byte_grads.shape[1:]
    width = feats // ten_n
    patch_rows = attn_context.shape[1]
    starts = patch_starts.reshape(-1, LANES)
    owner = patch_owner.reshape(-1, LANES)
    line = ("dp", "tensor")

    def moves(target):
        pairs = []
        for d in range(dp_n):
            for x in range(ten_n):
                to = target(d, x)
                if to is not None:
                    pairs.append((d * ten_n + x, to[0] * ten_n + to[1]))
        return pairs

    swap = [(i, dp_n - 1 - i) for i in range(dp_n)]
    pair = [(x, x ^ 1) for x in range(ten_n)]
    near0 = attn_context[0]
    far0 = lax.ppermute(near0, "dp", swap)
    near1 = [lax.ppermute(near0[:CUT], "tensor", pair)]

    def along(target):
        return [
            (i * SIDE + j, target(i, j)[0] * SIDE + target(i, j)[1]) for i in range(SIDE) for j in range(SIDE)
        ]

    both_t, own, paired, away = chain_terms(w_value, w_out, w_global)
    away = lax.ppermute(away, "tensor", [(x, ten_n - 1 - x) for x in range(ten_n)])

    outgoing = segment_sums(after(starts, both_t), owner, byte_grads[0], ctx_n, width)
    outgoing = after(outgoing, near1[0], away)
    incoming = lax.all_to_all(outgoing, "context", split_axis=0, concat_axis=0, tiled=True)

    away = after(away, outgoing)
    paired = (paired.astype(f32) + away[1].astype(f32)).astype(bf16)
    paired = lax.ppermute(paired, "tensor", pair)
    chain = (own.astype(f32) + away[0].astype(f32) + paired.astype(f32)).astype(bf16)
    edges = jnp.arange(ctx_n, dtype=jnp.int32) * bytes_n
    counts = jnp.sum((patch_starts[0][None, :] <= edges[:, None]).astype(jnp.int32), axis=1)
    first = jnp.minimum((counts - 1) // LANES, starts.shape[0] - WIN)
    far1 = [lax.ppermute(near1[0], "dp", swap)]
    incoming = after(incoming, first, far0, far1[0], chain)

    near1.append(lax.ppermute(after(near0, incoming)[CUT:], "tensor", pair))
    sums = collect(first, incoming, patch_rows)
    cross = lax.ppermute(sums, line, moves(lambda d, x: (0, x) if d == 1 else (1, ten_n - 1 - x)))
    third = lax.ppermute(sums, line, moves(lambda d, x: (1, ten_n - 1 - x) if d == 1 else None))
    other = lax.ppermute(after(chain, sums), "context", along(lambda i, j: (i, j ^ 1)))
    far1.append(lax.ppermute(after(near1[1], cross, third, other), "dp", swap))
    chain = jnp.stack([chain, other])
    other = lax.ppermute(chain, "context", along(lambda i, j: (i ^ 1, j)))
    columns = (near0, *near1, far0, *far1)
    partial, near = outer((after(sums, other), third, cross), columns)
    pieces = lax.all_to_all(partial, "context", split_axis=0, concat_axis=0, tiled=True)
    chain = jnp.stack([after(chain, partial), after(other, partial)])
    rest = lax.ppermute(chain, "context", along(lambda i, j: (SIDE - 1 - i, j)))

    far = lax.ppermute(near, "tensor", pair)
    piece = jnp.sum(pieces.astype(f32), axis=0).astype(bf16)
    parts = []
    for s in range(ten_n):
        parts.append(lax.ppermute(piece, line, moves(lambda d, x, s=s: (x // 2, (2 * d + x % 2) ^ s))))
    give = context_rows(1, after(near, *parts), far, chain, rest)
    back = lax.ppermute(give, "dp", swap)
    context_grad = context_rows(0, near, far, chain, rest, back)
    weight_grad = last(parts, both_t)
    return (context_grad[None], weight_grad)


def solution(mesh):
    placed = (
        P("dp", "context", None),
        P("dp", None),
        P("dp", None),
        P("dp", "context", "tensor"),
        P(None, "tensor"),
        P("tensor", None),
        P(),
    )
    return jax.shard_map(
        local,
        mesh=mesh,
        in_specs=placed,
        out_specs=(P("dp", "context", "tensor"), P(("dp", "context"), "tensor")),
        check_vma=False,
    )
```

```python
import functools

import jax
import jax.numpy as jnp
from jax import lax
from jax.experimental import pallas as pl
from jax.experimental.pallas import tpu as pltpu
from jax.sharding import PartitionSpec as P

LANES = 128
GROUP = 16
SUB = LANES // GROUP
WIN = 9
SLOT = WIN * SUB
SIDE = 4
CUT = 320
VMEM = 24 * 1024 * 1024
WIDE = 56 * 1024 * 1024


def seg_kernel(starts_ref, owner_ref, bytes_ref, out_ref, next_ref, low_ref, high_ref, acc_ref, turn_ref, held_ref, row_ref, sems):
    steps = sems.shape[0]
    shard, width = held_ref.shape
    block = shard // steps
    owners = LANES // SUB
    from_col = pl.ds(pl.multiple_of(lax.axis_index("tensor") * width, width), width)
    copies = []
    for k in range(steps):
        at = pl.ds(k * block, block)
        copies.append(pltpu.make_async_copy(bytes_ref.at[at, from_col], held_ref.at[at, :], sems.at[k]))
        copies[k].start()

    starts = starts_ref[...]
    rows = starts.shape[0]
    base = lax.axis_index("context") * shard
    for k in range(steps + 1):
        count = jnp.sum((starts <= base + k * block).astype(jnp.float32)).astype(jnp.int32)
        row_ref[k] = lax.shift_right_logical(count - 1, 7)
    first = jnp.minimum(row_ref[0], rows - WIN)
    lane = lax.broadcasted_iota(jnp.int32, starts.shape, 1)
    turned = pltpu.roll(starts, LANES - 1, 1)
    below = jnp.concatenate([turned[1:], jnp.full((1, LANES), 2**30, jnp.int32)], axis=0)
    next_ref[...] = jnp.where(lane == LANES - 1, below, turned)
    lane = lax.broadcasted_iota(jnp.int32, (SUB, LANES), 1)
    mine = lax.shift_right_logical(lane, 4) == lax.broadcasted_iota(jnp.int32, (SUB, LANES), 0)
    for t in range(WIN):
        low = jnp.clip(starts_ref[pl.ds(first + t, 1), :] - base, 0, shard).astype(jnp.float32)
        high = jnp.clip(next_ref[pl.ds(first + t, 1), :] - base, 0, shard).astype(jnp.float32)
        low = jnp.broadcast_to(low, (SUB, LANES))
        high = jnp.broadcast_to(high, (SUB, LANES))
        owner = jnp.broadcast_to(owner_ref[pl.ds(first + t, 1), :], (SUB, LANES))
        owner = jnp.where(mine, owner, -1)
        for j in range(owners):
            held = owner == j
            at = t * LANES + j * SUB
            one = jnp.sum(jnp.where(held, low, 0.0), axis=1, keepdims=True)
            low_ref[at : at + SUB, :] = jnp.broadcast_to(one, (SUB, LANES))
            one = jnp.sum(jnp.where(held, high, 0.0), axis=1, keepdims=True)
            high_ref[at : at + SUB, :] = jnp.broadcast_to(one, (SUB, LANES))
    acc_ref[...] = jnp.zeros_like(acc_ref)

    for k in range(steps):
        copies[k].wait()

        def one_row(t, carry, k=k):
            at = pl.ds(pl.multiple_of(t * LANES, LANES), LANES)
            low = low_ref[at, :]
            high = high_ref[at, :]
            parts = []
            for q in range(block // LANES):
                place = lax.broadcasted_iota(jnp.int32, (1, LANES), 1) + (k * block + q * LANES)
                place = place.astype(jnp.float32)
                parts.append(jnp.where((place >= low) & (place < high), 1.0, 0.0).astype(jnp.bfloat16))
            onehot = jnp.concatenate(parts, axis=1)
            acc_ref[at, :] += jnp.dot(
                onehot, held_ref[k * block : (k + 1) * block, :], preferred_element_type=jnp.float32
            )
            return carry

        lax.fori_loop(row_ref[k] - first, jnp.minimum(row_ref[k + 1] - first, WIN - 1) + 1, one_row, 0)

    for t in range(WIN):
        for j in range(owners):
            turn_ref[j * SLOT + t * SUB : j * SLOT + (t + 1) * SUB, :] = acc_ref[
                t * LANES + j * SUB : t * LANES + (j + 1) * SUB, :
            ]
    out_ref[...] = turn_ref[...].astype(jnp.bfloat16)


def segment_sums(starts, owner, grads, owners, width):
    steps = 8
    rows = owners * SLOT
    vmem = pl.BlockSpec(memory_space=pltpu.VMEM)
    return pl.pallas_call(
        seg_kernel,
        in_specs=[vmem, vmem, pl.BlockSpec(memory_space=pl.ANY)],
        out_shape=jax.ShapeDtypeStruct((rows, width), jnp.bfloat16),
        scratch_shapes=[
            pltpu.VMEM(starts.shape, jnp.int32),
            pltpu.VMEM((rows, LANES), jnp.float32),
            pltpu.VMEM((rows, LANES), jnp.float32),
            pltpu.VMEM((rows, width), jnp.float32),
            pltpu.VMEM((rows, width), jnp.float32),
            pltpu.VMEM((grads.shape[0], width), jnp.bfloat16),
            pltpu.SMEM((steps + 1,), jnp.int32),
            pltpu.SemaphoreType.DMA((steps,)),
        ],
        compiler_params=pltpu.CompilerParams(vmem_limit_bytes=WIDE),
    )(starts, owner, grads)


def collect_kernel(first_ref, in_ref, out_ref, wide_ref, acc_ref):
    wide_ref[...] = in_ref[...].astype(jnp.float32)
    acc_ref[...] = jnp.zeros_like(acc_ref)
    for s in range(in_ref.shape[0] // SLOT):
        at = pl.ds(pl.multiple_of(first_ref[s] * SUB, SUB), SLOT)
        acc_ref[at, :] += wide_ref[s * SLOT : (s + 1) * SLOT, :]
    out_ref[...] = acc_ref[...].T.astype(jnp.bfloat16)


def collect(first, incoming, patch_rows, interpret=False):
    rows, width = incoming.shape
    return pl.pallas_call(
        collect_kernel,
        in_specs=[pl.BlockSpec(memory_space=pltpu.SMEM), pl.BlockSpec(memory_space=pltpu.VMEM)],
        out_specs=pl.BlockSpec(memory_space=pltpu.VMEM),
        out_shape=jax.ShapeDtypeStruct((width, patch_rows), jnp.bfloat16),
        scratch_shapes=[pltpu.VMEM((rows, width), jnp.float32), pltpu.VMEM((patch_rows, width), jnp.float32)],
        compiler_params=pltpu.CompilerParams(vmem_limit_bytes=VMEM),
        interpret=interpret,
    )(first, incoming)


def outer_kernel(mine_ref, third_ref, cross_ref, n0_ref, n1a_ref, n1b_ref, f0_ref, f1a_ref, f1b_ref, out_ref, both_ref, cols_ref, held_ref, in_sems, sems):
    cut, cols = n1a_ref.shape
    rows = n0_ref.shape[0]
    arrivals = []
    for k, (ref, to, low, high) in enumerate((
        (n0_ref, 0, 0, rows),
        (f0_ref, 1, 0, rows),
        (n1a_ref, 2, 0, cut),
        (n1b_ref, 2, cut, rows),
        (f1a_ref, 3, 0, cut),
        (f1b_ref, 3, cut, rows),
    )):
        arrivals.append(pltpu.make_async_copy(ref, cols_ref.at[to, pl.ds(low, high - low)], in_sems.at[k]))
        arrivals[k].start()
    near_t = jnp.where(lax.axis_index("dp") == 0, mine_ref[...], third_ref[...])
    far_t = cross_ref[...]
    both_ref[0] = near_t
    both_ref[1] = far_t
    low = lax.rem(lax.axis_index("tensor"), 2)
    blocks = out_ref.shape[0] // 2
    wide = 256
    per = wide // LANES
    copies = []
    for k, which in ((0, low), (1, 1 - low)):
        for arrival in arrivals[:2] if k == 0 else arrivals[2:]:
            arrival.wait()
        for i in range(cols // wide):
            at = slice(i * wide, (i + 1) * wide)
            total = jnp.dot(near_t, cols_ref[2 * k, :, at], preferred_element_type=jnp.float32)
            total += jnp.dot(far_t, cols_ref[2 * k + 1, :, at], preferred_element_type=jnp.float32)
            total = total.astype(jnp.bfloat16)
            here = k * blocks + i * per
            for j in range(per):
                held_ref[here + j] = total[:, j * LANES : (j + 1) * LANES]
            copy = pltpu.make_async_copy(
                held_ref.at[pl.ds(here, per)],
                out_ref.at[pl.ds(which * blocks + i * per, per)],
                sems.at[2 * i + k],
            )
            copy.start()
            copies.append(copy)
    for copy in copies:
        copy.wait()


def outer(sums, columns):
    width, rows = sums[0].shape
    cols = columns[0].shape[1]
    vmem = pl.BlockSpec(memory_space=pltpu.VMEM)
    shape = (2 * cols // LANES, width, LANES)
    return pl.pallas_call(
        outer_kernel,
        in_specs=[vmem] * len(sums) + [pl.BlockSpec(memory_space=pl.ANY)] * len(columns),
        out_specs=[pl.BlockSpec(memory_space=pltpu.HBM), vmem],
        out_shape=[
            jax.ShapeDtypeStruct(shape, jnp.bfloat16),
            jax.ShapeDtypeStruct((2, width, rows), jnp.bfloat16),
        ],
        scratch_shapes=[
            pltpu.VMEM((4, rows, cols), jnp.bfloat16),
            pltpu.VMEM(shape, jnp.bfloat16),
            pltpu.SemaphoreType.DMA((len(columns),)),
            pltpu.SemaphoreType.DMA((2 * cols // 256,)),
        ],
        compiler_params=pltpu.CompilerParams(vmem_limit_bytes=62 * 1024 * 1024),
    )(*sums, *columns)


def eighth():
    ctx = lax.axis_index("context")
    return 2 * lax.div(ctx, SIDE) + lax.rem(ctx, 2)


def flip(a, b):
    return a + b - 2 * b * lax.rem(a, 2)


def chain_kernel(value_ref, out_w_ref, global_ref, both_ref, own_ref, pair_ref, away_ref, held_ref, sems):
    rows, wide = own_ref.shape
    dp, ten = lax.axis_index("dp"), lax.axis_index("tensor")
    targets = (ten, flip(ten, 1), 3 - ten, flip(3 - ten, 1))
    copies = []
    for s, target in enumerate(targets):
        at = (target * 8 + eighth()) * rows
        copy = pltpu.make_async_copy(global_ref.at[pl.ds(pl.multiple_of(at, rows), rows)], held_ref.at[s], sems.at[s])
        copy.start()
        copies.append(copy)
    both_ref[...] = jnp.dot(
        value_ref[...], out_w_ref[...], preferred_element_type=jnp.float32
    ).astype(jnp.bfloat16)
    for s in range(0, 4, 2):
        copies[s].wait()
        copies[s + 1].wait()
        half = flip(dp, lax.div(targets[s], 2))
        cols = pl.ds(pl.multiple_of(half * wide, wide), wide)
        left = jnp.concatenate([held_ref[s], held_ref[s + 1]], axis=0)
        total = jnp.dot(left, both_ref[:, cols], preferred_element_type=jnp.float32).astype(jnp.bfloat16)
        if s == 0:
            own_ref[...] = total[:rows]
            pair_ref[...] = total[rows:]
        else:
            away_ref[0] = total[:rows]
            away_ref[1] = total[rows:]


def chain_terms(w_value, w_out, w_global):
    deep, feats = w_value.shape
    rows = w_global.shape[0] // 32
    vmem = pl.BlockSpec(memory_space=pltpu.VMEM)
    part = jax.ShapeDtypeStruct((rows, feats // 2), jnp.bfloat16)
    return pl.pallas_call(
        chain_kernel,
        in_specs=[vmem, vmem, pl.BlockSpec(memory_space=pl.ANY)],
        out_specs=[vmem] * 4,
        out_shape=[
            jax.ShapeDtypeStruct((deep, feats), jnp.bfloat16),
            part,
            part,
            jax.ShapeDtypeStruct((2, rows, feats // 2), jnp.bfloat16),
        ],
        scratch_shapes=[pltpu.VMEM((4, rows, deep), jnp.bfloat16), pltpu.SemaphoreType.DMA((4,))],
        compiler_params=pltpu.CompilerParams(vmem_limit_bytes=WIDE),
    )(w_value, w_out, w_global)


def rows_kernel(which, near_ref, far_ref, low_ref, high_ref, *rest):
    out_ref, table_ref = rest[-2:]
    deep = near_ref.shape[1]
    rows = low_ref.shape[2]
    z, y = lax.div(eighth(), 2), lax.rem(eighth(), 2)
    for ref, base in ((low_ref, z), (high_ref, SIDE - 1 - z)):
        for i in range(2):
            for j in range(2):
                to = 2 * flip(base, i) + flip(y, j)
                table_ref[pl.ds(pl.multiple_of(to * rows, rows), rows), :] = ref[i, j]
    odd = lax.rem(lax.axis_index("tensor") + lax.axis_index("dp"), 2)
    dims = (((1,), (1,)), ((), ()))
    first = table_ref[:, pl.ds(pl.multiple_of(odd * deep, deep), deep)]
    second = table_ref[:, pl.ds(pl.multiple_of((1 - odd) * deep, deep), deep)]
    total = lax.dot_general(near_ref[which].T, first, dims, preferred_element_type=jnp.float32)
    total += lax.dot_general(far_ref[which].T, second, dims, preferred_element_type=jnp.float32)
    if len(rest) > 2:
        total += rest[0][...].astype(jnp.float32)
    out_ref[...] = total.astype(jnp.bfloat16)


def context_rows(which, near, far, low, high, *back):
    vmem = pl.BlockSpec(memory_space=pltpu.VMEM)
    cols, half = 8 * low.shape[2], low.shape[3]
    return pl.pallas_call(
        functools.partial(rows_kernel, which),
        in_specs=[vmem] * (4 + len(back)),
        out_specs=vmem,
        out_shape=jax.ShapeDtypeStruct((near.shape[2], cols), jnp.bfloat16),
        scratch_shapes=[pltpu.VMEM((cols, half), jnp.bfloat16)],
        compiler_params=pltpu.CompilerParams(vmem_limit_bytes=VMEM),
    )(near, far, low, high, *back)


def last_kernel(a_ref, b_ref, c_ref, d_ref, w_ref, out_ref):
    width = a_ref.shape[0]
    dp, ten = lax.axis_index("dp"), lax.axis_index("tensor")
    total = jnp.zeros(out_ref.shape, jnp.float32)
    for s, ref in enumerate((a_ref, b_ref, c_ref, d_ref)):
        source = lax.bitwise_xor(ten, s)
        near = 2 * dp + lax.rem(source, 2)
        at = jnp.where(source < 2, near, 3 - near)
        total += lax.dot_general(
            ref[...].T,
            w_ref[:, pl.ds(pl.multiple_of(at * width, width), width)],
            (((1,), (1,)), ((), ())),
            preferred_element_type=jnp.float32,
        )
    out_ref[...] = total


def last(pieces, weights):
    vmem = pl.BlockSpec(memory_space=pltpu.VMEM)
    return pl.pallas_call(
        last_kernel,
        in_specs=[vmem] * (len(pieces) + 1),
        out_shape=jax.ShapeDtypeStruct((pieces[0].shape[1], weights.shape[0]), jnp.float32),
        compiler_params=pltpu.CompilerParams(vmem_limit_bytes=VMEM),
    )(*pieces, weights)


def after(value, *others):
    return lax.optimization_barrier((value, *others))[0]


def local(byte_grads, patch_starts, patch_owner, attn_context, w_global, w_value, w_out):
    dp_n, ctx_n, ten_n = (lax.axis_size(a) for a in ("dp", "context", "tensor"))
    f32, bf16 = jnp.float32, jnp.bfloat16
    bytes_n, feats = byte_grads.shape[1:]
    width = feats // ten_n
    patch_rows = attn_context.shape[1]
    starts = patch_starts.reshape(-1, LANES)
    owner = patch_owner.reshape(-1, LANES)
    line = ("dp", "tensor")

    def moves(target):
        pairs = []
        for d in range(dp_n):
            for x in range(ten_n):
                to = target(d, x)
                if to is not None:
                    pairs.append((d * ten_n + x, to[0] * ten_n + to[1]))
        return pairs

    swap = [(i, dp_n - 1 - i) for i in range(dp_n)]
    pair = [(x, x ^ 1) for x in range(ten_n)]
    near0 = attn_context[0]
    far0 = lax.ppermute(near0, "dp", swap)
    near1 = [lax.ppermute(near0[:CUT], "tensor", pair)]

    def along(target):
        return [
            (i * SIDE + j, target(i, j)[0] * SIDE + target(i, j)[1]) for i in range(SIDE) for j in range(SIDE)
        ]

    both_t, own, paired, away = chain_terms(w_value, w_out, w_global)
    away = lax.ppermute(away, "tensor", [(x, ten_n - 1 - x) for x in range(ten_n)])

    outgoing = segment_sums(after(starts, both_t), owner, byte_grads[0], ctx_n, width)
    outgoing = after(outgoing, near1[0], away)
    incoming = lax.all_to_all(outgoing, "context", split_axis=0, concat_axis=0, tiled=True)

    away = after(away, outgoing)
    paired = (paired.astype(f32) + away[1].astype(f32)).astype(bf16)
    paired = lax.ppermute(paired, "tensor", pair)
    chain = (own.astype(f32) + away[0].astype(f32) + paired.astype(f32)).astype(bf16)
    chain = jnp.stack([chain, lax.ppermute(chain, "context", along(lambda i, j: (i, j ^ 1)))])
    edges = jnp.arange(ctx_n, dtype=jnp.int32) * bytes_n
    counts = jnp.sum((patch_starts[0][None, :] <= edges[:, None]).astype(jnp.int32), axis=1)
    first = jnp.minimum((counts - 1) // LANES, starts.shape[0] - WIN)
    far1 = [lax.ppermute(near1[0], "dp", swap)]
    incoming = after(incoming, first, far0, far1[0], chain)

    near1.append(lax.ppermute(after(near0, incoming)[CUT:], "tensor", pair))
    sums = collect(first, incoming, patch_rows)
    cross = lax.ppermute(sums, line, moves(lambda d, x: (0, x) if d == 1 else (1, ten_n - 1 - x)))
    third = lax.ppermute(sums, line, moves(lambda d, x: (1, ten_n - 1 - x) if d == 1 else None))
    other = lax.ppermute(after(chain, sums), "context", along(lambda i, j: (i ^ 1, j)))
    far1.append(lax.ppermute(after(near1[1], cross, third, other), "dp", swap))
    columns = (near0, *near1, far0, *far1)
    partial, near = outer((sums, third, cross), columns)
    pieces = lax.all_to_all(partial, "context", split_axis=0, concat_axis=0, tiled=True)
    chain = jnp.stack([after(chain, partial), after(other, partial)])
    rest = lax.ppermute(chain, "context", along(lambda i, j: (SIDE - 1 - i, j)))

    far = lax.ppermute(near, "tensor", pair)
    piece = jnp.sum(pieces.astype(f32), axis=0).astype(bf16)
    parts = []
    for s in range(ten_n):
        parts.append(lax.ppermute(piece, line, moves(lambda d, x, s=s: (x // 2, (2 * d + x % 2) ^ s))))
    give = context_rows(1, after(near, *parts), far, chain, rest)
    back = lax.ppermute(give, "dp", swap)
    context_grad = context_rows(0, near, far, chain, rest, back)
    weight_grad = last(parts, both_t)
    return (context_grad[None], weight_grad)


def solution(mesh):
    placed = (
        P("dp", "context", None),
        P("dp", None),
        P("dp", None),
        P("dp", "context", "tensor"),
        P(None, "tensor"),
        P("tensor", None),
        P(),
    )
    return jax.shard_map(
        local,
        mesh=mesh,
        in_specs=placed,
        out_specs=(P("dp", "context", "tensor"), P(("dp", "context"), "tensor")),
        check_vma=False,
    )
```

```python
import functools

import jax
import jax.numpy as jnp
from jax import lax
from jax.experimental import pallas as pl
from jax.experimental.pallas import tpu as pltpu
from jax.sharding import PartitionSpec as P

LANES = 128
GROUP = 16
SUB = LANES // GROUP
WIN = 9
SLOT = WIN * SUB
SIDE = 4
CUT = 320
VMEM = 24 * 1024 * 1024
WIDE = 56 * 1024 * 1024


def seg_kernel(starts_ref, owner_ref, bytes_ref, out_ref, next_ref, low_ref, high_ref, acc_ref, turn_ref, held_ref, row_ref, sems):
    steps = sems.shape[0]
    shard, width = held_ref.shape
    block = shard // steps
    owners = LANES // SUB
    from_col = pl.ds(pl.multiple_of(lax.axis_index("tensor") * width, width), width)
    copies = []
    for k in range(steps):
        at = pl.ds(k * block, block)
        copies.append(pltpu.make_async_copy(bytes_ref.at[at, from_col], held_ref.at[at, :], sems.at[k]))
        copies[k].start()

    starts = starts_ref[...]
    rows = starts.shape[0]
    base = lax.axis_index("context") * shard
    for k in range(steps + 1):
        count = jnp.sum((starts <= base + k * block).astype(jnp.float32)).astype(jnp.int32)
        row_ref[k] = lax.shift_right_logical(count - 1, 7)
    first = jnp.minimum(row_ref[0], rows - WIN)
    lane = lax.broadcasted_iota(jnp.int32, starts.shape, 1)
    turned = pltpu.roll(starts, LANES - 1, 1)
    below = jnp.concatenate([turned[1:], jnp.full((1, LANES), 2**30, jnp.int32)], axis=0)
    next_ref[...] = jnp.where(lane == LANES - 1, below, turned)
    lane = lax.broadcasted_iota(jnp.int32, (SUB, LANES), 1)
    mine = lax.shift_right_logical(lane, 4) == lax.broadcasted_iota(jnp.int32, (SUB, LANES), 0)
    for t in range(WIN):
        low = jnp.clip(starts_ref[pl.ds(first + t, 1), :] - base, 0, shard).astype(jnp.float32)
        high = jnp.clip(next_ref[pl.ds(first + t, 1), :] - base, 0, shard).astype(jnp.float32)
        low = jnp.broadcast_to(low, (SUB, LANES))
        high = jnp.broadcast_to(high, (SUB, LANES))
        owner = jnp.broadcast_to(owner_ref[pl.ds(first + t, 1), :], (SUB, LANES))
        owner = jnp.where(mine, owner, -1)
        for j in range(owners):
            held = owner == j
            at = t * LANES + j * SUB
            one = jnp.sum(jnp.where(held, low, 0.0), axis=1, keepdims=True)
            low_ref[at : at + SUB, :] = jnp.broadcast_to(one, (SUB, LANES))
            one = jnp.sum(jnp.where(held, high, 0.0), axis=1, keepdims=True)
            high_ref[at : at + SUB, :] = jnp.broadcast_to(one, (SUB, LANES))
    acc_ref[...] = jnp.zeros_like(acc_ref)

    for k in range(steps):
        copies[k].wait()

        def one_row(t, carry, k=k):
            at = pl.ds(pl.multiple_of(t * LANES, LANES), LANES)
            low = low_ref[at, :]
            high = high_ref[at, :]
            parts = []
            for q in range(block // LANES):
                place = lax.broadcasted_iota(jnp.int32, (1, LANES), 1) + (k * block + q * LANES)
                place = place.astype(jnp.float32)
                parts.append(jnp.where((place >= low) & (place < high), 1.0, 0.0).astype(jnp.bfloat16))
            onehot = jnp.concatenate(parts, axis=1)
            acc_ref[at, :] += jnp.dot(
                onehot, held_ref[k * block : (k + 1) * block, :], preferred_element_type=jnp.float32
            )
            return carry

        lax.fori_loop(row_ref[k] - first, jnp.minimum(row_ref[k + 1] - first, WIN - 1) + 1, one_row, 0)

    for t in range(WIN):
        for j in range(owners):
            turn_ref[j * SLOT + t * SUB : j * SLOT + (t + 1) * SUB, :] = acc_ref[
                t * LANES + j * SUB : t * LANES + (j + 1) * SUB, :
            ]
    out_ref[...] = turn_ref[...].astype(jnp.bfloat16)


def segment_sums(starts, owner, grads, owners, width):
    steps = 8
    rows = owners * SLOT
    vmem = pl.BlockSpec(memory_space=pltpu.VMEM)
    return pl.pallas_call(
        seg_kernel,
        in_specs=[vmem, vmem, pl.BlockSpec(memory_space=pl.ANY)],
        out_shape=jax.ShapeDtypeStruct((rows, width), jnp.bfloat16),
        scratch_shapes=[
            pltpu.VMEM(starts.shape, jnp.int32),
            pltpu.VMEM((rows, LANES), jnp.float32),
            pltpu.VMEM((rows, LANES), jnp.float32),
            pltpu.VMEM((rows, width), jnp.float32),
            pltpu.VMEM((rows, width), jnp.float32),
            pltpu.VMEM((grads.shape[0], width), jnp.bfloat16),
            pltpu.SMEM((steps + 1,), jnp.int32),
            pltpu.SemaphoreType.DMA((steps,)),
        ],
        compiler_params=pltpu.CompilerParams(vmem_limit_bytes=WIDE),
    )(starts, owner, grads)


def collect_kernel(first_ref, in_ref, out_ref, wide_ref, acc_ref):
    wide_ref[...] = in_ref[...].astype(jnp.float32)
    acc_ref[...] = jnp.zeros_like(acc_ref)
    for s in range(in_ref.shape[0] // SLOT):
        at = pl.ds(pl.multiple_of(first_ref[s] * SUB, SUB), SLOT)
        acc_ref[at, :] += wide_ref[s * SLOT : (s + 1) * SLOT, :]
    out_ref[...] = acc_ref[...].T.astype(jnp.bfloat16)


def collect(first, incoming, patch_rows, interpret=False):
    rows, width = incoming.shape
    return pl.pallas_call(
        collect_kernel,
        in_specs=[pl.BlockSpec(memory_space=pltpu.SMEM), pl.BlockSpec(memory_space=pltpu.VMEM)],
        out_specs=pl.BlockSpec(memory_space=pltpu.VMEM),
        out_shape=jax.ShapeDtypeStruct((width, patch_rows), jnp.bfloat16),
        scratch_shapes=[pltpu.VMEM((rows, width), jnp.float32), pltpu.VMEM((patch_rows, width), jnp.float32)],
        compiler_params=pltpu.CompilerParams(vmem_limit_bytes=VMEM),
        interpret=interpret,
    )(first, incoming)


def outer_kernel(mine_ref, third_ref, cross_ref, n0_ref, n1a_ref, n1b_ref, f0_ref, f1a_ref, f1b_ref, out_ref, both_ref, held_ref, sems):
    near_t = jnp.where(lax.axis_index("dp") == 0, mine_ref[...], third_ref[...])
    far_t = cross_ref[...]
    both_ref[0] = near_t
    both_ref[1] = far_t
    low = lax.rem(lax.axis_index("tensor"), 2)
    blocks = out_ref.shape[0] // 2
    cols = n0_ref.shape[1]
    wide = 256
    per = wide // LANES
    copies = []
    for i in range(cols // wide):
        at = slice(i * wide, (i + 1) * wide)
        near1 = jnp.concatenate([n1a_ref[:, at], n1b_ref[:, at]], axis=0)
        far1 = jnp.concatenate([f1a_ref[:, at], f1b_ref[:, at]], axis=0)
        for k, (near, far, which) in enumerate(((n0_ref[:, at], f0_ref[:, at], low), (near1, far1, 1 - low))):
            total = jnp.dot(near_t, near, preferred_element_type=jnp.float32)
            total += jnp.dot(far_t, far, preferred_element_type=jnp.float32)
            total = total.astype(jnp.bfloat16)
            here = k * blocks + i * per
            for j in range(per):
                held_ref[here + j] = total[:, j * LANES : (j + 1) * LANES]
            copy = pltpu.make_async_copy(
                held_ref.at[pl.ds(here, per)],
                out_ref.at[pl.ds(which * blocks + i * per, per)],
                sems.at[2 * i + k],
            )
            copy.start()
            copies.append(copy)
    for copy in copies:
        copy.wait()


def outer(sums, columns):
    width, rows = sums[0].shape
    cols = columns[0].shape[1]
    vmem = pl.BlockSpec(memory_space=pltpu.VMEM)
    shape = (2 * cols // LANES, width, LANES)
    return pl.pallas_call(
        outer_kernel,
        in_specs=[vmem] * (len(sums) + len(columns)),
        out_specs=[pl.BlockSpec(memory_space=pltpu.HBM), vmem],
        out_shape=[
            jax.ShapeDtypeStruct(shape, jnp.bfloat16),
            jax.ShapeDtypeStruct((2, width, rows), jnp.bfloat16),
        ],
        scratch_shapes=[pltpu.VMEM(shape, jnp.bfloat16), pltpu.SemaphoreType.DMA((2 * cols // 256,))],
        compiler_params=pltpu.CompilerParams(vmem_limit_bytes=VMEM),
    )(*sums, *columns)


def eighth():
    ctx = lax.axis_index("context")
    return 2 * lax.div(ctx, SIDE) + lax.rem(ctx, 2)


def flip(a, b):
    return a + b - 2 * b * lax.rem(a, 2)


def chain_kernel(value_ref, out_w_ref, global_ref, both_ref, own_ref, pair_ref, away_ref, held_ref, sems):
    rows, wide = own_ref.shape
    dp, ten = lax.axis_index("dp"), lax.axis_index("tensor")
    targets = (ten, flip(ten, 1), 3 - ten, flip(3 - ten, 1))
    copies = []
    for s, target in enumerate(targets):
        at = (target * 8 + eighth()) * rows
        copy = pltpu.make_async_copy(global_ref.at[pl.ds(pl.multiple_of(at, rows), rows)], held_ref.at[s], sems.at[s])
        copy.start()
        copies.append(copy)
    both_ref[...] = jnp.dot(
        value_ref[...], out_w_ref[...], preferred_element_type=jnp.float32
    ).astype(jnp.bfloat16)
    for s in range(0, 4, 2):
        copies[s].wait()
        copies[s + 1].wait()
        half = flip(dp, lax.div(targets[s], 2))
        cols = pl.ds(pl.multiple_of(half * wide, wide), wide)
        left = jnp.concatenate([held_ref[s], held_ref[s + 1]], axis=0)
        total = jnp.dot(left, both_ref[:, cols], preferred_element_type=jnp.float32).astype(jnp.bfloat16)
        if s == 0:
            own_ref[...] = total[:rows]
            pair_ref[...] = total[rows:]
        else:
            away_ref[0] = total[:rows]
            away_ref[1] = total[rows:]


def chain_terms(w_value, w_out, w_global):
    deep, feats = w_value.shape
    rows = w_global.shape[0] // 32
    vmem = pl.BlockSpec(memory_space=pltpu.VMEM)
    part = jax.ShapeDtypeStruct((rows, feats // 2), jnp.bfloat16)
    return pl.pallas_call(
        chain_kernel,
        in_specs=[vmem, vmem, pl.BlockSpec(memory_space=pl.ANY)],
        out_specs=[vmem] * 4,
        out_shape=[
            jax.ShapeDtypeStruct((deep, feats), jnp.bfloat16),
            part,
            part,
            jax.ShapeDtypeStruct((2, rows, feats // 2), jnp.bfloat16),
        ],
        scratch_shapes=[pltpu.VMEM((4, rows, deep), jnp.bfloat16), pltpu.SemaphoreType.DMA((4,))],
        compiler_params=pltpu.CompilerParams(vmem_limit_bytes=WIDE),
    )(w_value, w_out, w_global)


def rows_kernel(which, near_ref, far_ref, low_ref, high_ref, *rest):
    out_ref, table_ref = rest[-2:]
    deep = near_ref.shape[1]
    rows = low_ref.shape[2]
    z, y = lax.div(eighth(), 2), lax.rem(eighth(), 2)
    for ref, base in ((low_ref, z), (high_ref, SIDE - 1 - z)):
        for i in range(2):
            for j in range(2):
                to = 2 * flip(base, i) + flip(y, j)
                table_ref[pl.ds(pl.multiple_of(to * rows, rows), rows), :] = ref[i, j]
    odd = lax.rem(lax.axis_index("tensor") + lax.axis_index("dp"), 2)
    dims = (((1,), (1,)), ((), ()))
    first = table_ref[:, pl.ds(pl.multiple_of(odd * deep, deep), deep)]
    second = table_ref[:, pl.ds(pl.multiple_of((1 - odd) * deep, deep), deep)]
    total = lax.dot_general(near_ref[which].T, first, dims, preferred_element_type=jnp.float32)
    total += lax.dot_general(far_ref[which].T, second, dims, preferred_element_type=jnp.float32)
    if len(rest) > 2:
        total += rest[0][...].astype(jnp.float32)
    out_ref[...] = total.astype(jnp.bfloat16)


def context_rows(which, near, far, low, high, *back):
    vmem = pl.BlockSpec(memory_space=pltpu.VMEM)
    cols, half = 8 * low.shape[2], low.shape[3]
    return pl.pallas_call(
        functools.partial(rows_kernel, which),
        in_specs=[vmem] * (4 + len(back)),
        out_specs=vmem,
        out_shape=jax.ShapeDtypeStruct((near.shape[2], cols), jnp.bfloat16),
        scratch_shapes=[pltpu.VMEM((cols, half), jnp.bfloat16)],
        compiler_params=pltpu.CompilerParams(vmem_limit_bytes=VMEM),
    )(near, far, low, high, *back)


def last_kernel(a_ref, b_ref, c_ref, d_ref, w_ref, out_ref):
    width = a_ref.shape[0]
    dp, ten = lax.axis_index("dp"), lax.axis_index("tensor")
    total = jnp.zeros(out_ref.shape, jnp.float32)
    for s, ref in enumerate((a_ref, b_ref, c_ref, d_ref)):
        source = lax.bitwise_xor(ten, s)
        near = 2 * dp + lax.rem(source, 2)
        at = jnp.where(source < 2, near, 3 - near)
        total += lax.dot_general(
            ref[...].T,
            w_ref[:, pl.ds(pl.multiple_of(at * width, width), width)],
            (((1,), (1,)), ((), ())),
            preferred_element_type=jnp.float32,
        )
    out_ref[...] = total


def last(pieces, weights):
    vmem = pl.BlockSpec(memory_space=pltpu.VMEM)
    return pl.pallas_call(
        last_kernel,
        in_specs=[vmem] * (len(pieces) + 1),
        out_shape=jax.ShapeDtypeStruct((pieces[0].shape[1], weights.shape[0]), jnp.float32),
        compiler_params=pltpu.CompilerParams(vmem_limit_bytes=VMEM),
    )(*pieces, weights)


def after(value, *others):
    return lax.optimization_barrier((value, *others))[0]


def local(byte_grads, patch_starts, patch_owner, attn_context, w_global, w_value, w_out):
    dp_n, ctx_n, ten_n = (lax.axis_size(a) for a in ("dp", "context", "tensor"))
    f32, bf16 = jnp.float32, jnp.bfloat16
    bytes_n, feats = byte_grads.shape[1:]
    width = feats // ten_n
    patch_rows = attn_context.shape[1]
    starts = patch_starts.reshape(-1, LANES)
    owner = patch_owner.reshape(-1, LANES)
    line = ("dp", "tensor")

    def moves(target):
        pairs = []
        for d in range(dp_n):
            for x in range(ten_n):
                to = target(d, x)
                if to is not None:
                    pairs.append((d * ten_n + x, to[0] * ten_n + to[1]))
        return pairs

    swap = [(i, dp_n - 1 - i) for i in range(dp_n)]
    pair = [(x, x ^ 1) for x in range(ten_n)]
    near0 = attn_context[0]
    far0 = lax.ppermute(near0, "dp", swap)
    near1 = [lax.ppermute(near0[:CUT], "tensor", pair)]

    def along(target):
        return [
            (i * SIDE + j, target(i, j)[0] * SIDE + target(i, j)[1]) for i in range(SIDE) for j in range(SIDE)
        ]

    both_t, own, paired, away = chain_terms(w_value, w_out, w_global)
    away = lax.ppermute(away, "tensor", [(x, ten_n - 1 - x) for x in range(ten_n)])

    outgoing = segment_sums(after(starts, both_t), owner, byte_grads[0], ctx_n, width)
    outgoing = after(outgoing, near1[0], away)
    incoming = lax.all_to_all(outgoing, "context", split_axis=0, concat_axis=0, tiled=True)

    away = after(away, outgoing)
    paired = (paired.astype(f32) + away[1].astype(f32)).astype(bf16)
    paired = lax.ppermute(paired, "tensor", pair)
    chain = (own.astype(f32) + away[0].astype(f32) + paired.astype(f32)).astype(bf16)
    chain = jnp.stack([chain, lax.ppermute(chain, "context", along(lambda i, j: (i, j ^ 1)))])
    edges = jnp.arange(ctx_n, dtype=jnp.int32) * bytes_n
    counts = jnp.sum((patch_starts[0][None, :] <= edges[:, None]).astype(jnp.int32), axis=1)
    first = jnp.minimum((counts - 1) // LANES, starts.shape[0] - WIN)
    far1 = [lax.ppermute(near1[0], "dp", swap)]
    incoming = after(incoming, first, far0, far1[0], chain)

    near1.append(lax.ppermute(after(near0, incoming)[CUT:], "tensor", pair))
    sums = collect(first, incoming, patch_rows)
    cross = lax.ppermute(sums, line, moves(lambda d, x: (0, x) if d == 1 else (1, ten_n - 1 - x)))
    third = lax.ppermute(sums, line, moves(lambda d, x: (1, ten_n - 1 - x) if d == 1 else None))
    other = lax.ppermute(after(chain, sums), "context", along(lambda i, j: (i ^ 1, j)))
    far1.append(lax.ppermute(after(near1[1], cross, third, other), "dp", swap))
    columns = (near0, *near1, far0, *far1)
    partial, near = outer((sums, third, cross), columns)
    pieces = lax.all_to_all(partial, "context", split_axis=0, concat_axis=0, tiled=True)
    chain = jnp.stack([after(chain, partial), after(other, partial)])
    rest = lax.ppermute(chain, "context", along(lambda i, j: (SIDE - 1 - i, j)))

    far = lax.ppermute(near, "tensor", pair)
    piece = jnp.sum(pieces.astype(f32), axis=0).astype(bf16)
    parts = []
    for s in range(ten_n):
        parts.append(lax.ppermute(piece, line, moves(lambda d, x, s=s: (x // 2, (2 * d + x % 2) ^ s))))
    give = context_rows(1, after(near, *parts), far, chain, rest)
    back = lax.ppermute(give, "dp", swap)
    context_grad = context_rows(0, near, far, chain, rest, back)
    weight_grad = last(parts, both_t)
    return (context_grad[None], weight_grad)


def solution(mesh):
    placed = (
        P("dp", "context", None),
        P("dp", None),
        P("dp", None),
        P("dp", "context", "tensor"),
        P(None, "tensor"),
        P("tensor", None),
        P(),
    )
    return jax.shard_map(
        local,
        mesh=mesh,
        in_specs=placed,
        out_specs=(P("dp", "context", "tensor"), P(("dp", "context"), "tensor")),
        check_vma=False,
    )
```

```python
import functools

import jax
import jax.numpy as jnp
from jax import lax
from jax.experimental import pallas as pl
from jax.experimental.pallas import tpu as pltpu
from jax.sharding import PartitionSpec as P

LANES = 128
GROUP = 16
SUB = LANES // GROUP
WIN = 9
SLOT = WIN * SUB
SIDE = 4
CUT = 320
VMEM = 24 * 1024 * 1024
WIDE = 56 * 1024 * 1024


def seg_kernel(starts_ref, owner_ref, bytes_ref, out_ref, next_ref, low_ref, high_ref, acc_ref, turn_ref, held_ref, row_ref, sems):
    steps = sems.shape[0]
    shard, width = held_ref.shape
    block = shard // steps
    owners = LANES // SUB
    from_col = pl.ds(pl.multiple_of(lax.axis_index("tensor") * width, width), width)
    copies = []
    for k in range(steps):
        at = pl.ds(k * block, block)
        copies.append(pltpu.make_async_copy(bytes_ref.at[at, from_col], held_ref.at[at, :], sems.at[k]))
        copies[k].start()

    starts = starts_ref[...]
    rows = starts.shape[0]
    base = lax.axis_index("context") * shard
    for k in range(steps + 1):
        count = jnp.sum((starts <= base + k * block).astype(jnp.float32)).astype(jnp.int32)
        row_ref[k] = lax.shift_right_logical(count - 1, 7)
    first = jnp.minimum(row_ref[0], rows - WIN)
    lane = lax.broadcasted_iota(jnp.int32, starts.shape, 1)
    turned = pltpu.roll(starts, LANES - 1, 1)
    below = jnp.concatenate([turned[1:], jnp.full((1, LANES), 2**30, jnp.int32)], axis=0)
    next_ref[...] = jnp.where(lane == LANES - 1, below, turned)
    lane = lax.broadcasted_iota(jnp.int32, (SUB, LANES), 1)
    mine = lax.shift_right_logical(lane, 4) == lax.broadcasted_iota(jnp.int32, (SUB, LANES), 0)
    for t in range(WIN):
        low = jnp.clip(starts_ref[pl.ds(first + t, 1), :] - base, 0, shard).astype(jnp.float32)
        high = jnp.clip(next_ref[pl.ds(first + t, 1), :] - base, 0, shard).astype(jnp.float32)
        low = jnp.broadcast_to(low, (SUB, LANES))
        high = jnp.broadcast_to(high, (SUB, LANES))
        owner = jnp.broadcast_to(owner_ref[pl.ds(first + t, 1), :], (SUB, LANES))
        owner = jnp.where(mine, owner, -1)
        for j in range(owners):
            held = owner == j
            at = t * LANES + j * SUB
            one = jnp.sum(jnp.where(held, low, 0.0), axis=1, keepdims=True)
            low_ref[at : at + SUB, :] = jnp.broadcast_to(one, (SUB, LANES))
            one = jnp.sum(jnp.where(held, high, 0.0), axis=1, keepdims=True)
            high_ref[at : at + SUB, :] = jnp.broadcast_to(one, (SUB, LANES))
    acc_ref[...] = jnp.zeros_like(acc_ref)

    for k in range(steps):
        copies[k].wait()

        def one_row(t, carry, k=k):
            at = pl.ds(pl.multiple_of(t * LANES, LANES), LANES)
            low = low_ref[at, :]
            high = high_ref[at, :]
            parts = []
            for q in range(block // LANES):
                place = lax.broadcasted_iota(jnp.int32, (1, LANES), 1) + (k * block + q * LANES)
                place = place.astype(jnp.float32)
                parts.append(jnp.where((place >= low) & (place < high), 1.0, 0.0).astype(jnp.bfloat16))
            onehot = jnp.concatenate(parts, axis=1)
            acc_ref[at, :] += jnp.dot(
                onehot, held_ref[k * block : (k + 1) * block, :], preferred_element_type=jnp.float32
            )
            return carry

        lax.fori_loop(row_ref[k] - first, jnp.minimum(row_ref[k + 1] - first, WIN - 1) + 1, one_row, 0)

    for t in range(WIN):
        for j in range(owners):
            turn_ref[j * SLOT + t * SUB : j * SLOT + (t + 1) * SUB, :] = acc_ref[
                t * LANES + j * SUB : t * LANES + (j + 1) * SUB, :
            ]
    out_ref[...] = turn_ref[...].astype(jnp.bfloat16)


def segment_sums(starts, owner, grads, owners, width):
    steps = 8
    rows = owners * SLOT
    vmem = pl.BlockSpec(memory_space=pltpu.VMEM)
    return pl.pallas_call(
        seg_kernel,
        in_specs=[vmem, vmem, pl.BlockSpec(memory_space=pl.ANY)],
        out_shape=jax.ShapeDtypeStruct((rows, width), jnp.bfloat16),
        scratch_shapes=[
            pltpu.VMEM(starts.shape, jnp.int32),
            pltpu.VMEM((rows, LANES), jnp.float32),
            pltpu.VMEM((rows, LANES), jnp.float32),
            pltpu.VMEM((rows, width), jnp.float32),
            pltpu.VMEM((rows, width), jnp.float32),
            pltpu.VMEM((grads.shape[0], width), jnp.bfloat16),
            pltpu.SMEM((steps + 1,), jnp.int32),
            pltpu.SemaphoreType.DMA((steps,)),
        ],
        compiler_params=pltpu.CompilerParams(vmem_limit_bytes=WIDE),
    )(starts, owner, grads)


def collect_kernel(first_ref, in_ref, out_ref, wide_ref, acc_ref):
    wide_ref[...] = in_ref[...].astype(jnp.float32)
    acc_ref[...] = jnp.zeros_like(acc_ref)
    for s in range(in_ref.shape[0] // SLOT):
        at = pl.ds(pl.multiple_of(first_ref[s] * SUB, SUB), SLOT)
        acc_ref[at, :] += wide_ref[s * SLOT : (s + 1) * SLOT, :]
    out_ref[...] = acc_ref[...].T.astype(jnp.bfloat16)


def collect(first, incoming, patch_rows, interpret=False):
    rows, width = incoming.shape
    return pl.pallas_call(
        collect_kernel,
        in_specs=[pl.BlockSpec(memory_space=pltpu.SMEM), pl.BlockSpec(memory_space=pltpu.VMEM)],
        out_specs=pl.BlockSpec(memory_space=pltpu.VMEM),
        out_shape=jax.ShapeDtypeStruct((width, patch_rows), jnp.bfloat16),
        scratch_shapes=[pltpu.VMEM((rows, width), jnp.float32), pltpu.VMEM((patch_rows, width), jnp.float32)],
        compiler_params=pltpu.CompilerParams(vmem_limit_bytes=VMEM),
        interpret=interpret,
    )(first, incoming)


def outer_kernel(mine_ref, third_ref, cross_ref, n0_ref, n1a_ref, n1b_ref, f0_ref, f1a_ref, f1b_ref, out_ref, both_ref, held_ref, sems):
    near_t = jnp.where(lax.axis_index("dp") == 0, mine_ref[...], third_ref[...])
    far_t = cross_ref[...]
    both_ref[0] = near_t
    both_ref[1] = far_t
    low = lax.rem(lax.axis_index("tensor"), 2)
    blocks = out_ref.shape[0] // 2
    cols = n0_ref.shape[1]
    wide = 256
    per = wide // LANES
    copies = []
    for i in range(cols // wide):
        at = slice(i * wide, (i + 1) * wide)
        near1 = jnp.concatenate([n1a_ref[:, at], n1b_ref[:, at]], axis=0)
        far1 = jnp.concatenate([f1a_ref[:, at], f1b_ref[:, at]], axis=0)
        for k, (near, far, which) in enumerate(((n0_ref[:, at], f0_ref[:, at], low), (near1, far1, 1 - low))):
            total = jnp.dot(near_t, near, preferred_element_type=jnp.float32)
            total += jnp.dot(far_t, far, preferred_element_type=jnp.float32)
            total = total.astype(jnp.bfloat16)
            here = k * blocks + i * per
            for j in range(per):
                held_ref[here + j] = total[:, j * LANES : (j + 1) * LANES]
            copy = pltpu.make_async_copy(
                held_ref.at[pl.ds(here, per)],
                out_ref.at[pl.ds(which * blocks + i * per, per)],
                sems.at[2 * i + k],
            )
            copy.start()
            copies.append(copy)
    for copy in copies:
        copy.wait()


def outer(sums, columns):
    width, rows = sums[0].shape
    cols = columns[0].shape[1]
    vmem = pl.BlockSpec(memory_space=pltpu.VMEM)
    shape = (2 * cols // LANES, width, LANES)
    return pl.pallas_call(
        outer_kernel,
        in_specs=[vmem] * (len(sums) + len(columns)),
        out_specs=[pl.BlockSpec(memory_space=pltpu.HBM), vmem],
        out_shape=[
            jax.ShapeDtypeStruct(shape, jnp.bfloat16),
            jax.ShapeDtypeStruct((2, width, rows), jnp.bfloat16),
        ],
        scratch_shapes=[pltpu.VMEM(shape, jnp.bfloat16), pltpu.SemaphoreType.DMA((2 * cols // 256,))],
        compiler_params=pltpu.CompilerParams(vmem_limit_bytes=VMEM),
    )(*sums, *columns)


def eighth():
    ctx = lax.axis_index("context")
    return 2 * lax.div(ctx, SIDE) + lax.rem(ctx, 2)


def flip(a, b):
    return a + b - 2 * b * lax.rem(a, 2)


def chain_kernel(value_ref, out_w_ref, global_ref, both_ref, own_ref, pair_ref, away_ref, held_ref, sems):
    rows, wide = own_ref.shape
    dp, ten = lax.axis_index("dp"), lax.axis_index("tensor")
    targets = (ten, flip(ten, 1), 3 - ten, flip(3 - ten, 1))
    copies = []
    for s, target in enumerate(targets):
        at = (target * 8 + eighth()) * rows
        copy = pltpu.make_async_copy(global_ref.at[pl.ds(pl.multiple_of(at, rows), rows)], held_ref.at[s], sems.at[s])
        copy.start()
        copies.append(copy)
    both_ref[...] = jnp.dot(
        value_ref[...], out_w_ref[...], preferred_element_type=jnp.float32
    ).astype(jnp.bfloat16)
    for s in range(0, 4, 2):
        copies[s].wait()
        copies[s + 1].wait()
        half = flip(dp, lax.div(targets[s], 2))
        cols = pl.ds(pl.multiple_of(half * wide, wide), wide)
        left = jnp.concatenate([held_ref[s], held_ref[s + 1]], axis=0)
        total = jnp.dot(left, both_ref[:, cols], preferred_element_type=jnp.float32).astype(jnp.bfloat16)
        if s == 0:
            own_ref[...] = total[:rows]
            pair_ref[...] = total[rows:]
        else:
            away_ref[0] = total[:rows]
            away_ref[1] = total[rows:]


def chain_terms(w_value, w_out, w_global):
    deep, feats = w_value.shape
    rows = w_global.shape[0] // 32
    vmem = pl.BlockSpec(memory_space=pltpu.VMEM)
    part = jax.ShapeDtypeStruct((rows, feats // 2), jnp.bfloat16)
    return pl.pallas_call(
        chain_kernel,
        in_specs=[vmem, vmem, pl.BlockSpec(memory_space=pl.ANY)],
        out_specs=[vmem] * 4,
        out_shape=[
            jax.ShapeDtypeStruct((deep, feats), jnp.bfloat16),
            part,
            part,
            jax.ShapeDtypeStruct((2, rows, feats // 2), jnp.bfloat16),
        ],
        scratch_shapes=[pltpu.VMEM((4, rows, deep), jnp.bfloat16), pltpu.SemaphoreType.DMA((4,))],
        compiler_params=pltpu.CompilerParams(vmem_limit_bytes=WIDE),
    )(w_value, w_out, w_global)


def rows_kernel(which, near_ref, far_ref, low_ref, high_ref, *rest):
    out_ref, table_ref = rest[-2:]
    deep = near_ref.shape[1]
    rows = low_ref.shape[2]
    z, y = lax.div(eighth(), 2), lax.rem(eighth(), 2)
    for ref, base in ((low_ref, z), (high_ref, SIDE - 1 - z)):
        for i in range(2):
            for j in range(2):
                to = 2 * flip(base, i) + flip(y, j)
                table_ref[pl.ds(pl.multiple_of(to * rows, rows), rows), :] = ref[i, j]
    odd = lax.rem(lax.axis_index("tensor") + lax.axis_index("dp"), 2)
    dims = (((1,), (1,)), ((), ()))
    first = table_ref[:, pl.ds(pl.multiple_of(odd * deep, deep), deep)]
    second = table_ref[:, pl.ds(pl.multiple_of((1 - odd) * deep, deep), deep)]
    total = lax.dot_general(near_ref[which].T, first, dims, preferred_element_type=jnp.float32)
    total += lax.dot_general(far_ref[which].T, second, dims, preferred_element_type=jnp.float32)
    if len(rest) > 2:
        total += rest[0][...].astype(jnp.float32)
    out_ref[...] = total.astype(jnp.bfloat16)


def context_rows(which, near, far, low, high, *back):
    vmem = pl.BlockSpec(memory_space=pltpu.VMEM)
    cols, half = 8 * low.shape[2], low.shape[3]
    return pl.pallas_call(
        functools.partial(rows_kernel, which),
        in_specs=[vmem] * (4 + len(back)),
        out_specs=vmem,
        out_shape=jax.ShapeDtypeStruct((near.shape[2], cols), jnp.bfloat16),
        scratch_shapes=[pltpu.VMEM((cols, half), jnp.bfloat16)],
        compiler_params=pltpu.CompilerParams(vmem_limit_bytes=VMEM),
    )(near, far, low, high, *back)


def last_kernel(a_ref, b_ref, c_ref, d_ref, w_ref, out_ref):
    width = a_ref.shape[0]
    dp, ten = lax.axis_index("dp"), lax.axis_index("tensor")
    total = jnp.zeros(out_ref.shape, jnp.float32)
    for s, ref in enumerate((a_ref, b_ref, c_ref, d_ref)):
        source = lax.bitwise_xor(ten, s)
        near = 2 * dp + lax.rem(source, 2)
        at = jnp.where(source < 2, near, 3 - near)
        total += lax.dot_general(
            ref[...].T,
            w_ref[:, pl.ds(pl.multiple_of(at * width, width), width)],
            (((1,), (1,)), ((), ())),
            preferred_element_type=jnp.float32,
        )
    out_ref[...] = total


def last(pieces, weights):
    vmem = pl.BlockSpec(memory_space=pltpu.VMEM)
    return pl.pallas_call(
        last_kernel,
        in_specs=[vmem] * (len(pieces) + 1),
        out_shape=jax.ShapeDtypeStruct((pieces[0].shape[1], weights.shape[0]), jnp.float32),
        compiler_params=pltpu.CompilerParams(vmem_limit_bytes=VMEM),
    )(*pieces, weights)


def after(value, *others):
    return lax.optimization_barrier((value, *others))[0]


def local(byte_grads, patch_starts, patch_owner, attn_context, w_global, w_value, w_out):
    dp_n, ctx_n, ten_n = (lax.axis_size(a) for a in ("dp", "context", "tensor"))
    f32, bf16 = jnp.float32, jnp.bfloat16
    bytes_n, feats = byte_grads.shape[1:]
    width = feats // ten_n
    patch_rows = attn_context.shape[1]
    starts = patch_starts.reshape(-1, LANES)
    owner = patch_owner.reshape(-1, LANES)
    line = ("dp", "tensor")

    def moves(target):
        pairs = []
        for d in range(dp_n):
            for x in range(ten_n):
                to = target(d, x)
                if to is not None:
                    pairs.append((d * ten_n + x, to[0] * ten_n + to[1]))
        return pairs

    swap = [(i, dp_n - 1 - i) for i in range(dp_n)]
    pair = [(x, x ^ 1) for x in range(ten_n)]
    near0 = attn_context[0]
    near1 = [lax.ppermute(near0[:CUT], "tensor", pair)]

    def along(target):
        return [
            (i * SIDE + j, target(i, j)[0] * SIDE + target(i, j)[1]) for i in range(SIDE) for j in range(SIDE)
        ]

    both_t, own, paired, away = chain_terms(w_value, w_out, w_global)
    away = lax.ppermute(away, "tensor", [(x, ten_n - 1 - x) for x in range(ten_n)])

    outgoing = segment_sums(after(starts, both_t), owner, byte_grads[0], ctx_n, width)
    outgoing = after(outgoing, near1[0], away)
    incoming = lax.all_to_all(outgoing, "context", split_axis=0, concat_axis=0, tiled=True)

    away = after(away, outgoing)
    paired = (paired.astype(f32) + away[1].astype(f32)).astype(bf16)
    paired = lax.ppermute(paired, "tensor", pair)
    chain = (own.astype(f32) + away[0].astype(f32) + paired.astype(f32)).astype(bf16)
    chain = jnp.stack([chain, lax.ppermute(chain, "context", along(lambda i, j: (i, j ^ 1)))])
    edges = jnp.arange(ctx_n, dtype=jnp.int32) * bytes_n
    counts = jnp.sum((patch_starts[0][None, :] <= edges[:, None]).astype(jnp.int32), axis=1)
    first = jnp.minimum((counts - 1) // LANES, starts.shape[0] - WIN)
    incoming = after(incoming, first, chain)

    near1.append(lax.ppermute(after(near0, incoming)[CUT:], "tensor", pair))
    sums = collect(first, incoming, patch_rows)
    cross = lax.ppermute(sums, line, moves(lambda d, x: (0, x) if d == 1 else (1, ten_n - 1 - x)))
    third = lax.ppermute(sums, line, moves(lambda d, x: (1, ten_n - 1 - x) if d == 1 else None))
    other = lax.ppermute(after(chain, sums), "context", along(lambda i, j: (i ^ 1, j)))
    far0 = lax.ppermute(after(near0, sums), "dp", swap)
    far1 = [lax.ppermute(after(near1[0], sums), "dp", swap)]
    far1.append(lax.ppermute(after(near1[1], cross, third, other), "dp", swap))
    columns = (near0, *near1, far0, *far1)
    partial, near = outer((sums, third, cross), columns)
    pieces = lax.all_to_all(partial, "context", split_axis=0, concat_axis=0, tiled=True)
    chain = jnp.stack([after(chain, partial), after(other, partial)])
    rest = lax.ppermute(chain, "context", along(lambda i, j: (SIDE - 1 - i, j)))

    far = lax.ppermute(near, "tensor", pair)
    piece = jnp.sum(pieces.astype(f32), axis=0).astype(bf16)
    parts = []
    for s in range(ten_n):
        parts.append(lax.ppermute(piece, line, moves(lambda d, x, s=s: (x // 2, (2 * d + x % 2) ^ s))))
    give = context_rows(1, after(near, *parts), far, chain, rest)
    back = lax.ppermute(give, "dp", swap)
    context_grad = context_rows(0, near, far, chain, rest, back)
    weight_grad = last(parts, both_t)
    return (context_grad[None], weight_grad)


def solution(mesh):
    placed = (
        P("dp", "context", None),
        P("dp", None),
        P("dp", None),
        P("dp", "context", "tensor"),
        P(None, "tensor"),
        P("tensor", None),
        P(),
    )
    return jax.shard_map(
        local,
        mesh=mesh,
        in_specs=placed,
        out_specs=(P("dp", "context", "tensor"), P(("dp", "context"), "tensor")),
        check_vma=False,
    )
```

```python
import functools

import jax
import jax.numpy as jnp
from jax import lax
from jax.experimental import pallas as pl
from jax.experimental.pallas import tpu as pltpu
from jax.sharding import PartitionSpec as P

LANES = 128
GROUP = 16
SUB = LANES // GROUP
WIN = 9
SLOT = WIN * SUB
SIDE = 4
CUT = 352
VMEM = 24 * 1024 * 1024
WIDE = 56 * 1024 * 1024


def seg_kernel(starts_ref, owner_ref, bytes_ref, out_ref, next_ref, low_ref, high_ref, acc_ref, turn_ref, held_ref, row_ref, sems):
    steps = sems.shape[0]
    shard, width = held_ref.shape
    block = shard // steps
    owners = LANES // SUB
    from_col = pl.ds(pl.multiple_of(lax.axis_index("tensor") * width, width), width)
    copies = []
    for k in range(steps):
        at = pl.ds(k * block, block)
        copies.append(pltpu.make_async_copy(bytes_ref.at[at, from_col], held_ref.at[at, :], sems.at[k]))
        copies[k].start()

    starts = starts_ref[...]
    rows = starts.shape[0]
    base = lax.axis_index("context") * shard
    for k in range(steps + 1):
        count = jnp.sum((starts <= base + k * block).astype(jnp.float32)).astype(jnp.int32)
        row_ref[k] = lax.shift_right_logical(count - 1, 7)
    first = jnp.minimum(row_ref[0], rows - WIN)
    lane = lax.broadcasted_iota(jnp.int32, starts.shape, 1)
    turned = pltpu.roll(starts, LANES - 1, 1)
    below = jnp.concatenate([turned[1:], jnp.full((1, LANES), 2**30, jnp.int32)], axis=0)
    next_ref[...] = jnp.where(lane == LANES - 1, below, turned)
    lane = lax.broadcasted_iota(jnp.int32, (SUB, LANES), 1)
    mine = lax.shift_right_logical(lane, 4) == lax.broadcasted_iota(jnp.int32, (SUB, LANES), 0)
    for t in range(WIN):
        low = jnp.clip(starts_ref[pl.ds(first + t, 1), :] - base, 0, shard).astype(jnp.float32)
        high = jnp.clip(next_ref[pl.ds(first + t, 1), :] - base, 0, shard).astype(jnp.float32)
        low = jnp.broadcast_to(low, (SUB, LANES))
        high = jnp.broadcast_to(high, (SUB, LANES))
        owner = jnp.broadcast_to(owner_ref[pl.ds(first + t, 1), :], (SUB, LANES))
        owner = jnp.where(mine, owner, -1)
        for j in range(owners):
            held = owner == j
            at = t * LANES + j * SUB
            one = jnp.sum(jnp.where(held, low, 0.0), axis=1, keepdims=True)
            low_ref[at : at + SUB, :] = jnp.broadcast_to(one, (SUB, LANES))
            one = jnp.sum(jnp.where(held, high, 0.0), axis=1, keepdims=True)
            high_ref[at : at + SUB, :] = jnp.broadcast_to(one, (SUB, LANES))
    acc_ref[...] = jnp.zeros_like(acc_ref)

    for k in range(steps):
        copies[k].wait()

        def one_row(t, carry, k=k):
            at = pl.ds(pl.multiple_of(t * LANES, LANES), LANES)
            low = low_ref[at, :]
            high = high_ref[at, :]
            parts = []
            for q in range(block // LANES):
                place = lax.broadcasted_iota(jnp.int32, (1, LANES), 1) + (k * block + q * LANES)
                place = place.astype(jnp.float32)
                parts.append(jnp.where((place >= low) & (place < high), 1.0, 0.0).astype(jnp.bfloat16))
            onehot = jnp.concatenate(parts, axis=1)
            acc_ref[at, :] += jnp.dot(
                onehot, held_ref[k * block : (k + 1) * block, :], preferred_element_type=jnp.float32
            )
            return carry

        lax.fori_loop(row_ref[k] - first, jnp.minimum(row_ref[k + 1] - first, WIN - 1) + 1, one_row, 0)

    for t in range(WIN):
        for j in range(owners):
            turn_ref[j * SLOT + t * SUB : j * SLOT + (t + 1) * SUB, :] = acc_ref[
                t * LANES + j * SUB : t * LANES + (j + 1) * SUB, :
            ]
    out_ref[...] = turn_ref[...].astype(jnp.bfloat16)


def segment_sums(starts, owner, grads, owners, width):
    steps = 8
    rows = owners * SLOT
    vmem = pl.BlockSpec(memory_space=pltpu.VMEM)
    return pl.pallas_call(
        seg_kernel,
        in_specs=[vmem, vmem, pl.BlockSpec(memory_space=pl.ANY)],
        out_shape=jax.ShapeDtypeStruct((rows, width), jnp.bfloat16),
        scratch_shapes=[
            pltpu.VMEM(starts.shape, jnp.int32),
            pltpu.VMEM((rows, LANES), jnp.float32),
            pltpu.VMEM((rows, LANES), jnp.float32),
            pltpu.VMEM((rows, width), jnp.float32),
            pltpu.VMEM((rows, width), jnp.float32),
            pltpu.VMEM((grads.shape[0], width), jnp.bfloat16),
            pltpu.SMEM((steps + 1,), jnp.int32),
            pltpu.SemaphoreType.DMA((steps,)),
        ],
        compiler_params=pltpu.CompilerParams(vmem_limit_bytes=WIDE),
    )(starts, owner, grads)


def collect_kernel(first_ref, in_ref, out_ref, wide_ref, acc_ref):
    wide_ref[...] = in_ref[...].astype(jnp.float32)
    acc_ref[...] = jnp.zeros_like(acc_ref)
    for s in range(in_ref.shape[0] // SLOT):
        at = pl.ds(pl.multiple_of(first_ref[s] * SUB, SUB), SLOT)
        acc_ref[at, :] += wide_ref[s * SLOT : (s + 1) * SLOT, :]
    out_ref[...] = acc_ref[...].T.astype(jnp.bfloat16)


def collect(first, incoming, patch_rows, interpret=False):
    rows, width = incoming.shape
    return pl.pallas_call(
        collect_kernel,
        in_specs=[pl.BlockSpec(memory_space=pltpu.SMEM), pl.BlockSpec(memory_space=pltpu.VMEM)],
        out_specs=pl.BlockSpec(memory_space=pltpu.VMEM),
        out_shape=jax.ShapeDtypeStruct((width, patch_rows), jnp.bfloat16),
        scratch_shapes=[pltpu.VMEM((rows, width), jnp.float32), pltpu.VMEM((patch_rows, width), jnp.float32)],
        compiler_params=pltpu.CompilerParams(vmem_limit_bytes=VMEM),
        interpret=interpret,
    )(first, incoming)


def outer_kernel(mine_ref, third_ref, cross_ref, n0_ref, n1a_ref, n1b_ref, f0_ref, f1a_ref, f1b_ref, out_ref, both_ref, held_ref, sems):
    near_t = jnp.where(lax.axis_index("dp") == 0, mine_ref[...], third_ref[...])
    far_t = cross_ref[...]
    both_ref[0] = near_t
    both_ref[1] = far_t
    low = lax.rem(lax.axis_index("tensor"), 2)
    blocks = out_ref.shape[0] // 2
    cols = n0_ref.shape[1]
    wide = 256
    per = wide // LANES
    copies = []
    for i in range(cols // wide):
        at = slice(i * wide, (i + 1) * wide)
        near1 = jnp.concatenate([n1a_ref[:, at], n1b_ref[:, at]], axis=0)
        far1 = jnp.concatenate([f1a_ref[:, at], f1b_ref[:, at]], axis=0)
        for k, (near, far, which) in enumerate(((n0_ref[:, at], f0_ref[:, at], low), (near1, far1, 1 - low))):
            total = jnp.dot(near_t, near, preferred_element_type=jnp.float32)
            total += jnp.dot(far_t, far, preferred_element_type=jnp.float32)
            total = total.astype(jnp.bfloat16)
            here = k * blocks + i * per
            for j in range(per):
                held_ref[here + j] = total[:, j * LANES : (j + 1) * LANES]
            copy = pltpu.make_async_copy(
                held_ref.at[pl.ds(here, per)],
                out_ref.at[pl.ds(which * blocks + i * per, per)],
                sems.at[2 * i + k],
            )
            copy.start()
            copies.append(copy)
    for copy in copies:
        copy.wait()


def outer(sums, columns):
    width, rows = sums[0].shape
    cols = columns[0].shape[1]
    vmem = pl.BlockSpec(memory_space=pltpu.VMEM)
    shape = (2 * cols // LANES, width, LANES)
    return pl.pallas_call(
        outer_kernel,
        in_specs=[vmem] * (len(sums) + len(columns)),
        out_specs=[pl.BlockSpec(memory_space=pltpu.HBM), vmem],
        out_shape=[
            jax.ShapeDtypeStruct(shape, jnp.bfloat16),
            jax.ShapeDtypeStruct((2, width, rows), jnp.bfloat16),
        ],
        scratch_shapes=[pltpu.VMEM(shape, jnp.bfloat16), pltpu.SemaphoreType.DMA((2 * cols // 256,))],
        compiler_params=pltpu.CompilerParams(vmem_limit_bytes=VMEM),
    )(*sums, *columns)


def eighth():
    ctx = lax.axis_index("context")
    return 2 * lax.div(ctx, SIDE) + lax.rem(ctx, 2)


def flip(a, b):
    return a + b - 2 * b * lax.rem(a, 2)


def chain_kernel(value_ref, out_w_ref, global_ref, both_ref, own_ref, pair_ref, away_ref, held_ref, sems):
    rows, wide = own_ref.shape
    dp, ten = lax.axis_index("dp"), lax.axis_index("tensor")
    targets = (ten, flip(ten, 1), 3 - ten, flip(3 - ten, 1))
    copies = []
    for s, target in enumerate(targets):
        at = (target * 8 + eighth()) * rows
        copy = pltpu.make_async_copy(global_ref.at[pl.ds(pl.multiple_of(at, rows), rows)], held_ref.at[s], sems.at[s])
        copy.start()
        copies.append(copy)
    both_ref[...] = jnp.dot(
        value_ref[...], out_w_ref[...], preferred_element_type=jnp.float32
    ).astype(jnp.bfloat16)
    for s in range(0, 4, 2):
        copies[s].wait()
        copies[s + 1].wait()
        half = flip(dp, lax.div(targets[s], 2))
        cols = pl.ds(pl.multiple_of(half * wide, wide), wide)
        left = jnp.concatenate([held_ref[s], held_ref[s + 1]], axis=0)
        total = jnp.dot(left, both_ref[:, cols], preferred_element_type=jnp.float32).astype(jnp.bfloat16)
        if s == 0:
            own_ref[...] = total[:rows]
            pair_ref[...] = total[rows:]
        else:
            away_ref[0] = total[:rows]
            away_ref[1] = total[rows:]


def chain_terms(w_value, w_out, w_global):
    deep, feats = w_value.shape
    rows = w_global.shape[0] // 32
    vmem = pl.BlockSpec(memory_space=pltpu.VMEM)
    part = jax.ShapeDtypeStruct((rows, feats // 2), jnp.bfloat16)
    return pl.pallas_call(
        chain_kernel,
        in_specs=[vmem, vmem, pl.BlockSpec(memory_space=pl.ANY)],
        out_specs=[vmem] * 4,
        out_shape=[
            jax.ShapeDtypeStruct((deep, feats), jnp.bfloat16),
            part,
            part,
            jax.ShapeDtypeStruct((2, rows, feats // 2), jnp.bfloat16),
        ],
        scratch_shapes=[pltpu.VMEM((4, rows, deep), jnp.bfloat16), pltpu.SemaphoreType.DMA((4,))],
        compiler_params=pltpu.CompilerParams(vmem_limit_bytes=WIDE),
    )(w_value, w_out, w_global)


def rows_kernel(which, near_ref, far_ref, low_ref, high_ref, *rest):
    out_ref, table_ref = rest[-2:]
    deep = near_ref.shape[1]
    rows = low_ref.shape[2]
    z, y = lax.div(eighth(), 2), lax.rem(eighth(), 2)
    for ref, base in ((low_ref, z), (high_ref, SIDE - 1 - z)):
        for i in range(2):
            for j in range(2):
                to = 2 * flip(base, i) + flip(y, j)
                table_ref[pl.ds(pl.multiple_of(to * rows, rows), rows), :] = ref[i, j]
    odd = lax.rem(lax.axis_index("tensor") + lax.axis_index("dp"), 2)
    dims = (((1,), (1,)), ((), ()))
    first = table_ref[:, pl.ds(pl.multiple_of(odd * deep, deep), deep)]
    second = table_ref[:, pl.ds(pl.multiple_of((1 - odd) * deep, deep), deep)]
    total = lax.dot_general(near_ref[which].T, first, dims, preferred_element_type=jnp.float32)
    total += lax.dot_general(far_ref[which].T, second, dims, preferred_element_type=jnp.float32)
    if len(rest) > 2:
        total += rest[0][...].astype(jnp.float32)
    out_ref[...] = total.astype(jnp.bfloat16)


def context_rows(which, near, far, low, high, *back):
    vmem = pl.BlockSpec(memory_space=pltpu.VMEM)
    cols, half = 8 * low.shape[2], low.shape[3]
    return pl.pallas_call(
        functools.partial(rows_kernel, which),
        in_specs=[vmem] * (4 + len(back)),
        out_specs=vmem,
        out_shape=jax.ShapeDtypeStruct((near.shape[2], cols), jnp.bfloat16),
        scratch_shapes=[pltpu.VMEM((cols, half), jnp.bfloat16)],
        compiler_params=pltpu.CompilerParams(vmem_limit_bytes=VMEM),
    )(near, far, low, high, *back)


def last_kernel(a_ref, b_ref, c_ref, d_ref, w_ref, out_ref):
    width = a_ref.shape[0]
    dp, ten = lax.axis_index("dp"), lax.axis_index("tensor")
    total = jnp.zeros(out_ref.shape, jnp.float32)
    for s, ref in enumerate((a_ref, b_ref, c_ref, d_ref)):
        source = lax.bitwise_xor(ten, s)
        near = 2 * dp + lax.rem(source, 2)
        at = jnp.where(source < 2, near, 3 - near)
        total += lax.dot_general(
            ref[...].T,
            w_ref[:, pl.ds(pl.multiple_of(at * width, width), width)],
            (((1,), (1,)), ((), ())),
            preferred_element_type=jnp.float32,
        )
    out_ref[...] = total


def last(pieces, weights):
    vmem = pl.BlockSpec(memory_space=pltpu.VMEM)
    return pl.pallas_call(
        last_kernel,
        in_specs=[vmem] * (len(pieces) + 1),
        out_shape=jax.ShapeDtypeStruct((pieces[0].shape[1], weights.shape[0]), jnp.float32),
        compiler_params=pltpu.CompilerParams(vmem_limit_bytes=VMEM),
    )(*pieces, weights)


def after(value, *others):
    return lax.optimization_barrier((value, *others))[0]


def local(byte_grads, patch_starts, patch_owner, attn_context, w_global, w_value, w_out):
    dp_n, ctx_n, ten_n = (lax.axis_size(a) for a in ("dp", "context", "tensor"))
    f32, bf16 = jnp.float32, jnp.bfloat16
    bytes_n, feats = byte_grads.shape[1:]
    width = feats // ten_n
    patch_rows = attn_context.shape[1]
    starts = patch_starts.reshape(-1, LANES)
    owner = patch_owner.reshape(-1, LANES)
    line = ("dp", "tensor")

    def moves(target):
        pairs = []
        for d in range(dp_n):
            for x in range(ten_n):
                to = target(d, x)
                if to is not None:
                    pairs.append((d * ten_n + x, to[0] * ten_n + to[1]))
        return pairs

    swap = [(i, dp_n - 1 - i) for i in range(dp_n)]
    pair = [(x, x ^ 1) for x in range(ten_n)]
    near0 = attn_context[0]
    near1 = [lax.ppermute(near0[:CUT], "tensor", pair)]

    def along(target):
        return [
            (i * SIDE + j, target(i, j)[0] * SIDE + target(i, j)[1]) for i in range(SIDE) for j in range(SIDE)
        ]

    both_t, own, paired, away = chain_terms(w_value, w_out, w_global)
    away = lax.ppermute(away, "tensor", [(x, ten_n - 1 - x) for x in range(ten_n)])

    outgoing = segment_sums(after(starts, both_t), owner, byte_grads[0], ctx_n, width)
    outgoing = after(outgoing, near1[0], away)
    incoming = lax.all_to_all(outgoing, "context", split_axis=0, concat_axis=0, tiled=True)

    away = after(away, outgoing)
    paired = (paired.astype(f32) + away[1].astype(f32)).astype(bf16)
    paired = lax.ppermute(paired, "tensor", pair)
    chain = (own.astype(f32) + away[0].astype(f32) + paired.astype(f32)).astype(bf16)
    chain = jnp.stack([chain, lax.ppermute(chain, "context", along(lambda i, j: (i, j ^ 1)))])
    edges = jnp.arange(ctx_n, dtype=jnp.int32) * bytes_n
    counts = jnp.sum((patch_starts[0][None, :] <= edges[:, None]).astype(jnp.int32), axis=1)
    first = jnp.minimum((counts - 1) // LANES, starts.shape[0] - WIN)
    incoming = after(incoming, first, chain)

    near1.append(lax.ppermute(after(near0, incoming)[CUT:], "tensor", pair))
    sums = collect(first, incoming, patch_rows)
    cross = lax.ppermute(sums, line, moves(lambda d, x: (0, x) if d == 1 else (1, ten_n - 1 - x)))
    third = lax.ppermute(sums, line, moves(lambda d, x: (1, ten_n - 1 - x) if d == 1 else None))
    other = lax.ppermute(after(chain, sums), "context", along(lambda i, j: (i ^ 1, j)))
    far0 = lax.ppermute(after(near0, sums), "dp", swap)
    far1 = [lax.ppermute(after(near1[0], sums), "dp", swap)]
    far1.append(lax.ppermute(after(near1[1], cross, third, other), "dp", swap))
    columns = (near0, *near1, far0, *far1)
    partial, near = outer((sums, third, cross), columns)
    pieces = lax.all_to_all(partial, "context", split_axis=0, concat_axis=0, tiled=True)
    chain = jnp.stack([after(chain, partial), after(other, partial)])
    rest = lax.ppermute(chain, "context", along(lambda i, j: (SIDE - 1 - i, j)))

    far = lax.ppermute(near, "tensor", pair)
    piece = jnp.sum(pieces.astype(f32), axis=0).astype(bf16)
    parts = []
    for s in range(ten_n):
        parts.append(lax.ppermute(piece, line, moves(lambda d, x, s=s: (x // 2, (2 * d + x % 2) ^ s))))
    give = context_rows(1, after(near, *parts), far, chain, rest)
    back = lax.ppermute(give, "dp", swap)
    context_grad = context_rows(0, near, far, chain, rest, back)
    weight_grad = last(parts, both_t)
    return (context_grad[None], weight_grad)


def solution(mesh):
    placed = (
        P("dp", "context", None),
        P("dp", None),
        P("dp", None),
        P("dp", "context", "tensor"),
        P(None, "tensor"),
        P("tensor", None),
        P(),
    )
    return jax.shard_map(
        local,
        mesh=mesh,
        in_specs=placed,
        out_specs=(P("dp", "context", "tensor"), P(("dp", "context"), "tensor")),
        check_vma=False,
    )
```
